32 devices in a mesh: dp: 16 (over z, x, core), tensor: 2 (over y).
Axes of the slice: x: 2, y: 2, z: 4, core: 2. Of those that a mesh axis runs over, the one named last changes fastest.
Arguments:
- inputs: bfloat16 [64, 512, 768], P('dp', 'tensor'), may hold values from -6 to 6
- lengths: int32 [64], P('dp'), may hold values from 128 to 512, as said below
- query_weight: bfloat16 [768, 768], P(None, 'tensor'), may hold values from -0.21875 to 0.21875
- query_bias: float32 [768], P('tensor'), may hold values from -3 to 3
- key_weight: bfloat16 [768, 768], P(None, 'tensor'), may hold values from -0.21875 to 0.21875
- value_weight: bfloat16 [768, 768], P(None, 'tensor'), may hold values from -0.21875 to 0.21875
- value_bias: float32 [768], P('tensor'), may hold values from -0.6 to 0.6
- output_weight: bfloat16 [768, 768], P('tensor'), may hold values from -1.25 to 1.25
- output_bias: float32 [768], replicated, may hold values from -3 to 3
- first_gain: float32 [768], replicated, may hold values from 0.5 to 1.5
- first_shift: float32 [768], replicated, may hold values from -3 to 3
- up_weight: bfloat16 [768, 3072], P(None, 'tensor'), may hold values from -0.21875 to 0.21875
- up_bias: float32 [3072], P('tensor'), may hold values from -3 to 3
- down_weight: bfloat16 [3072, 768], P('tensor'), may hold values from -0.109375 to 0.109375
- down_bias: float32 [768], replicated, may hold values from -3 to 3
- second_gain: float32 [768], replicated, may hold values from 0.5 to 1.5
- second_shift: float32 [768], replicated, may hold values from -3 to 3
- cotangent: bfloat16 [64, 512, 768], P('dp', 'tensor'), may hold values from -6 to 6
Outputs:
- layer_output: bfloat16 [64, 512, 768], P('dp', 'tensor')
- inputs_gradient: bfloat16 [64, 512, 768], P('dp', 'tensor')
- query_weight_gradient: float32 [768, 768], P(None, 'tensor')
- query_bias_gradient: float32 [768], P('tensor')
- key_weight_gradient: float32 [768, 768], P(None, 'tensor')
- value_weight_gradient: float32 [768, 768], P(None, 'tensor')
- value_bias_gradient: float32 [768], P('tensor')
- output_weight_gradient: float32 [768, 768], P('tensor')
- output_bias_gradient: float32 [768], replicated
- first_gain_gradient: float32 [768], replicated
- first_shift_gradient: float32 [768], replicated
- up_weight_gradient: float32 [768, 3072], P(None, 'tensor')
- up_bias_gradient: float32 [3072], P('tensor')
- down_weight_gradient: float32 [3072, 768], P('tensor')
- down_bias_gradient: float32 [768], replicated
- second_gain_gradient: float32 [768], replicated
- second_shift_gradient: float32 [768], replicated
The draws below stay inside these ranges and needn't reach their ends.
Inputs may be any that keep to these rules, and one draw needn't show every extreme that they name: Among the 4 consecutive sequences of each aligned block, one has all 512 slots filled; slots at positions lengths and beyond are padding.
All inputs are finite; a program needn't handle non-finite values.
Results may differ from the reference program's by a relative error of at most 0.015.
Values may be sent and summed in bfloat16 or wider, within the bound.
No kernel may reach another device: no remote copies, remote signals or barrier semaphores. Data moves between devices by JAX's collectives and lax.ppermute only.
A program may use at most 192 MiB of HBM per device.

```python
import math
import jax
import jax.numpy as jnp
from jax import lax

D = 768
HEADS = 12
HD = 64
FF = 3072
L = 512
SEQ_DEV = 4
SEQS = 64


def draw_lengths(key, part):
    key = jax.random.fold_in(key, 7)
    first_key, second_key = jax.random.split(key)
    spread = jax.random.randint(first_key, (SEQS,), L // 4, L + 1)
    groups = SEQS // SEQ_DEV
    chosen = jax.random.randint(second_key, (groups, 1), 0, SEQ_DEV)
    filled = (jnp.arange(SEQ_DEV)[None, :] == chosen).reshape(SEQS)
    return jnp.where(filled, L, spread).astype(jnp.int32)


def shard_levels(key, extent, pieces, low, high):
    level, own = 1.0, jax.random.fold_in(key, 6)
    for position, shards_of in pieces:
        heights = jnp.exp(jax.random.uniform(jax.random.fold_in(own, position), (shards_of,), jnp.float32, low / len(pieces), high / len(pieces)))
        level = level * jnp.repeat(heights, extent[position] // shards_of).reshape([-1 if axis == position else 1 for axis in range(len(extent))])
    return level


def bell_draw(rng, dims, deviation, most, cuts=(), held_as=jnp.bfloat16):
    values = deviation * jax.random.normal(rng, dims, jnp.float32)
    if cuts:
        values = values * shard_levels(rng, dims, cuts, -0.22, 0.18)
    return jnp.clip(values, -most, most).astype(held_as)


def setup_inputs(seed: int = 0) -> dict:
    splits = jax.random.split(jax.random.key(seed), 19)
    return {
        "inputs": bell_draw(splits[0], (SEQS, L, D), 1.0, 6.0, ((0, 16), (1, 2))),
        "lengths": draw_lengths(jax.random.fold_in(splits[18], 71), 0),
        "query_weight": bell_draw(splits[2], (D, D), D ** -0.5, 0.21875, ((1, 2),)),
        "query_bias": bell_draw(splits[3], (D,), 0.5, 3.0, ((0, 2),), jnp.float32),
        "key_weight": bell_draw(splits[4], (D, D), D ** -0.5, 0.21875, ((1, 2),)),
        "value_weight": bell_draw(splits[5], (D, D), D ** -0.5, 0.21875, ((1, 2),)),
        "value_bias": bell_draw(splits[6], (D,), 0.1, 0.6, ((0, 2),), jnp.float32),
        "output_weight": bell_draw(splits[7], (D, D), (D * 16 // L) ** -0.5, 1.25, ((0, 2),)),
        "output_bias": bell_draw(splits[8], (D,), 0.5, 3.0, (), jnp.float32),
        "first_gain": jnp.clip(1.0 + 0.1 * jax.random.normal(splits[9], (D,), jnp.float32), 0.5, 1.5),
        "first_shift": bell_draw(splits[10], (D,), 0.5, 3.0, (), jnp.float32),
        "up_weight": bell_draw(splits[11], (D, FF), D ** -0.5, 0.21875, ((1, 2),)),
        "up_bias": bell_draw(splits[12], (FF,), 0.5, 3.0, ((0, 2),), jnp.float32),
        "down_weight": bell_draw(splits[13], (FF, D), FF ** -0.5, 0.109375, ((0, 2),)),
        "down_bias": bell_draw(splits[14], (D,), 0.5, 3.0, (), jnp.float32),
        "second_gain": jnp.clip(1.0 + 0.1 * jax.random.normal(splits[15], (D,), jnp.float32), 0.5, 1.5),
        "second_shift": bell_draw(splits[16], (D,), 0.5, 3.0, (), jnp.float32),
        "cotangent": bell_draw(splits[17], (SEQS, L, D), 1.0, 6.0, ((0, 16), (1, 2))),
    }


EPSILON = 1e-06
MASKED = -1000000000.0
HIGH = lax.Precision.HIGHEST

@jax.custom_vjp
def low(v):
    return lax.optimization_barrier(v.astype(jnp.bfloat16)).astype(jnp.float32)

@jax.custom_vjp
def low_back(v):
    return v

def low_keep(v):
    return (low(v), None)

def low_pass(kept, grad):
    return (grad,)

def back_keep(v):
    return (v, None)

def back_low(kept, grad):
    return (low(grad),)
low.defvjp(low_keep, low_pass)
low_back.defvjp(back_keep, back_low)

def rounded(value):
    return low(low_back(value))

def layer_norm(hidden, gain, shift):
    centre = hidden - lax.optimization_barrier(jnp.mean(hidden, -1, keepdims=True))
    scale = lax.rsqrt(lax.optimization_barrier(jnp.mean(centre * centre, -1, keepdims=True)) + EPSILON)
    return centre * scale * gain + shift

def product(left, right):
    return jnp.dot(left, right, precision=HIGH)

def attend(item):
    queries, keys, values, length = item
    factor = 1.0 / math.sqrt(HD)
    scores = jnp.einsum('qhd,khd->hqk', queries, keys, precision=HIGH) * factor
    visible = (jnp.arange(L) < length)[None, None, :]
    scores = low_back(jnp.where(visible, scores, MASKED))
    weights = jax.nn.softmax(scores, axis=-1)
    return jnp.einsum('hqk,khd->qhd', low(weights), values, precision=HIGH)

def forward(block, lens, query_weight, query_bias, key_weight, value_weight, value_bias, output_weight, output_bias, first_gain, first_shift, up_weight, up_bias, down_weight, down_bias, second_gain, second_shift):
    group = block.shape[0]
    flat = block.reshape(group * L, D)
    shape4 = (group, L, HEADS, HD)
    queries = rounded(product(flat, query_weight) + query_bias).reshape(shape4)
    keys = rounded(product(flat, key_weight)).reshape(shape4)
    values = rounded(product(flat, value_weight) + value_bias).reshape(shape4)
    context = lax.map(jax.checkpoint(attend), (queries, keys, values, lens))
    context = rounded(context.reshape(group * L, D))
    mixed = low_back(product(context, output_weight)) + output_bias
    middle = layer_norm(flat + mixed, first_gain, first_shift)
    lifted = low_back(product(low(middle), up_weight) + up_bias)
    activated = low(jax.nn.gelu(lifted, approximate=False))
    feed = low_back(product(activated, down_weight)) + down_bias
    return layer_norm(middle + feed, second_gain, second_shift)

def reference(inputs, lengths, query_weight, query_bias, key_weight, value_weight, value_bias, output_weight, output_bias, first_gain, first_shift, up_weight, up_bias, down_weight, down_bias, second_gain, second_shift, cotangent):
    params = tuple((p.astype(jnp.float32) for p in (query_weight, query_bias, key_weight, value_weight, value_bias, output_weight, output_bias, first_gain, first_shift, up_weight, up_bias, down_weight, down_bias, second_gain, second_shift)))
    groups = SEQS // SEQ_DEV
    blocks = inputs.astype(jnp.float32).reshape(groups, SEQ_DEV, L, D)
    slopes = cotangent.astype(jnp.float32).reshape(groups, SEQ_DEV * L, D)
    lens_all = lengths.reshape(groups, SEQ_DEV)
    zeros = tuple((jnp.zeros(p.shape, jnp.float32) for p in params))

    def step(total, item):
        block, lens, slope = item
        result, back = jax.vjp(lambda xv, *pv: forward(xv, lens, *pv), block, *params)
        grads = back(slope)
        new_total = tuple((t + g for t, g in zip(total, grads[1:])))
        return (new_total, (result.astype(jnp.bfloat16), grads[0].astype(jnp.bfloat16)))
    total, (outputs, input_grads) = lax.scan(step, zeros, (blocks, lens_all, slopes))
    return (outputs.reshape(SEQS, L, D), input_grads.reshape(SEQS, L, D), total[0], total[1], total[2], total[3], total[4], total[5], total[6], total[7], total[8], total[9], total[10], total[11], total[12], total[13], total[14])
```

```python
import functools

import jax
import jax.numpy as jnp
from jax import lax
from jax.experimental import pallas as pl
from jax.experimental.pallas import tpu as pltpu
from jax.sharding import PartitionSpec as P

HD = 64
EPSILON = 1e-06
MASKED = -1000000000.0
BF = jnp.bfloat16
F32 = jnp.float32
VMEM_LIMIT = 60 * 1024 * 1024
LANES = 128

ANY = pl.BlockSpec(memory_space=pl.ANY)
SMEM = pl.BlockSpec(memory_space=pltpu.SMEM)


def dot(left, right):
    return lax.dot_general(left, right, (((1,), (0,)), ((), ())), preferred_element_type=F32)


def dot_nt(left, right):
    return lax.dot_general(left, right, (((1,), (1,)), ((), ())), preferred_element_type=F32)


def dot_tn(left, right):
    return lax.dot_general(left, right, (((0,), (0,)), ((), ())), preferred_element_type=F32)


def shape_of(dims, kind=BF):
    return jax.ShapeDtypeStruct(dims, kind)


def fixed(dims):
    return pl.BlockSpec(dims, lambda *_: (0,) * len(dims))


def params(*names):
    return pltpu.CompilerParams(dimension_semantics=names, vmem_limit_bytes=VMEM_LIMIT)


def cost(flops, nbytes, transcendentals=0):
    return pl.CostEstimate(
        flops=int(flops), bytes_accessed=int(nbytes), transcendentals=int(transcendentals)
    )


def piece_copies(place, pieces, target, sems, first, lead):
    copies = []
    for d, piece in enumerate(pieces):
        rows = piece.shape[-2]
        start = pl.multiple_of((place ^ d) * rows, rows)
        where = target.at[:, pl.ds(start, rows)] if lead else target.at[pl.ds(start, rows)]
        copies.append(pltpu.make_async_copy(piece, where, sems.at[first + d]))
    return copies


def attend_kernel(gathered, *refs):
    if gathered:
        place, refs = refs[0], refs[1:]
    xo, xr, seen, qb, vb, *refs = refs
    if gathered:
        pieces, refs = refs[:4], refs[4:]
        q_out, k_out, v_out, p_out, c_out, w_out, w, sems = refs

        @pl.when(pl.program_id(0) == 0)
        def _():
            copies = piece_copies(place[0], pieces, w, sems, 0, True)
            for copy in copies:
                copy.start()
            for copy in copies:
                copy.wait()
            w_out[...] = w[...]

        wq, wk, wv = w[0], w[1], w[2]
    else:
        wq, wk, wv, q_out, k_out, v_out, p_out, c_out = refs
        wq, wk, wv = wq[...], wk[...], wv[...]
    x = jnp.concatenate([xo[0], xr[0]], 0)
    q = (dot(x, wq) + qb[...]).astype(BF) * jnp.asarray(HD**-0.5, BF)
    k = dot(x, wk).astype(BF)
    v = (dot(x, wv) + vb[...]).astype(BF)
    q_out[...] = q
    k_out[...] = k
    v_out[...] = v
    bias = seen[0]
    low = lax.broadcasted_iota(jnp.int32, (x.shape[0], LANES), 1) < HD
    zero = jnp.zeros((), BF)
    for pair in range(q.shape[1] // LANES):
        part = slice(pair * LANES, (pair + 1) * LANES)
        qp, kp, vp = q[:, part], k[:, part], v[:, part]
        joined = []
        for b in range(2):
            qm = jnp.where(low, qp, zero) if b == 0 else jnp.where(low, zero, qp)
            s = dot_nt(qm, kp) + bias
            e = jnp.exp(s - jnp.max(s, -1, keepdims=True))
            p = (e * (1.0 / jnp.sum(e, -1, keepdims=True))).astype(BF)
            p_out[0, pair * 2 + b] = p
            joined.append(dot(p, vp))
        c_out[:, part] = jnp.where(low, joined[0], joined[1]).astype(BF)


def attend(xo, xr, seen, qb, vb, weights, place=None):
    seqs, half, width = xo.shape
    span = 2 * half
    cols = qb.shape[1]
    heads = cols // HD
    gathered = place is not None
    in_specs = [
        pl.BlockSpec((1, half, width), lambda s: (s, 0, 0)),
        pl.BlockSpec((1, half, width), lambda s: (s, 0, 0)),
        pl.BlockSpec((1, 1, span), lambda s: (s, 0, 0)),
        fixed((1, cols)),
        fixed((1, cols)),
    ]
    rows = pl.BlockSpec((span, cols), lambda s: (s, 0))
    out_specs = [
        rows,
        rows,
        rows,
        pl.BlockSpec((1, heads, span, span), lambda s: (s, 0, 0, 0)),
        rows,
    ]
    out_shape = [shape_of((seqs * span, cols))] * 3 + [
        shape_of((seqs, heads, span, span)),
        shape_of((seqs * span, cols)),
    ]
    args = [xo, xr, seen, qb, vb, *weights]
    scratch = []
    if gathered:
        in_specs = [SMEM] + in_specs + [ANY] * len(weights)
        args = [place] + args
        out_specs.append(fixed((3, width, cols)))
        out_shape.append(shape_of((3, width, cols)))
        scratch = [pltpu.VMEM((3, width, cols), BF), pltpu.SemaphoreType.DMA((4,))]
    else:
        in_specs = in_specs + [fixed((width, cols))] * 3
    flops = 2 * seqs * span * (3 * width * cols + 2 * span * LANES * 2 * heads)
    return pl.pallas_call(
        functools.partial(attend_kernel, gathered),
        grid=(seqs,),
        in_specs=in_specs,
        out_specs=out_specs,
        out_shape=out_shape,
        scratch_shapes=scratch,
        compiler_params=params("arbitrary"),
        cost_estimate=cost(flops, 12e6, seqs * heads * span * span),
        name="attend",
    )(*args)


def normed(hidden):
    centre = hidden - jnp.mean(hidden, -1, keepdims=True)
    scale = lax.rsqrt(jnp.mean(centre * centre, -1, keepdims=True) + EPSILON)
    return centre * scale, scale


def norm_back(upper, unit, scale, gain):
    through = upper * gain
    return scale * (
        through
        - jnp.mean(through, -1, keepdims=True)
        - unit * jnp.mean(through * unit, -1, keepdims=True)
    )


def gelu_and_slope(u):
    cdf = 0.5 + 0.5 * lax.erf(u * 0.7071067811865476)
    density = jnp.exp(-0.5 * u * u) * 0.3989422804014327
    return (u * cdf).astype(BF), (cdf + u * density).astype(BF)


def add_rows(ref, step, values):
    for row, value in enumerate(values):
        total = jnp.sum(value, 0, keepdims=True)

        @pl.when(step == 0)
        def _():
            ref[row : row + 1, :] = total

        @pl.when(step > 0)
        def _():
            ref[row : row + 1, :] += total


def forward_kernel(
    place,
    xo,
    xr,
    eo,
    er,
    c_own,
    c_oth,
    wo_own,
    wu_own,
    wd_own,
    *refs,
):
    wo_p, wu_p, wd_p, refs = refs[:4], refs[4:8], refs[8:12], refs[12:]
    (bo, g1, b1, bu_own, bu_oth, bd, g2, b2, *refs) = refs
    (
        out_own,
        out_send,
        y_out,
        n_out,
        r_out,
        ga_own,
        ga_oth,
        sl_own,
        sl_oth,
        dh_out,
        sums,
        wo_oth,
        wu_oth,
        wd_oth,
        sems,
    ) = refs
    step = pl.program_id(0)

    @pl.when(step == 0)
    def _():
        copies = (
            piece_copies(place[0], wo_p, wo_oth, sems, 0, False)
            + piece_copies(place[0], wu_p, wu_oth, sems, 4, False)
            + piece_copies(place[0], wd_p, wd_oth, sems, 8, False)
        )
        for copy in copies:
            copy.start()
        for copy in copies:
            copy.wait()

    mine = step % 2 == 0
    x = jnp.where(mine, xo[0], xr[0]).astype(F32)
    first = x + dot(c_own[...], wo_own[...]) + dot(c_oth[...], wo_oth[...]) + bo[...]
    unit, scale = normed(first)
    n_out[...] = unit
    r_out[...] = scale
    middle = unit * g1[...] + b1[...]
    y = middle.astype(BF)
    y_out[...] = y
    total = middle + bd[...]
    for wu, wd, bu, ga, sl in (
        (wu_own, wd_own, bu_own, ga_own, sl_own),
        (wu_oth, wd_oth, bu_oth, ga_oth, sl_oth),
    ):
        active, slope = gelu_and_slope(dot(y, wu[...]) + bu[...])
        ga[...] = active
        sl[...] = slope
        total = total + dot(active, wd[...])
    unit2, scale2 = normed(total)
    result = (unit2 * g2[...] + b2[...]).astype(BF)

    @pl.when(mine)
    def _():
        out_own[0] = result

    @pl.when(jnp.logical_not(mine))
    def _():
        out_send[0] = result

    upper = jnp.where(mine, eo[0], er[0]).astype(F32)
    back = norm_back(upper, unit2, scale2, g2[...])
    dh_out[...] = back.astype(BF)
    add_rows(sums, step, (upper * unit2, upper, back))


def forward(place, xo, xr, eo, er, c_own, c_oth, own, others, vectors):
    seqs, half, width = xo.shape
    rows = seqs * 2 * half
    wo, wu, wd = own
    cols, units = wo.shape[0], wu.shape[1]
    pair = pl.BlockSpec((1, half, width), lambda i: (i // 2, 0, 0))

    def block(n):
        return pl.BlockSpec((half, n), lambda i: (i, 0))

    in_specs = (
        [SMEM]
        + [pair] * 4
        + [block(cols)] * 2
        + [fixed(wo.shape), fixed(wu.shape), fixed(wd.shape)]
        + [ANY] * 12
        + [fixed(v.shape) for v in vectors]
    )
    out_specs = [
        pair,
        pair,
        block(width),
        block(width),
        block(1),
        block(units),
        block(units),
        block(units),
        block(units),
        block(width),
        fixed((3, width)),
    ]
    out_shape = [
        shape_of((seqs, half, width)),
        shape_of((seqs, half, width)),
        shape_of((rows, width)),
        shape_of((rows, width), F32),
        shape_of((rows, 1), F32),
        shape_of((rows, units)),
        shape_of((rows, units)),
        shape_of((rows, units)),
        shape_of((rows, units)),
        shape_of((rows, width)),
        shape_of((3, width), F32),
    ]
    return pl.pallas_call(
        forward_kernel,
        grid=(rows // half,),
        in_specs=in_specs,
        out_specs=out_specs,
        out_shape=out_shape,
        scratch_shapes=[
            pltpu.VMEM(wo.shape, BF),
            pltpu.VMEM(wu.shape, BF),
            pltpu.VMEM(wd.shape, BF),
            pltpu.SemaphoreType.DMA((12,)),
        ],
        compiler_params=params("arbitrary"),
        cost_estimate=cost(4 * rows * width * (cols + 2 * units), 40e6, 4 * rows * units),
        name="forward",
    )(place, xo, xr, eo, er, c_own, c_oth, wo, wu, wd, *others, *vectors)


def backward_kernel(
    place,
    dh,
    unit,
    scale,
    sl_own,
    sl_oth,
    wo_own,
    wu_own,
    wd_own,
    *refs,
):
    wo_p, wu_p, wd_p, refs = refs[:4], refs[4:8], refs[8:12], refs[12:]
    (
        g1,
        du_own,
        du_oth,
        d1_out,
        dc_own,
        dc_oth,
        sums,
        bsum_own,
        bsum_oth,
        wo_oth,
        wu_oth,
        wd_oth,
        sems,
    ) = refs
    step = pl.program_id(0)

    @pl.when(step == 0)
    def _():
        copies = (
            piece_copies(place[0], wd_p, wd_oth, sems, 8, False)
            + piece_copies(place[0], wu_p, wu_oth, sems, 4, False)
            + piece_copies(place[0], wo_p, wo_oth, sems, 0, False)
        )
        for copy in copies:
            copy.start()
        for copy in copies:
            copy.wait()

    h = dh[...]
    upper = h.astype(F32)
    for wu, wd, sl, du, bsum in (
        (wu_oth, wd_oth, sl_oth, du_oth, bsum_oth),
        (wu_own, wd_own, sl_own, du_own, bsum_own),
    ):
        lifted = (dot_nt(h, wd[...]) * sl[...].astype(F32)).astype(BF)
        du[...] = lifted
        add_rows(bsum, step, (lifted.astype(F32),))
        upper = upper + dot_nt(lifted, wu[...])
    back = norm_back(upper, unit[...], scale[...], g1[...])
    add_rows(sums, step, (upper * unit[...], upper, back))
    lower = back.astype(BF)
    d1_out[...] = lower
    dc_own[...] = dot_nt(lower, wo_own[...]).astype(BF)
    dc_oth[...] = dot_nt(lower, wo_oth[...]).astype(BF)


def backward(place, dh, unit, scale, sl_own, sl_oth, own, others, g1, half):
    rows, width = dh.shape
    wo, wu, wd = own
    cols, units = wo.shape[0], wu.shape[1]

    def block(n):
        return pl.BlockSpec((half, n), lambda i: (i, 0))

    in_specs = (
        [SMEM, block(width), block(width), block(1), block(units), block(units)]
        + [fixed(wo.shape), fixed(wu.shape), fixed(wd.shape)]
        + [ANY] * 12
        + [fixed(g1.shape)]
    )
    out_specs = [
        block(units),
        block(units),
        block(width),
        block(cols),
        block(cols),
        fixed((3, width)),
        fixed((1, units)),
        fixed((1, units)),
    ]
    out_shape = [
        shape_of((rows, units)),
        shape_of((rows, units)),
        shape_of((rows, width)),
        shape_of((rows, cols)),
        shape_of((rows, cols)),
        shape_of((3, width), F32),
        shape_of((1, units), F32),
        shape_of((1, units), F32),
    ]
    return pl.pallas_call(
        backward_kernel,
        grid=(rows // half,),
        in_specs=in_specs,
        out_specs=out_specs,
        out_shape=out_shape,
        scratch_shapes=[
            pltpu.VMEM(wo.shape, BF),
            pltpu.VMEM(wu.shape, BF),
            pltpu.VMEM(wd.shape, BF),
            pltpu.SemaphoreType.DMA((12,)),
        ],
        compiler_params=params("arbitrary"),
        cost_estimate=cost(4 * rows * width * (cols + 2 * units), 40e6),
        name="backward",
    )(place, dh, unit, scale, sl_own, sl_oth, wo, wu, wd, *others, g1)


def put_chunks(place, value, first, keep, send, rows):
    half = keep.shape[0]
    for n in range(value.shape[0] // rows):
        d = place ^ (first + n)
        chunk = value[n * rows : (n + 1) * rows].astype(BF)

        @pl.when(d < half)
        def _():
            keep[d] = chunk

        @pl.when(d >= half)
        def _():
            send[d - half] = chunk


def product_kernel(tile, rows, place, left, right, keep, send):
    step = pl.program_id(0)
    value = dot_tn(left[...], right[...])
    put_chunks(place[0], value, step * (tile // rows), keep, send, rows)


def weight_product(place, left, right, tile):
    total, m = left.shape
    n = right.shape[1]
    rows = m // 8
    kept = (4, rows, n)
    return pl.pallas_call(
        functools.partial(product_kernel, tile, rows),
        grid=(m // tile,),
        in_specs=[SMEM, pl.BlockSpec((total, tile), lambda i: (0, i)), fixed(right.shape)],
        out_specs=[fixed(kept), fixed(kept)],
        out_shape=[shape_of(kept), shape_of(kept)],
        compiler_params=params("arbitrary"),
        cost_estimate=cost(2 * total * m * n, 2 * (total * m + total * n + m * n)),
        name="weight_product",
    )(place, left, right)


def attend_back_kernel(last, *refs):
    place, xo, xr, p_in, q_in, k_in, v_in, c_in, dc_in, *refs = refs
    if last:
        wq, wk, wv, before, keep, send, sums, dx_own, dx_send, total, grads = refs
        weights = (wq[...], wk[...], wv[...])
    else:
        w, before, keep, send, sums, dx, total, grads = refs
        weights = (w[0], w[1], w[2])
    step = pl.program_id(0)
    x = jnp.concatenate([xo[0], xr[0]], 0)
    span = x.shape[0]
    cols = q_in.shape[1]
    low = lax.broadcasted_iota(jnp.int32, (span, LANES), 1) < HD
    zero = jnp.zeros((), BF)
    for pair in range(cols // LANES):
        part = slice(pair * LANES, (pair + 1) * LANES)
        qp, kp, vp, dcp = q_in[:, part], k_in[:, part], v_in[:, part], dc_in[:, part]
        shared = dcp.astype(F32) * c_in[:, part].astype(F32)
        found = []
        for b in range(2):
            dcm = jnp.where(low, dcp, zero) if b == 0 else jnp.where(low, zero, dcp)
            centre = jnp.sum(jnp.where(low, shared, 0.0) if b == 0 else jnp.where(low, 0.0, shared), -1, keepdims=True)
            p = p_in[0, pair * 2 + b]
            ds = (p.astype(F32) * (dot_nt(dcm, vp) - centre)).astype(BF)
            found.append((dot(ds, kp) * HD**-0.5, dot_tn(ds, qp), dot_tn(p, dcp)))
        for n in range(3):
            at = n * cols + pair * LANES
            grads[:, at : at + LANES] = jnp.where(low, found[0][n], found[1][n]).astype(BF)
    value = dot_tn(x, grads[...])

    @pl.when(step == 0)
    def _():
        total[...] = value

    @pl.when(step > 0)
    def _():
        total[...] += value

    add_rows(sums, step, (grads[...].astype(F32),))
    partial = before[...].astype(F32)
    for n in range(3):
        partial = partial + dot_nt(grads[:, n * cols : (n + 1) * cols], weights[n])
    if last:
        half = span // 2
        dx_own[0] = partial[:half].astype(BF)
        dx_send[0] = partial[half:].astype(BF)
    else:
        dx[...] = partial

    @pl.when(step == pl.num_programs(0) - 1)
    def _():
        put_chunks(place[0], total[...], 0, keep, send, total.shape[0] // 8)


def attend_back(place, xo, xr, p, q, k, v, c, dc, weights, before, last):
    seqs, half, width = xo.shape
    span = 2 * half
    cols = q.shape[1]
    heads = cols // HD
    pair = pl.BlockSpec((1, half, width), lambda s: (s, 0, 0))
    rows = pl.BlockSpec((span, cols), lambda s: (s, 0))
    wide = pl.BlockSpec((span, width), lambda s: (s, 0))
    kept = (4, width // 8, 3 * cols)
    in_specs = (
        [SMEM, pair, pair]
        + [pl.BlockSpec((1, heads, span, span), lambda s: (s, 0, 0, 0))]
        + [rows] * 5
        + [fixed(w.shape) for w in weights]
        + [wide]
    )
    out_specs = [fixed(kept), fixed(kept), fixed((1, 3 * cols))]
    out_shape = [shape_of(kept), shape_of(kept), shape_of((1, 3 * cols), F32)]
    if last:
        out_specs += [pair, pair]
        out_shape += [shape_of((seqs, half, width))] * 2
    else:
        out_specs += [wide]
        out_shape += [shape_of((seqs * span, width), F32)]
    flops = 2 * seqs * span * (6 * width * cols + 4 * span * LANES * 2 * heads)
    return pl.pallas_call(
        functools.partial(attend_back_kernel, last),
        grid=(seqs,),
        in_specs=in_specs,
        out_specs=out_specs,
        out_shape=out_shape,
        scratch_shapes=[
            pltpu.VMEM((width, 3 * cols), F32),
            pltpu.VMEM((span, 3 * cols), BF),
        ],
        compiler_params=params("arbitrary"),
        cost_estimate=cost(flops, 20e6),
        name="attend_back",
    )(place, xo, xr, p, q, k, v, c, dc, *weights, before)


def assemble_kernel(cuts, place, *refs):
    parts, outs = refs[:8], refs[8:]
    for d, part in enumerate(parts):
        rows = part.shape[0]
        at = pl.multiple_of((place[0] ^ d) * rows, rows)
        left = 0
        for out, cut in zip(outs, cuts, strict=True):
            out[pl.ds(at, rows), :] = part[:, left : left + cut].astype(F32)
            left += cut


def assemble(place, parts, cuts):
    rows, n = parts[0].shape
    return pl.pallas_call(
        functools.partial(assemble_kernel, cuts),
        in_specs=[SMEM] + [pl.BlockSpec(memory_space=pltpu.VMEM)] * 8,
        out_specs=[pl.BlockSpec(memory_space=pltpu.VMEM)] * len(cuts),
        out_shape=[shape_of((8 * rows, cut), F32) for cut in cuts],
        compiler_params=pltpu.CompilerParams(vmem_limit_bytes=VMEM_LIMIT),
        cost_estimate=cost(0, 8 * rows * n * 6),
        name="assemble",
    )(place, *parts)


def tensor_layer(
    dp,
    inputs,
    lengths,
    query_weight,
    query_bias,
    key_weight,
    value_weight,
    value_bias,
    output_weight,
    output_bias,
    first_gain,
    first_shift,
    up_weight,
    up_bias,
    down_weight,
    down_bias,
    second_gain,
    second_shift,
    cotangent,
):
    bits = dp.bit_length() - 1
    count, half, width = inputs.shape
    seqs = count // 2
    side = lax.axis_index("tensor")
    spot = lax.axis_index("dp")
    core, across, deep = spot & 1, (spot >> 1) & 1, (spot >> 2) & 1

    def swap(value):
        return lax.ppermute(value, "tensor", [(0, 1), (1, 0)])

    def flip(value, bit):
        return lax.ppermute(value, "dp", [(i, i ^ (1 << bit)) for i in range(dp)])

    def trade(value):
        mine = lax.dynamic_slice_in_dim(value, side * seqs, seqs, 0)
        sent = lax.dynamic_slice_in_dim(value, (1 - side) * seqs, seqs, 0)
        return mine, swap(sent)

    def untrade(mine, sent):
        got = swap(sent)
        return jnp.where(
            side == 0, jnp.concatenate([mine, got], 0), jnp.concatenate([got, mine], 0)
        )

    xo, xr = trade(inputs)
    square = (across * 2 + core).astype(jnp.int32)
    place4 = square.reshape(1)
    place8 = (core * 4 + across * 2 + deep).astype(jnp.int32).reshape(1)

    def fetch(value, axis=0):
        rows = value.shape[axis] // 4
        own = swap(lax.dynamic_slice_in_dim(value, square * rows, rows, axis))
        beside = flip(own, 1)
        return [own, flip(own, 0), beside, flip(beside, 0)]

    own_qkv = jnp.stack([query_weight, key_weight, value_weight])
    qkv_pieces = fetch(own_qkv, 1)
    small = jnp.concatenate([query_bias, value_bias, up_bias])
    small_other = swap(small)
    cols = query_weight.shape[1]
    others = fetch(output_weight) + fetch(up_weight) + fetch(down_weight)
    eo, er = trade(cotangent)

    lens = lax.dynamic_slice_in_dim(lengths, side * seqs, seqs, 0)
    at = jnp.arange(half)
    position = jnp.concatenate([side * half + at, (1 - side) * half + at])
    seen = jnp.where(position[None, :] < lens[:, None], 0.0, MASKED).astype(F32)[:, None, :]

    def row(value):
        return value.reshape(1, -1)

    q_own, k_own, v_own, p_own, c_own = attend(
        xo, xr, seen, row(query_bias), row(value_bias), [query_weight, key_weight, value_weight]
    )
    q_oth, k_oth, v_oth, p_oth, c_oth, w_oth = attend(
        xo, xr, seen, row(small_other[:cols]), row(small_other[cols : 2 * cols]), qkv_pieces, place4
    )
    own = (output_weight, up_weight, down_weight)
    vectors = [
        row(v)
        for v in (
            output_bias,
            first_gain,
            first_shift,
            up_bias,
            small_other[2 * cols :],
            down_bias,
            second_gain,
            second_shift,
        )
    ]
    (
        out_own,
        out_send,
        y,
        unit,
        scale,
        ga_own,
        ga_oth,
        sl_own,
        sl_oth,
        dh,
        sums2,
    ) = forward(place4, xo, xr, eo, er, c_own, c_oth, own, others, vectors)
    result = untrade(out_own, out_send)

    def reduce_out(oth, mine):
        keep, sent = oth
        other = keep.astype(F32) + flip(sent, 0).astype(F32)
        got = swap(other.astype(BF))
        keep, sent = mine
        total = keep.astype(F32) + flip(sent, 0).astype(F32) + got.astype(F32)
        total = total[:2] + flip(total[2:].astype(BF), 1).astype(F32)
        total = total[:1] + flip(total[1:].astype(BF), 2).astype(F32)
        for bit in range(3, bits):
            total = total.astype(BF)
            total = total.astype(F32) + flip(total, bit).astype(F32)
        return total[0].astype(BF)

    def gather_out(chunk):
        parts = [chunk]
        for bit in (2, 1, 0):
            parts = parts + [flip(part, bit) for part in parts]
        return parts

    down_oth = weight_product(place8, ga_oth, dh, 768)
    down_own = weight_product(place8, ga_own, dh, 768)
    du_own, du_oth, d1, dc_own, dc_oth, sums1, bu_own, bu_oth = backward(
        place4, dh, unit, scale, sl_own, sl_oth, own, others, row(first_gain), half
    )
    up_oth = weight_product(place8, y, du_oth, 384)
    up_own = weight_product(place8, y, du_own, 384)
    out_oth = weight_product(place8, c_oth, d1, 384)
    out_mine = weight_product(place8, c_own, d1, 384)
    qkv_oth_keep, qkv_oth_send, s_oth, dx_oth = attend_back(
        place8, xo, xr, p_oth, q_oth, k_oth, v_oth, c_oth, dc_oth, [w_oth], d1, False
    )
    qkv_own_keep, qkv_own_send, s_own, dx_own, dx_send = attend_back(
        place8,
        xo,
        xr,
        p_own,
        q_own,
        k_own,
        v_own,
        c_own,
        dc_own,
        [query_weight, key_weight, value_weight],
        dx_oth,
        True,
    )
    inputs_back = untrade(dx_own, dx_send)
    (down_back,) = assemble(place8, gather_out(reduce_out(down_oth, down_own)), (width,))
    (up_back,) = assemble(
        place8, gather_out(reduce_out(up_oth, up_own)), (up_weight.shape[1],)
    )
    (out_back,) = assemble(place8, gather_out(reduce_out(out_oth, out_mine)), (width,))
    query_back, key_back, value_back = assemble(
        place8,
        gather_out(reduce_out((qkv_oth_keep, qkv_oth_send), (qkv_own_keep, qkv_own_send))),
        (cols,) * 3,
    )

    whole = jnp.concatenate([sums2.reshape(-1), sums1.reshape(-1)])
    mine = jnp.concatenate([s_own[0, :cols], s_own[0, 2 * cols :], bu_own[0]])
    sent = jnp.concatenate([s_oth[0, :cols], s_oth[0, 2 * cols :], bu_oth[0]])
    flat = jnp.concatenate([whole, mine]) + swap(jnp.concatenate([whole, sent]))
    for bit in range(bits):
        flat = flat + flip(flat, bit)
    g2b, b2b, bdb, g1b, b1b, bob = [flat[n * width : (n + 1) * width] for n in range(6)]
    rest = flat[6 * width :]
    return (
        result,
        inputs_back,
        query_back,
        rest[:cols],
        key_back,
        value_back,
        rest[cols : 2 * cols],
        out_back,
        bob,
        g1b,
        b1b,
        up_back,
        rest[2 * cols :],
        down_back,
        bdb,
        g2b,
        b2b,
    )


def solution(mesh):
    in_specs = (
        P("dp", "tensor", None),
        P("dp"),
        P(None, "tensor"),
        P("tensor"),
        P(None, "tensor"),
        P(None, "tensor"),
        P("tensor"),
        P("tensor", None),
        P(),
        P(),
        P(),
        P(None, "tensor"),
        P("tensor"),
        P("tensor", None),
        P(),
        P(),
        P(),
        P("dp", "tensor", None),
    )
    out_specs = (
        P("dp", "tensor", None),
        P("dp", "tensor", None),
        P(None, "tensor"),
        P("tensor"),
        P(None, "tensor"),
        P(None, "tensor"),
        P("tensor"),
        P("tensor", None),
        P(),
        P(),
        P(),
        P(None, "tensor"),
        P("tensor"),
        P("tensor", None),
        P(),
        P(),
        P(),
    )
    return jax.shard_map(
        functools.partial(tensor_layer, mesh.shape["dp"]),
        mesh=mesh,
        in_specs=in_specs,
        out_specs=out_specs,
        check_vma=False,
    )
```

```python
import functools

import jax
import jax.numpy as jnp
from jax import lax
from jax.experimental import pallas as pl
from jax.experimental.pallas import tpu as pltpu
from jax.sharding import PartitionSpec as P

HD = 64
EPSILON = 1e-06
MASKED = -1000000000.0
BF = jnp.bfloat16
F32 = jnp.float32
MIB = 1024 * 1024
LANES = 128
CHUNKS = 8

ANY = pl.BlockSpec(memory_space=pl.ANY)
HBM = pl.BlockSpec(memory_space=pltpu.HBM)
SMEM = pl.BlockSpec(memory_space=pltpu.SMEM)
VMEM = pl.BlockSpec(memory_space=pltpu.VMEM)


def dot(left, right):
    return lax.dot_general(left, right, (((1,), (0,)), ((), ())), preferred_element_type=F32)


def dot_nt(left, right):
    return lax.dot_general(left, right, (((1,), (1,)), ((), ())), preferred_element_type=F32)


def dot_tn(left, right):
    return lax.dot_general(left, right, (((0,), (0,)), ((), ())), preferred_element_type=F32)


def shape_of(dims, kind=BF):
    return jax.ShapeDtypeStruct(dims, kind)


def fixed(dims):
    return pl.BlockSpec(dims, lambda *_: (0,) * len(dims))


def held(dims):
    return pl.BlockSpec(dims, lambda *_: (0,) * len(dims), pipeline_mode=pl.Buffered(1))


class Chain:
    def __init__(self):
        self.token = None

    def call(self, name, body, args, in_specs, out_specs, out_shape, grid=(), scratch=(), mib=62, aliases=None):
        taken, given = len(args), len(out_shape)
        linked = self.token is not None

        def kernel(*refs):
            rest = refs[taken + linked :]
            body(*refs[:taken], *rest[:given], *rest[given + 1 :])

        outs = pl.pallas_call(
            kernel,
            grid=grid,
            in_specs=list(in_specs) + [ANY] * linked,
            out_specs=list(out_specs) + [ANY],
            out_shape=list(out_shape) + [shape_of((8, LANES), F32)],
            scratch_shapes=list(scratch),
            input_output_aliases=aliases or {},
            compiler_params=pltpu.CompilerParams(
                dimension_semantics=("arbitrary",) * len(grid), vmem_limit_bytes=mib * MIB
            ),
            cost_estimate=pl.CostEstimate(flops=20000000000, bytes_accessed=40000000, transcendentals=0),
            name=name,
        )(*args, *([self.token] if linked else []))
        self.token = outs[-1]
        return outs[:-1]

    def gate(self, value):
        return self.call(
            "gate",
            lambda *_: None,
            [value],
            [ANY],
            [ANY],
            [shape_of(value.shape, value.dtype)],
            aliases={0: 0},
            mib=62,
        )[0]


BO, G1, B1, BD, G2, B2, QV, BU = range(8)


def start_all(copies):
    for copy in copies:
        copy.start()


def wait_all(copies):
    for copy in copies:
        copy.wait()


def copy_all(pairs, sems):
    copies = [pltpu.make_async_copy(a, b, sems.at[n]) for n, (a, b) in enumerate(pairs)]
    for copy in copies:
        copy.start()
    for copy in copies:
        copy.wait()


def chunk(ref, place, total=1, part=0):
    n = ref.shape[0] // CHUNKS
    first = pl.multiple_of(place * n + part * (n // total), n // total)
    return ref.at[pl.ds(first, n // total)]


def pack_heads_kernel(scal, wq, wk, wv, wo, qb, vb, bu, qkvo, table, sems):
    place, cols, width = scal[1], wq.shape[1], wo.shape[1]
    rows = width // CHUNKS
    half = rows // 2
    pairs = [
        (chunk(w, place), qkvo.at[:rows, n * cols : (n + 1) * cols])
        for n, w in enumerate((wq, wk, wv))
    ]
    out = chunk(wo, place)
    pairs.append((out.at[:, :cols], qkvo.at[:half, 3 * cols :]))
    pairs.append((out.at[:, cols:], qkvo.at[half:rows, 3 * cols :]))
    copies = [pltpu.make_async_copy(a, b, sems.at[n]) for n, (a, b) in enumerate(pairs)]
    start_all(copies)
    table[...] = jnp.zeros_like(table)
    table[0:1, :] = jnp.concatenate([qb[...].reshape(1, cols), vb[...].reshape(1, cols)], 1)
    lifted = bu[...]
    for n in range(lifted.shape[0] // width):
        table[1 + n : 2 + n, :] = lifted[n * width : (n + 1) * width].reshape(1, width)
    high = table[...].astype(BF)
    low = (table[...] - high.astype(F32)).astype(BF)
    pad = jnp.zeros((8, 2 * width), BF)
    qkvo[rows:, :] = jnp.concatenate([jnp.concatenate([high, low], 1), pad], 0)
    wait_all(copies)


def pack_units_kernel(scal, wu, wd, up, down, sems):
    place, width = scal[1], wd.shape[1]
    copy_all(
        [
            (chunk(wu, place), up),
            (chunk(wd, place, 2, 0), down.at[:, :width]),
            (chunk(wd, place, 2, 1), down.at[:, width:]),
        ],
        sems,
    )


def pack_inputs_kernel(scal, inputs, x_send, x_keep, sems):
    side, rows = scal[0], x_send.shape[0]
    copy_all(
        [
            (inputs.at[pl.ds((1 - side) * rows, rows)], x_send),
            (inputs.at[pl.ds(side * rows, rows)], x_keep),
        ],
        sems,
    )


def pack_cotangent_kernel(
    scal, cotangent, bo, g1, b1, bd, g2, b2, beside, e_send, e_keep, table, sems
):
    side = scal[0]
    rows, width = e_send.shape[0], e_send.shape[2]
    copy_all(
        [
            (cotangent.at[pl.ds((1 - side) * rows, rows)], e_send),
            (cotangent.at[pl.ds(side * rows, rows)], e_keep),
        ],
        sems,
    )
    for row, ref in ((BO, bo), (G1, g1), (B1, b1), (BD, bd), (G2, g2), (B2, b2)):
        table[row : row + 1, :] = ref[...].reshape(1, width)
    table[QV : QV + 8, :] = beside[...]


def pack(chain, name, kernel, hbm, small, outs, sems):
    return chain.call(
        name,
        kernel,
        [*hbm, *small],
        [SMEM] + [HBM] * (len(hbm) - 1) + [VMEM] * len(small),
        [VMEM] * len(outs),
        outs,
        scratch=[pltpu.SemaphoreType.DMA((sems,))],
    )


def attend_kernel(gathered, scal, *refs):
    if gathered:
        pieces, refs = refs[:CHUNKS], refs[CHUNKS:]
        xo, xr, seen, q_out, k_out, v_out, p_out, c_out, w, table, parts, sems = refs
    else:
        xo, xr, seen, table, wq, wk, wv, q_out, k_out, v_out, p_out, c_out = refs
    if gathered:

        @pl.when(pl.program_id(0) == 0)
        def _():
            cols, rows = w.shape[2], w.shape[1] // CHUNKS
            copies = [pltpu.make_async_copy(pieces[0].at[rows:], parts, sems.at[3, 0])]
            for d, piece in enumerate(pieces):
                at = pl.ds(pl.multiple_of((scal[1] ^ d) * rows, rows), rows)
                for n in range(3):
                    copies.append(
                        pltpu.make_async_copy(
                            piece.at[:rows, n * cols : (n + 1) * cols], w.at[n, at], sems.at[n, d]
                        )
                    )
            start_all(copies)
            wait_all(copies)
            width = table.shape[1]
            table[...] = parts[:8, :width].astype(F32) + parts[:8, width:].astype(F32)

        wq, wk, wv = w[0], w[1], w[2]
    else:
        wq, wk, wv = wq[...], wk[...], wv[...]
    cols = wq.shape[1]
    x = jnp.concatenate([xo[0], xr[0]], 0)
    q = (dot(x, wq) + table[0:1, :cols]).astype(BF) * jnp.asarray(HD**-0.5, BF)
    k = dot(x, wk).astype(BF)
    v = (dot(x, wv) + table[0:1, cols:]).astype(BF)
    q_out[...] = q
    k_out[...] = k
    v_out[...] = v
    bias = seen[0]
    low = lax.broadcasted_iota(jnp.int32, (x.shape[0], LANES), 1) < HD
    zero = jnp.zeros((), BF)
    for pair in range(cols // LANES):
        part = slice(pair * LANES, (pair + 1) * LANES)
        qp, kp, vp = q[:, part], k[:, part], v[:, part]
        joined = []
        for b in range(2):
            qm = jnp.where(low, qp, zero) if b == 0 else jnp.where(low, zero, qp)
            s = dot_nt(qm, kp) + bias
            e = jnp.exp(s - jnp.max(s, -1, keepdims=True))
            p = (e * (1.0 / jnp.sum(e, -1, keepdims=True))).astype(BF)
            p_out[0, pair * 2 + b] = p
            joined.append(dot(p, vp))
        c_out[:, part] = jnp.where(low, joined[0], joined[1]).astype(BF)


def attend(chain, scal, xo, xr, seen, table, weights):
    seqs, half, width = xo.shape
    span = 2 * half
    cols = width // 2
    heads = cols // HD
    gathered = table is None
    whole = pl.BlockSpec((1, half, width), lambda s: (s, 0, 0))
    in_specs = [whole, whole, pl.BlockSpec((1, 1, span), lambda s: (s, 0, 0))]
    rows = pl.BlockSpec((span, cols), lambda s: (s, 0))
    out_specs = [
        rows,
        rows,
        rows,
        pl.BlockSpec((1, heads, span, span), lambda s: (s, 0, 0, 0)),
        rows,
    ]
    out_shape = [shape_of((seqs * span, cols))] * 3 + [
        shape_of((seqs, heads, span, span)),
        shape_of((seqs * span, cols)),
    ]
    args = [xo, xr, seen]
    scratch = []
    if gathered:
        in_specs = [SMEM] + [ANY] * CHUNKS + in_specs
        args = [scal, *weights] + args
        out_specs += [held((3, width, cols)), held((8, width))]
        out_shape += [shape_of((3, width, cols)), shape_of((8, width), F32)]
        scratch = [pltpu.VMEM((16, 2 * width), BF), pltpu.SemaphoreType.DMA((4, CHUNKS))]
    else:
        in_specs = [SMEM] + in_specs + [held(table.shape)] + [held((width, cols))] * 3
        args = [scal] + args + [table, *weights]
    return chain.call(
        "attend",
        functools.partial(attend_kernel, gathered),
        args,
        in_specs,
        out_specs,
        out_shape,
        grid=(seqs,),
        scratch=scratch,
    )


def normed(hidden):
    centre = hidden - jnp.mean(hidden, -1, keepdims=True)
    scale = lax.rsqrt(jnp.mean(centre * centre, -1, keepdims=True) + EPSILON)
    return centre * scale, scale


def norm_back(upper, unit, scale, gain):
    through = upper * gain
    return scale * (
        through
        - jnp.mean(through, -1, keepdims=True)
        - unit * jnp.mean(through * unit, -1, keepdims=True)
    )


def gelu_and_slope(u):
    cdf = 0.5 + 0.5 * lax.erf(u * 0.7071067811865476)
    density = jnp.exp(-0.5 * u * u) * 0.3989422804014327
    return (u * cdf).astype(BF), (cdf + u * density).astype(BF)


ROWS = 128
COLUMNS = 256
FEW = 32


def folded(value):
    total = value[:8]
    for n in range(8, value.shape[0], 8):
        total = total + value[n : n + 8]
    return total


def put_chunks(place, value, first, out, rows, columns=slice(None)):
    for n in range(value.shape[0] // rows):
        out[place ^ (first + n), :, columns] = value[n * rows : (n + 1) * rows].astype(BF)


def weight_copies(place, own, pieces, targets, sems):
    wo, wu, wd = targets
    qkvo, up, down = pieces
    cols, width = wo.shape[1:]
    units = wu.shape[2]
    found = []

    def bring(a, b):
        found.append(pltpu.make_async_copy(a, b, sems.at[len(found)]))
        return found[-1]

    lists = [[bring(a, target.at[0])] for a, target in zip(own, targets, strict=True)]
    for d in range(CHUNKS):
        c = place ^ d
        n = cols // CHUNKS
        at = pl.ds(pl.multiple_of(c * n, n), n)
        m = width // CHUNKS
        p = units // CHUNKS // 2
        lists[0].append(bring(qkvo[d].at[:n, 3 * cols :], wo.at[1, at, :cols]))
        lists[0].append(bring(qkvo[d].at[n : 2 * n, 3 * cols :], wo.at[1, at, cols:]))
        lists[1].append(bring(up[d], wu.at[1, pl.ds(pl.multiple_of(c * m, m), m)]))
        for k in range(2):
            first = pl.multiple_of(c * 2 * p + k * p, p)
            lists[2].append(
                bring(down[d].at[:, k * width : (k + 1) * width], wd.at[1, pl.ds(first, p)])
            )
    return lists


def forward_kernel(scal, *refs):
    qkvo, up, down, refs = (
        refs[:CHUNKS],
        refs[CHUNKS : 2 * CHUNKS],
        refs[2 * CHUNKS : 3 * CHUNKS],
        refs[3 * CHUNKS :],
    )
    (
        xo,
        xr,
        eo,
        er,
        c_own,
        c_oth,
        table,
        table_oth,
        wo_own,
        wu_own,
        wd_own,
        out_own,
        out_send,
        r_out,
        sums,
        y_out,
        n_out,
        sl_own,
        sl_oth,
        dh_out,
        d_oth,
        d_oth_send,
        d_own,
        d_own_send,
        wo,
        wu,
        wd,
        active,
        slopes,
        unit_all,
        unit_low,
        y_all,
        dh_all,
        second,
        products,
        sums_8,
        sems,
        out_sems,
        product_sems,
    ) = refs
    step = pl.program_id(0)
    cols, width = wo.shape[1:]
    units = wu.shape[2]
    half = xo.shape[1]
    span = 2 * half
    tiles = units // width
    blocks = dh_all.shape[0] // span
    final = pl.num_programs(0) - 1

    bring_o, bring_u, bring_d = weight_copies(
        scal[1], (wo_own, wu_own, wd_own), (qkvo, up, down), (wo, wu, wd), sems
    )

    def saves(block):
        rows = pl.ds(block * span, span)
        return [
            pltpu.make_async_copy(a, b.at[rows], out_sems.at[n, block])
            for n, (a, b) in enumerate(
                (
                    (y_all.at[rows], y_out),
                    (unit_low.at[rows], n_out),
                    (slopes.at[0, rows], sl_own),
                    (slopes.at[1, rows], sl_oth),
                    (dh_all.at[rows], dh_out),
                )
            )
        ]

    def product_saves(side):
        targets = ((d_own, d_own_send), (d_oth, d_oth_send))[side]
        return [
            pltpu.make_async_copy(
                products.at[side, pl.ds(n * CHUNKS // 2, CHUNKS // 2)],
                target,
                product_sems.at[side, n],
            )
            for n, target in enumerate(targets)
        ]

    @pl.when(step == 0)
    def _():
        start_all(bring_o + bring_u + bring_d)
        sums_8[...] = jnp.zeros_like(sums_8)
        wait_all(bring_o)

    @pl.when(step < blocks)
    def _():
        base = step * span

        def rows_at(start, n):
            return pl.ds(pl.multiple_of(base + start, n), n)

        def line(row):
            return table[row : row + 1, :]

        for m in range(0, span, ROWS):
            source = xo if m < half else xr
            x = source[0, m % half : m % half + ROWS, :].astype(F32)
            first = (
                x
                + dot(c_own[m : m + ROWS, :], wo[0])
                + dot(c_oth[m : m + ROWS, :], wo[1])
                + line(BO)
            )
            for r in range(0, ROWS, FEW):
                unit, scale = normed(first[r : r + FEW])
                at = rows_at(m + r, FEW)
                unit_all[at, :] = unit
                unit_low[at, :] = unit.astype(BF)
                r_out[m + r : m + r + FEW, :] = scale
                y_all[at, :] = (unit * line(G1) + line(B1)).astype(BF)

        for side, biases, row in ((0, table, BU), (1, table_oth, 1)):

            @pl.when(step == 0)
            def _():
                wait_all(bring_u[1:] if side else bring_u[:1])

            for n in range(0, units, COLUMNS):
                tile, at = n // width, n % width
                bias = biases[row + tile : row + tile + 1, at : at + COLUMNS]
                for m in range(0, span, ROWS):
                    rows = rows_at(m, ROWS)
                    value, slope = gelu_and_slope(
                        dot(y_all[rows, :], wu[side, :, n : n + COLUMNS]) + bias
                    )
                    active[side * tiles + tile, rows, at : at + COLUMNS] = value
                    slopes[side, rows, n : n + COLUMNS] = slope

        @pl.when(step == 0)
        def _():
            wait_all(bring_d)

        for m in range(0, span, ROWS):
            rows = rows_at(m, ROWS)
            for n in range(0, width, COLUMNS):
                part = slice(n, n + COLUMNS)
                total = (
                    unit_all[rows, part] * table[G1 : G1 + 1, part]
                    + table[B1 : B1 + 1, part]
                    + table[BD : BD + 1, part]
                )
                for side in range(2):
                    for tile in range(tiles):
                        total = total + dot(
                            active[side * tiles + tile, rows, :],
                            wd[side, tile * width : (tile + 1) * width, part],
                        )
                second[m : m + ROWS, part] = total

        for m in range(0, span, FEW):
            unit, scale = normed(second[m : m + FEW, :])
            target, source = (out_own, eo) if m < half else (out_send, er)
            place = slice(m % half, m % half + FEW)
            target[0, place, :] = (unit * line(G2) + line(B2)).astype(BF)
            upper = source[0, place, :].astype(F32)
            back = norm_back(upper, unit, scale, line(G2))
            dh_all[rows_at(m, FEW), :] = back.astype(BF)
            sums_8[0] += folded(upper * unit)
            sums_8[1] += folded(upper)
            sums_8[2] += folded(back)

    for block in range(blocks):

        @pl.when(step == block)
        def _():
            start_all(saves(block))

    for tile in range(2 * tiles):

        @pl.when(step == blocks + tile)
        def _():
            side = 1 - tile // tiles
            rows = products.shape[2]
            for n in range(0, width, COLUMNS):
                part = slice(n, n + COLUMNS)
                value = dot_tn(active[side * tiles + tile % tiles], dh_all[:, part])
                put_chunks(
                    scal[1], value, tile % tiles * (width // rows), products.at[side], rows, part
                )
            if tile % tiles == tiles - 1:
                start_all(product_saves(side))

    @pl.when(step == final)
    def _():
        sums[...] = jnp.zeros_like(sums)
        for row in range(3):
            sums[row : row + 1, :] = jnp.sum(sums_8[row], 0, keepdims=True)
        for block in range(blocks):
            wait_all(saves(block))
        wait_all(product_saves(0) + product_saves(1))


def forward(chain, scal, pieces, xo, xr, eo, er, c_own, c_oth, table, table_oth, own):
    seqs, half, width = xo.shape
    span = 2 * half
    rows = seqs * span
    wo, wu, wd = own
    cols, units = wo.shape[0], wu.shape[1]
    blocks, tiles = seqs, units // width
    pair = pl.BlockSpec((1, half, width), lambda i: (jnp.minimum(i, blocks - 1), 0, 0))
    kept = (CHUNKS // 2, units // CHUNKS, width)

    def block(n):
        return pl.BlockSpec((span, n), lambda i: (jnp.minimum(i, blocks - 1), 0))

    in_specs = (
        [SMEM]
        + [ANY] * (3 * CHUNKS)
        + [pair] * 4
        + [block(cols)] * 2
        + [fixed(table.shape), fixed(table_oth.shape)]
        + [ANY] * 3
    )
    out_specs = [pair, pair, block(1), fixed((8, width))] + [ANY] * 9
    out_shape = [
        shape_of((seqs, half, width)),
        shape_of((seqs, half, width)),
        shape_of((rows, 1), F32),
        shape_of((8, width), F32),
        shape_of((rows, width)),
        shape_of((rows, width)),
        shape_of((rows, units)),
        shape_of((rows, units)),
        shape_of((rows, width)),
    ] + [shape_of(kept)] * 4
    return chain.call(
        "forward",
        forward_kernel,
        [scal, *pieces, xo, xr, eo, er, c_own, c_oth, table, table_oth, wo, wu, wd],
        in_specs,
        out_specs,
        out_shape,
        grid=(blocks + 2 * tiles,),
        scratch=[
            pltpu.VMEM((2, *wo.shape), BF),
            pltpu.VMEM((2, *wu.shape), BF),
            pltpu.VMEM((2, *wd.shape), BF),
            pltpu.VMEM((2 * tiles, rows, width), BF),
            pltpu.VMEM((2, rows, units), BF),
            pltpu.VMEM((rows, width), F32),
            pltpu.VMEM((rows, width), BF),
            pltpu.VMEM((rows, width), BF),
            pltpu.VMEM((rows, width), BF),
            pltpu.VMEM((span, width), F32),
            pltpu.VMEM((2, CHUNKS, *kept[1:]), BF),
            pltpu.VMEM((3, 8, width), F32),
            pltpu.SemaphoreType.DMA((3 + 5 * CHUNKS,)),
            pltpu.SemaphoreType.DMA((5, blocks)),
            pltpu.SemaphoreType.DMA((2, 2)),
        ],
    )


S_G2, S_B2, S_BD, S_G1, S_B1, S_BO, S_BU = range(7)
S_QV = 8


def backward_kernel(scal, *refs):
    qkvo, up, down, refs = (
        refs[:CHUNKS],
        refs[CHUNKS : 2 * CHUNKS],
        refs[2 * CHUNKS : 3 * CHUNKS],
        refs[3 * CHUNKS :],
    )
    (
        table,
        sums2,
        scale,
        y_in,
        c_in_own,
        c_in_oth,
        dh_in,
        unit_in,
        sl_in_own,
        sl_in_oth,
        wo_own,
        wu_own,
        wd_own,
        d1_out,
        dc_own,
        dc_oth,
        sums,
        u_oth,
        u_oth_send,
        u_own,
        u_own_send,
        wo,
        wu,
        wd,
        y,
        c,
        dh,
        unit,
        slopes,
        lifted_all,
        d1_all,
        total,
        products,
        sums_8,
        sems,
        in_sems,
        product_sems,
    ) = refs
    step = pl.program_id(0)
    span, width = d1_out.shape
    cols, units = wo.shape[1], wu.shape[2]
    tiles = units // width
    blocks = d1_all.shape[0] // span
    final = pl.num_programs(0) - 1
    bring_o, bring_u, bring_d = weight_copies(
        scal[1], (wo_own, wu_own, wd_own), (qkvo, up, down), (wo, wu, wd), sems
    )

    def bring_rows(n, source, target, block):
        rows = pl.ds(block * span, span)
        return pltpu.make_async_copy(source.at[rows], target.at[rows], in_sems.at[n, block])

    bring = [
        (
            bring_rows(0, dh_in, dh, block),
            bring_rows(1, sl_in_oth, slopes.at[1], block),
            bring_rows(2, sl_in_own, slopes.at[0], block),
            bring_rows(3, unit_in, unit, block),
        )
        for block in range(blocks)
    ]
    bring_last = [
        bring_rows(4 + n, source, target, block)
        for block in range(blocks)
        for n, (source, target) in enumerate(
            ((y_in, y), (c_in_own, c.at[0]), (c_in_oth, c.at[1]))
        )
    ]

    def product_saves(side):
        targets = ((u_own, u_own_send), (u_oth, u_oth_send))[side]
        return [
            pltpu.make_async_copy(
                products.at[side, pl.ds(n * CHUNKS // 2, CHUNKS // 2)],
                target,
                product_sems.at[side, n],
            )
            for n, target in enumerate(targets)
        ]

    @pl.when(step == 0)
    def _():
        bring[0][0].start()
        start_all(bring_d[1:])
        bring[0][1].start()
        bring_d[0].start()
        bring[0][2].start()
        start_all(bring_u[1:] + bring_u[:1])
        bring[0][3].start()
        start_all(bring_o)
        for later in bring[1:]:
            start_all(later)
        start_all(bring_last)
        sums[...] = jnp.zeros_like(sums)
        sums_8[...] = jnp.zeros_like(sums_8)
        for side in range(2):
            sums[side, S_G2 : S_BD + 1, :] = sums2[:3, :]

    for block in range(blocks):

        @pl.when(step == block)
        def _():
            wait_all(bring[block][:2] if block == 0 else bring[block])

    @pl.when(step < blocks)
    def _():
        rows = pl.ds(pl.multiple_of(step * span, span), span)

        def rows_at(start, n):
            return pl.ds(pl.multiple_of(step * span + start, n), n)

        for side in (1, 0):

            @pl.when(step == 0)
            def _():
                wait_all(bring_d[1:] if side else bring_d[:1] + [bring[0][2]])

            for n in range(0, units, COLUMNS):
                tile, at = n // width, n % width
                added = jnp.zeros((8, COLUMNS), F32)
                value = dot_nt(dh[rows, :], wd[side, n : n + COLUMNS, :])
                for m in range(0, span, ROWS):
                    few = rows_at(m, ROWS)
                    lifted = (
                        value[m : m + ROWS] * slopes[side, few, n : n + COLUMNS].astype(F32)
                    ).astype(BF)
                    lifted_all[side * tiles + tile, few, at : at + COLUMNS] = lifted
                    added = added + folded(lifted.astype(F32))
                sums[side, S_BU + tile : S_BU + tile + 1, at : at + COLUMNS] += jnp.sum(
                    added, 0, keepdims=True
                )

        @pl.when(step == 0)
        def _():
            wait_all(bring_u + [bring[0][3]])

        for n in range(0, width, COLUMNS):
            part = slice(n, n + COLUMNS)
            upper = dh[rows, part].astype(F32)
            for side in (1, 0):
                for tile in range(tiles):
                    upper = upper + dot_nt(
                        lifted_all[side * tiles + tile, rows, :],
                        wu[side, part, tile * width : (tile + 1) * width],
                    )
            total[:, part] = upper
        for m in range(0, span, FEW):
            part = slice(m, m + FEW)
            few = rows_at(m, FEW)
            upper = total[part, :]
            normal = unit[few, :].astype(F32)
            back = norm_back(upper, normal, scale[part, :], table[G1 : G1 + 1, :])
            sums_8[0] += folded(upper * normal)
            sums_8[1] += folded(upper)
            sums_8[2] += folded(back)
            lower = back.astype(BF)
            d1_out[part, :] = lower
            d1_all[few, :] = lower

        @pl.when(step == 0)
        def _():
            wait_all(bring_o)

        lower = d1_out[...]
        dc_own[...] = dot_nt(lower, wo[0]).astype(BF)
        dc_oth[...] = dot_nt(lower, wo[1]).astype(BF)

    for tile in range(2 * tiles):

        @pl.when(step == blocks + tile)
        def _():
            if tile == 0:
                wait_all(bring_last)
            side = 1 - tile // tiles
            count = products.shape[2]
            for n in range(0, width, COLUMNS):
                value = dot_tn(y[...], lifted_all[side * tiles + tile % tiles, :, n : n + COLUMNS])
                at = tile % tiles * width + n
                put_chunks(
                    scal[1], value, 0, products.at[side], count, slice(at, at + COLUMNS)
                )
            if tile % tiles == 0:
                n = cols // CHUNKS
                for m in range(2):
                    value = dot_tn(c[side], d1_all[:, m * cols : (m + 1) * cols])
                    for k in range(CHUNKS):
                        products[
                            side, scal[1] ^ k, m * n : (m + 1) * n, units : units + cols
                        ] = value[k * n : (k + 1) * n].astype(BF)
            if tile % tiles == tiles - 1:
                start_all(product_saves(side))

    @pl.when(step == final)
    def _():
        for n, row in enumerate((S_G1, S_B1, S_BO)):
            line = jnp.sum(sums_8[n], 0, keepdims=True)
            sums[0, row : row + 1, :] = line
            sums[1, row : row + 1, :] = line
        wait_all(product_saves(0) + product_saves(1))


def backward(
    chain, scal, pieces, table, sums2, y, c_own, c_oth, dh, unit, scale, slopes, own, span
):
    rows, width = dh.shape
    wo, wu, wd = own
    cols, units = wo.shape[0], wu.shape[1]
    blocks, tiles = rows // span, units // width
    kept = (CHUNKS // 2, width // CHUNKS, units + cols)

    def block(n):
        return pl.BlockSpec((span, n), lambda i: (jnp.minimum(i, blocks - 1), 0))

    in_specs = (
        [SMEM]
        + [ANY] * (3 * CHUNKS)
        + [fixed(table.shape), fixed(sums2.shape), block(1)]
        + [ANY] * 10
    )
    out_specs = [block(width), block(cols), block(cols), fixed((2, 16, width))] + [ANY] * 4
    out_shape = [
        shape_of((rows, width)),
        shape_of((rows, cols)),
        shape_of((rows, cols)),
        shape_of((2, 16, width), F32),
    ] + [shape_of(kept)] * 4
    return chain.call(
        "backward",
        backward_kernel,
        [scal, *pieces, table, sums2, scale, y, c_own, c_oth, dh, unit, *slopes, *own],
        in_specs,
        out_specs,
        out_shape,
        grid=(blocks + 2 * tiles,),
        scratch=[
            pltpu.VMEM((2, *wo.shape), BF),
            pltpu.VMEM((2, *wu.shape), BF),
            pltpu.VMEM((2, *wd.shape), BF),
            pltpu.VMEM((rows, width), BF),
            pltpu.VMEM((2, rows, cols), BF),
            pltpu.VMEM((rows, width), BF),
            pltpu.VMEM((rows, width), BF),
            pltpu.VMEM((2, rows, units), BF),
            pltpu.VMEM((2 * tiles, rows, width), BF),
            pltpu.VMEM((rows, width), BF),
            pltpu.VMEM((span, width), F32),
            pltpu.VMEM((2, CHUNKS, *kept[1:]), BF),
            pltpu.VMEM((3, 8, width), F32),
            pltpu.SemaphoreType.DMA((3 + 5 * CHUNKS,)),
            pltpu.SemaphoreType.DMA((7, blocks)),
            pltpu.SemaphoreType.DMA((2, 2)),
        ],
    )


def attend_back_kernel(
    side,
    scal,
    xo,
    xr,
    p_in,
    q_in,
    k_in,
    v_in,
    c_in,
    dc_in,
    vectors,
    grads,
    keep,
    send,
    total,
    table,
    products,
    sems,
):
    step = pl.program_id(0)
    final = pl.num_programs(0) - 1
    span, cols = q_in.shape
    width = total.shape[0]
    rows = width // CHUNKS
    low = lax.broadcasted_iota(jnp.int32, (span, LANES), 1) < HD
    zero = jnp.zeros((), BF)
    x = jnp.concatenate([xo[0], xr[0]], 0)

    @pl.when(step == 0)
    def _():
        table[...] = vectors[side]
        products[...] = jnp.zeros_like(products)

    for pair in range(cols // LANES):
        part = slice(pair * LANES, (pair + 1) * LANES)
        qp, kp, vp, dcp = q_in[:, part], k_in[:, part], v_in[:, part], dc_in[:, part]
        shared = dcp.astype(F32) * c_in[:, part].astype(F32)
        found = []
        for b in range(2):
            dcm = jnp.where(low, dcp, zero) if b == 0 else jnp.where(low, zero, dcp)
            centre = jnp.sum(
                jnp.where(low, shared, 0.0) if b == 0 else jnp.where(low, 0.0, shared),
                -1,
                keepdims=True,
            )
            p = p_in[0, pair * 2 + b]
            ds = (p.astype(F32) * (dot_nt(dcm, vp) - centre)).astype(BF)
            found.append((dot(ds, kp) * HD**-0.5, dot_tn(ds, qp), dot_tn(p, dcp)))
        for n in range(3):
            at = n * cols + pair * LANES
            grads[:, at : at + LANES] = jnp.where(low, found[0][n], found[1][n]).astype(BF)
    for m, n in enumerate((0, 2)):
        table[S_QV : S_QV + 1, m * cols : (m + 1) * cols] += jnp.sum(
            grads[:, n * cols : (n + 1) * cols].astype(F32), 0, keepdims=True
        )
    for n in range(0, 3 * cols, cols):
        part = slice(n, n + cols)
        value = dot_tn(x, grads[:, part])

        @pl.when(step == 0)
        def _():
            total[:, part] = value

        @pl.when((step > 0) & (step < final))
        def _():
            total[:, part] += value

        @pl.when(step == final)
        def _():
            if n == 0:
                high = table[...].astype(BF).astype(F32)
                low_part = table[...] - high
                blank = jnp.zeros((8 - 2, width), F32)
                for m in range(CHUNKS):
                    at = slice(2 * m, 2 * m + 2)
                    products[scal[1] ^ m, rows:, :width] = jnp.concatenate(
                        [high[at], blank, low_part[at], blank], 0
                    ).astype(BF)
            for m in range(CHUNKS):
                at = slice(m * rows, (m + 1) * rows)
                products[scal[1] ^ m, :rows, part] = (total[at, part] + value[at]).astype(BF)

    @pl.when(step == final)
    def _():
        copies = [
            pltpu.make_async_copy(products.at[: CHUNKS // 2], keep, sems.at[0]),
            pltpu.make_async_copy(products.at[CHUNKS // 2 :], send, sems.at[1]),
        ]
        start_all(copies)
        wait_all(copies)


def attend_back(chain, scal, xo, xr, p, q, k, v, c, dc, vectors, side):
    seqs, half, width = xo.shape
    span = 2 * half
    cols = q.shape[1]
    heads = cols // HD
    whole = pl.BlockSpec((1, half, width), lambda s: (s, 0, 0))
    rows = pl.BlockSpec((span, cols), lambda s: (s, 0))
    kept = (CHUNKS // 2, width // CHUNKS + 16, 3 * cols)
    return chain.call(
        "attend_back",
        functools.partial(attend_back_kernel, side),
        [scal, xo, xr, p, q, k, v, c, dc, vectors],
        [SMEM, whole, whole]
        + [pl.BlockSpec((1, heads, span, span), lambda s: (s, 0, 0, 0))]
        + [rows] * 5
        + [held(vectors.shape)],
        [pl.BlockSpec((span, 3 * cols), lambda s: (s, 0)), ANY, ANY],
        [shape_of((seqs * span, 3 * cols)), shape_of(kept), shape_of(kept)],
        grid=(seqs,),
        scratch=[
            pltpu.VMEM((width, 3 * cols), F32),
            pltpu.VMEM(vectors.shape[1:], F32),
            pltpu.VMEM((CHUNKS, *kept[1:]), BF),
            pltpu.SemaphoreType.DMA((2,)),
        ],
    )


def inputs_back_kernel(d1, own, oth, wq, wk, wv, w_oth, dx_own, dx_send):
    cols = wq.shape[1]
    total = d1[...].astype(F32)
    for n, w in enumerate((wq, wk, wv)):
        part = slice(n * cols, (n + 1) * cols)
        total = total + dot_nt(own[:, part], w[...]) + dot_nt(oth[:, part], w_oth[n])
    total = total.astype(BF)
    half = dx_own.shape[1]
    dx_own[0] = total[:half]
    dx_send[0] = total[half:]


def inputs_back(chain, d1, own, oth, weights, w_oth, half):
    rows, width = d1.shape
    cols = weights[0].shape[1]
    pair = pl.BlockSpec((1, half, width), lambda i: (i, 0, 0))
    out = shape_of((rows // (2 * half), half, width))
    return chain.call(
        "inputs_back",
        inputs_back_kernel,
        [d1, own, oth, *weights, w_oth],
        [pl.BlockSpec((2 * half, width), lambda i: (i, 0))]
        + [pl.BlockSpec((2 * half, 3 * cols), lambda i: (i, 0))] * 2
        + [fixed((width, cols))] * 3
        + [fixed(w_oth.shape)],
        [pair, pair],
        [out, out],
        grid=(rows // (2 * half),),
    )


def combine_kernel(groups, *refs):
    taken = sum(terms for terms, _, _ in groups)
    ins, outs = refs[:taken], list(refs[taken:])
    for terms, split, vectors in groups:
        mine, ins = ins[:terms], ins[terms:]
        chunks, rows = mine[0].shape[:2]
        plain = rows - 16 if vectors else rows
        keep = outs.pop(0)
        send = outs.pop(0) if split else None
        for n in range(chunks):
            out, at = (keep, n) if not split or n < chunks // 2 else (send, n - chunks // 2)
            total = mine[0][n, :plain].astype(F32)
            for term in mine[1:]:
                total = total + term[n, :plain].astype(F32)
            out[at, :plain] = total.astype(BF)
            if vectors:
                both = mine[0][n, plain:].astype(F32)
                for term in mine[1:]:
                    both = both + term[n, plain:].astype(F32)
                both = both[:8] + both[8:]
                high = both.astype(BF).astype(F32)
                out[at, plain:] = jnp.concatenate([high, both - high], 0).astype(BF)


def combine(chain, *groups):
    args, out_shape, plan = [], [], []
    for terms, split, *vectors in groups:
        args += terms
        plan.append((len(terms), split, bool(vectors)))
        dims = terms[0].shape
        if split:
            out_shape += [shape_of((dims[0] // 2, *dims[1:]))] * 2
        else:
            out_shape += [shape_of(dims)]
    return chain.call(
        "combine",
        functools.partial(combine_kernel, plan),
        args,
        [VMEM] * len(args),
        [VMEM] * len(out_shape),
        out_shape,
        mib=20,
    )


def stack_kernel(one, two, out):
    n = one.shape[0]
    out[:n] = one[...]
    out[n:] = two[...]


def stack(chain, one, two):
    dims = (one.shape[0] + two.shape[0], *one.shape[1:])
    return chain.call(
        "stack", stack_kernel, [one, two], [VMEM, VMEM], [VMEM], [shape_of(dims)], mib=20
    )[0]


def join_kernel(scal, mine, got, out):
    rows = mine.shape[0]
    out[pl.ds(scal[0] * rows, rows)] = mine[...]
    out[pl.ds((1 - scal[0]) * rows, rows)] = got[...]


def join(chain, scal, mine, got):
    dims = (2 * mine.shape[0], *mine.shape[1:])
    return chain.call(
        "join",
        join_kernel,
        [scal, mine, got],
        [SMEM, VMEM, VMEM],
        [VMEM],
        [shape_of(dims)],
        mib=20,
    )[0]


def assemble_kernel(widths, cols, scal, one, two, *outs):
    for d in range(CHUNKS):
        part, m = (one, d) if d < CHUNKS // 2 else (two, d - CHUNKS // 2)
        c = scal[1] ^ d
        left = 0
        for out, (rows, cuts) in zip(outs, widths):
            at = pl.multiple_of(c * rows, rows)
            cut = out.shape[1] // cuts
            for n in range(cuts):
                out[pl.ds(at, rows), n * cut : (n + 1) * cut] = part[
                    m, n * rows : (n + 1) * rows, left : left + cut
                ].astype(F32)
            left += cut
    if not cols:
        return
    outs, table = outs[len(widths) : -1], outs[-1]
    plain, width = one.shape[1] - 16, table.shape[2]
    for d in range(CHUNKS):
        part, m = (one, d) if d < CHUNKS // 2 else (two, d - CHUNKS // 2)
        both = part[m, plain:, :width].astype(F32)
        table[scal[1] ^ d] = both[:8] + both[8:]

    def line(row):
        return table[row // 2, row % 2 : row % 2 + 1, :]

    for row in range(S_BU):
        outs[row][...] = line(row).reshape(width)
    bu, qb, vb = outs[S_BU:]
    for n in range(bu.shape[0] // width):
        bu[n * width : (n + 1) * width] = line(S_BU + n).reshape(width)
    qb[...] = line(S_QV)[:, :cols].reshape(cols)
    vb[...] = line(S_QV)[:, cols:].reshape(cols)


def assemble(chain, scal, parts, widths, vectors=()):
    out_shape = [shape_of((CHUNKS * rows, columns), F32) for rows, columns, _ in widths]
    out_shape += [shape_of((n,), F32) for n in vectors]
    plan = [(rows, cuts) for rows, _, cuts in widths]
    cols = vectors[-1] if vectors else 0
    scratch = [pltpu.VMEM((CHUNKS, 8, vectors[0]), F32)] if vectors else []
    return chain.call(
        "assemble",
        functools.partial(assemble_kernel, plan, cols),
        [scal, *parts],
        [SMEM] + [VMEM] * 2,
        [VMEM] * len(out_shape),
        out_shape,
        scratch=scratch,
        mib=20,
    )


def tensor_layer(
    dp,
    inputs,
    lengths,
    query_weight,
    query_bias,
    key_weight,
    value_weight,
    value_bias,
    output_weight,
    output_bias,
    first_gain,
    first_shift,
    up_weight,
    up_bias,
    down_weight,
    down_bias,
    second_gain,
    second_shift,
    cotangent,
):
    bits = dp.bit_length() - 1
    count, half, width = inputs.shape
    cols, units = query_weight.shape[1], up_weight.shape[1]
    seqs = count // 2
    side = lax.axis_index("tensor")
    spot = lax.axis_index("dp")
    core, across, deep = spot & 1, (spot >> 1) & 1, (spot >> 2) & 1
    scal = jnp.stack([side, core * 4 + across * 2 + deep]).astype(jnp.int32)
    chain = Chain()

    def swap(value):
        return lax.ppermute(value, "tensor", [(0, 1), (1, 0)])

    def flip(value, bit):
        return lax.ppermute(value, "dp", [(i, i ^ (1 << bit)) for i in range(dp)])

    def flip_far(value):
        return lax.ppermute(value, "dp", [(i, i ^ 6) for i in range(dp)])

    def fetch(piece):
        first = chain.gate(swap(piece))
        found = [first, flip(first, 2), flip(first, 1), flip_far(first)]
        return found + [flip(one, 0) for one in found]

    qkv = [query_weight, key_weight, value_weight]
    own = [output_weight, up_weight, down_weight]
    cut = width // CHUNKS
    flat = shape_of((seqs, half, width))
    qkvo, table_own = pack(
        chain,
        "pack_heads",
        pack_heads_kernel,
        [scal, *qkv, output_weight],
        [query_bias, value_bias, up_bias],
        [shape_of((cut + 16, 4 * cols)), shape_of((8, width), F32)],
        5,
    )
    up, down = pack(
        chain,
        "pack_units",
        pack_units_kernel,
        [scal, up_weight, down_weight],
        [],
        [shape_of((cut, units)), shape_of((cut, 2 * width))],
        3,
    )
    x_send, xo = pack(
        chain, "pack_inputs", pack_inputs_kernel, [scal, inputs], [], [flat, flat], 2
    )
    xr = swap(x_send)
    qkvo, up, down = fetch(qkvo), fetch(up), fetch(down)

    lens = lax.dynamic_slice_in_dim(lengths, side * seqs, seqs, 0)
    at = jnp.arange(half)
    position = jnp.concatenate([side * half + at, (1 - side) * half + at])
    seen = jnp.where(position[None, :] < lens[:, None], 0.0, MASKED).astype(F32)[:, None, :]

    q_own, k_own, v_own, p_own, c_own = attend(chain, scal, xo, xr, seen, table_own, qkv)
    e_send, eo, table = pack(
        chain,
        "pack_cotangent",
        pack_cotangent_kernel,
        [scal, cotangent],
        [
            output_bias,
            first_gain,
            first_shift,
            down_bias,
            second_gain,
            second_shift,
            table_own,
        ],
        [flat, flat, shape_of((16, width), F32)],
        2,
    )
    er = swap(e_send)
    q_oth, k_oth, v_oth, p_oth, c_oth, w_oth, table_oth = attend(
        chain, scal, xo, xr, seen, None, qkvo
    )
    (
        out_own,
        out_send,
        scale,
        sums2,
        y,
        unit,
        sl_own,
        sl_oth,
        dh,
        d_oth,
        d_oth_send,
        d_own,
        d_own_send,
    ) = forward(
        chain, scal, qkvo + up + down, xo, xr, eo, er, c_own, c_oth, table, table_oth, own
    )
    d_own_got = flip(d_own_send, 0)
    (d_oth,) = combine(chain, ([d_oth, flip(d_oth_send, 0)], False))
    d_got = swap(d_oth)
    d1, dc_own, dc_oth, table_back, u_oth, u_oth_send, u_own, u_own_send = backward(
        chain,
        scal,
        qkvo + up + down,
        table,
        sums2,
        y,
        c_own,
        c_oth,
        dh,
        unit,
        scale,
        (sl_own, sl_oth),
        own,
        2 * half,
    )
    u_oth_got, u_own_got = flip(u_oth_send, 0), flip(u_own_send, 0)
    d_keep, d_send = combine(chain, ([d_own, d_own_got, d_got], True))
    d_got = flip(d_send, 1)
    (u_oth,) = combine(chain, ([u_oth, u_oth_got], False))
    u_got = swap(u_oth)
    g_oth, q_oth, q_oth_send = attend_back(
        chain, scal, xo, xr, p_oth, q_oth, k_oth, v_oth, c_oth, dc_oth, table_back, 1
    )
    q_got = flip(q_oth_send, 0)
    d_keep, d_send = combine(chain, ([d_keep, d_got], True))
    d_got = flip(d_send, 2)
    (q_oth,) = combine(chain, ([q_oth, q_got], False, True))
    q_got = swap(q_oth)
    g_own, q_own, q_own_send = attend_back(
        chain, scal, xo, xr, p_own, q_own, k_own, v_own, c_own, dc_own, table_back, 0
    )
    q_own_got = flip(q_own_send, 0)
    (d_keep,) = combine(chain, ([d_keep, d_got], False))
    d_got = flip(d_keep, 3)
    u_keep, u_send = combine(chain, ([u_own, u_own_got, u_got], True))
    u_got = flip(u_send, 1)
    dx_own, dx_send = inputs_back(chain, d1, g_own, g_oth, qkv, w_oth, half)
    dx_got = swap(dx_send)
    (d_sum,) = combine(chain, ([d_keep, d_got], False))

    def rest(value, *vectors):
        for bit in range(4, bits):
            (value,) = combine(chain, ([value, flip(value, bit)], False, *vectors))
        return value

    d_sum = rest(d_sum)
    d_got = flip(d_sum, 2)
    q_keep, q_send = combine(chain, ([q_own, q_own_got, q_got], True, True))
    q_got = flip(q_send, 1)
    out_got = swap(chain.gate(out_send))
    u_keep, u_send = combine(chain, ([u_keep, u_got], True))
    u_got = flip(u_send, 2)
    d_two = stack(chain, d_sum, d_got)
    d_got = flip(d_two, 1)
    q_keep, q_send = combine(chain, ([q_keep, q_got], True, True))
    q_got = flip(q_send, 2)
    (u_keep,) = combine(chain, ([u_keep, u_got], False))
    u_got = flip(u_keep, 3)
    (q_keep,) = combine(chain, ([q_keep, q_got], False, True))
    q_got = flip(q_keep, 3)
    d_four = stack(chain, d_two, d_got)
    d_got = flip(d_four, 0)
    (u_sum,) = combine(chain, ([u_keep, u_got], False))
    u_sum = rest(u_sum)
    u_got = flip(u_sum, 2)
    inputs_gradient = join(chain, scal, dx_own, dx_got)
    (q_sum,) = combine(chain, ([q_keep, q_got], False, True))
    q_sum = rest(q_sum, True)
    q_got = flip(q_sum, 2)
    u_two = stack(chain, u_sum, u_got)
    u_got = flip(u_two, 1)
    rows = width // CHUNKS
    (down_back,) = assemble(chain, scal, (d_four, d_got), [(2 * rows, width, 1)])
    q_two = stack(chain, q_sum, q_got)
    q_got = flip(q_two, 1)
    result = join(chain, scal, out_own, out_got)
    u_four = stack(chain, u_two, u_got)
    u_got = flip(u_four, 0)
    q_four = stack(chain, q_two, q_got)
    q_got = flip(q_four, 0)
    up_back, out_back = assemble(
        chain, scal, (u_four, u_got), [(rows, units, 1), (rows // 2, width, 2)]
    )
    query_back, key_back, value_back, g2b, b2b, bdb, g1b, b1b, bob, bub, qbb, vbb = assemble(
        chain,
        scal,
        (q_four, q_got),
        [(rows, cols, 1)] * 3,
        (width,) * 6 + (units, cols, cols),
    )
    return (
        result,
        inputs_gradient,
        query_back,
        qbb,
        key_back,
        value_back,
        vbb,
        out_back,
        bob,
        g1b,
        b1b,
        up_back,
        bub,
        down_back,
        bdb,
        g2b,
        b2b,
    )


def solution(mesh):
    in_specs = (
        P("dp", "tensor", None),
        P("dp"),
        P(None, "tensor"),
        P("tensor"),
        P(None, "tensor"),
        P(None, "tensor"),
        P("tensor"),
        P("tensor", None),
        P(),
        P(),
        P(),
        P(None, "tensor"),
        P("tensor"),
        P("tensor", None),
        P(),
        P(),
        P(),
        P("dp", "tensor", None),
    )
    out_specs = (
        P("dp", "tensor", None),
        P("dp", "tensor", None),
        P(None, "tensor"),
        P("tensor"),
        P(None, "tensor"),
        P(None, "tensor"),
        P("tensor"),
        P("tensor", None),
        P(),
        P(),
        P(),
        P(None, "tensor"),
        P("tensor"),
        P("tensor", None),
        P(),
        P(),
        P(),
    )
    return jax.shard_map(
        functools.partial(tensor_layer, mesh.shape["dp"]),
        mesh=mesh,
        in_specs=in_specs,
        out_specs=out_specs,
        check_vma=False,
    )
```

```python
import functools

import jax
import jax.numpy as jnp
from jax import lax
from jax.experimental import pallas as pl
from jax.experimental.pallas import tpu as pltpu
from jax.sharding import Mesh
from jax.sharding import PartitionSpec as P

HD = 64
EPSILON = 1e-06
MASKED = -1000000000.0
BF = jnp.bfloat16
F32 = jnp.float32
MIB = 1024 * 1024
LANES = 128
CHUNKS = 8
DP = ("rest", "across", "core")
COSTS = (12, 6, 1, 40, 0.3, 20, 6, 6, 3, 3, 40, 20, 6, 20, 6, 3, 12, 6, 6, 3, 6, 12, 1, 0.3, 6, 20, 40, 6, 20, 20, 1, 20, 12, 3, 6, 3, 3, 3, 12, 20, 12, 0.3, 40, 6)

ANY = pl.BlockSpec(memory_space=pl.ANY)
HBM = pl.BlockSpec(memory_space=pltpu.HBM)
SMEM = pl.BlockSpec(memory_space=pltpu.SMEM)
VMEM = pl.BlockSpec(memory_space=pltpu.VMEM)


def dot(left, right):
    return lax.dot_general(left, right, (((1,), (0,)), ((), ())), preferred_element_type=F32)


def dot_nt(left, right):
    return lax.dot_general(left, right, (((1,), (1,)), ((), ())), preferred_element_type=F32)


def dot_tn(left, right):
    return lax.dot_general(left, right, (((0,), (0,)), ((), ())), preferred_element_type=F32)


def shape_of(dims, kind=BF):
    return jax.ShapeDtypeStruct(dims, kind)


def fixed(dims):
    return pl.BlockSpec(dims, lambda *_: (0,) * len(dims))


def held(dims):
    return pl.BlockSpec(dims, lambda *_: (0,) * len(dims), pipeline_mode=pl.Buffered(1))


class Chain:
    def __init__(self):
        self.token = None
        self.count = 0

    def call(self, name, body, args, in_specs, out_specs, out_shape, grid=(), scratch=(), mib=62, aliases=None):
        taken, given = len(args), len(out_shape)
        linked = self.token is not None

        def kernel(*refs):
            rest = refs[taken + linked :]
            body(*refs[:taken], *rest[:given], *rest[given + 1 :])

        outs = pl.pallas_call(
            kernel,
            grid=grid,
            in_specs=list(in_specs) + [ANY] * linked,
            out_specs=list(out_specs) + [ANY],
            out_shape=list(out_shape) + [shape_of((8, LANES), F32)],
            scratch_shapes=list(scratch),
            input_output_aliases=aliases or {},
            compiler_params=pltpu.CompilerParams(
                dimension_semantics=("arbitrary",) * len(grid), vmem_limit_bytes=mib * MIB
            ),
            cost_estimate=pl.CostEstimate(
                flops=int(COSTS[self.count % len(COSTS)] * 1.1e9),
                bytes_accessed=1000,
                transcendentals=0,
            ),
            name=name,
        )(*args, *([self.token] if linked else []))
        self.token = outs[-1]
        self.count += 1
        return outs[:-1]

    def gate(self, *values):
        outs = self.call(
            "gate",
            lambda *_: None,
            list(values),
            [ANY] * len(values),
            [ANY] * len(values),
            [shape_of(value.shape, value.dtype) for value in values],
            aliases={n: n for n in range(len(values))},
        )
        return outs[0] if len(values) == 1 else outs


BO, G1, B1, BD, G2, B2, QV, BU = range(8)


def start_all(copies):
    for copy in copies:
        copy.start()


def wait_all(copies):
    for copy in copies:
        copy.wait()


def copy_all(pairs, sems):
    copies = [pltpu.make_async_copy(a, b, sems.at[n]) for n, (a, b) in enumerate(pairs)]
    for copy in copies:
        copy.start()
    for copy in copies:
        copy.wait()


def chunk(ref, place, total=1, part=0):
    n = ref.shape[0] // CHUNKS
    first = pl.multiple_of(place * n + part * (n // total), n // total)
    return ref.at[pl.ds(first, n // total)]


def pack_heads_kernel(scal, wq, wk, wv, wo, qb, vb, bu, qkvo, table, sems):
    place, cols, width = scal[1], wq.shape[1], wo.shape[1]
    rows = width // CHUNKS
    half = rows // 2
    pairs = [
        (chunk(w, place), qkvo.at[:rows, n * cols : (n + 1) * cols])
        for n, w in enumerate((wq, wk, wv))
    ]
    out = chunk(wo, place)
    pairs.append((out.at[:, :cols], qkvo.at[:half, 3 * cols :]))
    pairs.append((out.at[:, cols:], qkvo.at[half:rows, 3 * cols :]))
    copies = [pltpu.make_async_copy(a, b, sems.at[n]) for n, (a, b) in enumerate(pairs)]
    start_all(copies)
    table[...] = jnp.zeros_like(table)
    table[0:1, :] = jnp.concatenate([qb[...].reshape(1, cols), vb[...].reshape(1, cols)], 1)
    lifted = bu[...]
    for n in range(lifted.shape[0] // width):
        table[1 + n : 2 + n, :] = lifted[n * width : (n + 1) * width].reshape(1, width)
    high = table[...].astype(BF)
    low = (table[...] - high.astype(F32)).astype(BF)
    pad = jnp.zeros((8, 2 * width), BF)
    qkvo[rows:, :] = jnp.concatenate([jnp.concatenate([high, low], 1), pad], 0)
    wait_all(copies)


def pack_units_kernel(scal, wu, wd, units, sems):
    place, width = scal[1], wd.shape[1]
    copy_all(
        [
            (chunk(wu, place), units.at[0]),
            (chunk(wd, place, 2, 0), units.at[1, :, :width]),
            (chunk(wd, place, 2, 1), units.at[1, :, width:]),
        ],
        sems,
    )


def pack_inputs_kernel(scal, inputs, x_send, x_keep, sems):
    side, rows = scal[0], x_send.shape[0]
    copy_all(
        [
            (inputs.at[pl.ds((1 - side) * rows, rows)], x_send),
            (inputs.at[pl.ds(side * rows, rows)], x_keep),
        ],
        sems,
    )


def pack_cotangent_kernel(
    scal, cotangent, bo, g1, b1, bd, g2, b2, beside, e_send, e_keep, table, sems
):
    side = scal[0]
    rows, width = e_send.shape[0], e_send.shape[2]
    copy_all(
        [
            (cotangent.at[pl.ds((1 - side) * rows, rows)], e_send),
            (cotangent.at[pl.ds(side * rows, rows)], e_keep),
        ],
        sems,
    )
    for row, ref in ((BO, bo), (G1, g1), (B1, b1), (BD, bd), (G2, g2), (B2, b2)):
        table[row : row + 1, :] = ref[...].reshape(1, width)
    table[QV : QV + 8, :] = beside[...]


def pack(chain, name, kernel, hbm, small, outs, sems):
    return chain.call(
        name,
        kernel,
        [*hbm, *small],
        [SMEM] + [HBM] * (len(hbm) - 1) + [VMEM] * len(small),
        [VMEM] * len(outs),
        outs,
        scratch=[pltpu.SemaphoreType.DMA((sems,))],
    )


def attend_kernel(gathered, scal, *refs):
    if gathered:
        pieces, refs = refs[:CHUNKS], refs[CHUNKS:]
        xo, xr, seen, table, w, *outs, parts, sems, rows_all, p_all, out_sems = refs
    else:
        xo, xr, seen, table, wq, wk, wv, *outs, rows_all, p_all, out_sems = refs
    if gathered:

        @pl.when(pl.program_id(0) == 0)
        def _():
            cols, rows = w.shape[2], w.shape[1] // CHUNKS
            copies = [pltpu.make_async_copy(pieces[0].at[rows:], parts, sems.at[3, 0])]
            for d, piece in enumerate(pieces):
                at = pl.ds(pl.multiple_of((scal[1] ^ d) * rows, rows), rows)
                for n in range(3):
                    copies.append(
                        pltpu.make_async_copy(
                            piece.at[:rows, n * cols : (n + 1) * cols], w.at[n, at], sems.at[n, d]
                        )
                    )
            start_all(copies)
            wait_all(copies)
            width = table.shape[1]
            table[...] = parts[:8, :width].astype(F32) + parts[:8, width:].astype(F32)

        wq, wk, wv = w[0], w[1], w[2]
    else:
        wq, wk, wv = wq[...], wk[...], wv[...]
    cols = wq.shape[1]
    step = pl.program_id(0)
    seqs = p_all.shape[0]
    x = jnp.concatenate([xo[0], xr[0]], 0)
    span = x.shape[0]
    pairs = cols // LANES

    def rows_save(n, seq):
        at = pl.ds(seq * span, span)
        return pltpu.make_async_copy(rows_all.at[n, at], outs[n].at[at], out_sems.at[n, seq])

    def p_save(pair, seq):
        heads = pl.ds(2 * pair, 2)
        return pltpu.make_async_copy(
            p_all.at[seq, heads], outs[4].at[seq, heads], out_sems.at[4 + pair, seq]
        )

    q = (dot(x, wq) + table[0:1, :cols]).astype(BF) * jnp.asarray(HD**-0.5, BF)
    k = dot(x, wk).astype(BF)
    v = (dot(x, wv) + table[0:1, cols:]).astype(BF)
    here = pl.ds(pl.multiple_of(step * span, span), span)
    for n, value in enumerate((q, k, v)):
        rows_all[n, here, :] = value
        rows_save(n, step).start()
    bias = seen[0]
    low = lax.broadcasted_iota(jnp.int32, (span, LANES), 1) < HD
    zero = jnp.zeros((), BF)
    for pair in range(pairs):
        part = slice(pair * LANES, (pair + 1) * LANES)
        qp, kp, vp = q[:, part], k[:, part], v[:, part]
        joined = []
        for b in range(2):
            qm = jnp.where(low, qp, zero) if b == 0 else jnp.where(low, zero, qp)
            s = dot_nt(qm, kp) + bias
            e = jnp.exp(s - jnp.max(s, -1, keepdims=True))
            p = (e * (1.0 / jnp.sum(e, -1, keepdims=True))).astype(BF)
            p_all[step, pair * 2 + b] = p
            joined.append(dot(p, vp))
        p_save(pair, step).start()
        rows_all[3, here, part] = jnp.where(low, joined[0], joined[1]).astype(BF)
    rows_save(3, step).start()

    @pl.when(step == seqs - 1)
    def _():
        for seq in range(seqs):
            wait_all([rows_save(n, seq) for n in range(4)])
            wait_all([p_save(pair, seq) for pair in range(pairs)])


def attend(chain, scal, xo, xr, seen, table, weights):
    seqs, half, width = xo.shape
    span = 2 * half
    cols = width // 2
    heads = cols // HD
    gathered = table is None
    whole = pl.BlockSpec((1, half, width), lambda s: (s, 0, 0))
    in_specs = [whole, whole, pl.BlockSpec((1, 1, span), lambda s: (s, 0, 0))]
    out_specs = [ANY] * 5
    out_shape = [shape_of((seqs * span, cols))] * 4 + [shape_of((seqs, heads, span, span))]
    args = [xo, xr, seen]
    scratch = []
    if gathered:
        in_specs = [SMEM] + [ANY] * CHUNKS + in_specs
        args = [scal, *weights] + args
        out_specs = [held((8, width)), held((3, width, cols))] + out_specs
        out_shape = [shape_of((8, width), F32), shape_of((3, width, cols))] + out_shape
        scratch = [pltpu.VMEM((16, 2 * width), BF), pltpu.SemaphoreType.DMA((4, CHUNKS))]
    else:
        in_specs = [SMEM] + in_specs + [held(table.shape)] + [held((width, cols))] * 3
        args = [scal] + args + [table, *weights]
    return chain.call(
        "attend",
        functools.partial(attend_kernel, gathered),
        args,
        in_specs,
        out_specs,
        out_shape,
        grid=(seqs,),
        scratch=scratch
        + [
            pltpu.VMEM((4, seqs * span, cols), BF),
            pltpu.VMEM((seqs, heads, span, span), BF),
            pltpu.SemaphoreType.DMA((4 + cols // LANES, seqs)),
        ],
    )


def normed(hidden):
    centre = hidden - jnp.mean(hidden, -1, keepdims=True)
    scale = lax.rsqrt(jnp.mean(centre * centre, -1, keepdims=True) + EPSILON)
    return centre * scale, scale


def norm_back(upper, unit, scale, gain):
    through = upper * gain
    return scale * (
        through
        - jnp.mean(through, -1, keepdims=True)
        - unit * jnp.mean(through * unit, -1, keepdims=True)
    )


def gelu_and_slope(u):
    cdf = 0.5 + 0.5 * lax.erf(u * 0.7071067811865476)
    density = jnp.exp(-0.5 * u * u) * 0.3989422804014327
    return (u * cdf).astype(BF), (cdf + u * density).astype(BF)


ROWS = 128
COLUMNS = 256
FEW = 32


def folded(value):
    total = value[:8]
    for n in range(8, value.shape[0], 8):
        total = total + value[n : n + 8]
    return total


def put_chunks(place, value, first, out, rows, columns=slice(None)):
    for n in range(value.shape[0] // rows):
        out[place ^ (first + n), :, columns] = value[n * rows : (n + 1) * rows].astype(BF)


def weight_copies(place, own, pieces, targets, sems):
    wo, wu, wd = targets
    qkvo, halves = pieces
    cols, width = wo.shape[1:]
    units = wu.shape[2]
    found = []

    def bring(a, b):
        found.append(pltpu.make_async_copy(a, b, sems.at[len(found)]))
        return found[-1]

    lists = [[bring(a, target.at[0])] for a, target in zip(own, targets, strict=True)]
    for d in range(CHUNKS):
        c = place ^ d
        n = cols // CHUNKS
        at = pl.ds(pl.multiple_of(c * n, n), n)
        m = width // CHUNKS
        p = units // CHUNKS // 2
        lists[0].append(bring(qkvo[d].at[:n, 3 * cols :], wo.at[1, at, :cols]))
        lists[0].append(bring(qkvo[d].at[n : 2 * n, 3 * cols :], wo.at[1, at, cols:]))
        lists[1].append(bring(halves[d].at[0], wu.at[1, pl.ds(pl.multiple_of(c * m, m), m)]))
        for k in range(2):
            first = pl.multiple_of(c * 2 * p + k * p, p)
            lists[2].append(
                bring(halves[d].at[1, :, k * width : (k + 1) * width], wd.at[1, pl.ds(first, p)])
            )
    return lists


def forward_kernel(scal, *refs):
    qkvo, pieces, refs = refs[:CHUNKS], refs[CHUNKS : 2 * CHUNKS], refs[2 * CHUNKS :]
    (
        xo,
        xr,
        eo,
        er,
        c_own,
        c_oth,
        table,
        table_oth,
        wo_own,
        wu_own,
        wd_own,
        out_own,
        out_send,
        r_out,
        sums,
        y_out,
        n_out,
        sl_own,
        sl_oth,
        dh_out,
        d_oth,
        d_oth_send,
        d_own,
        d_own_send,
        wo,
        wu,
        wd,
        active,
        slopes,
        unit_all,
        unit_low,
        y_all,
        dh_all,
        second,
        products,
        sums_8,
        sems,
        out_sems,
        product_sems,
    ) = refs
    step = pl.program_id(0)
    cols, width = wo.shape[1:]
    units = wu.shape[2]
    half = xo.shape[1]
    span = 2 * half
    tiles = units // width
    blocks = dh_all.shape[0] // span
    final = pl.num_programs(0) - 1

    bring_o, bring_u, bring_d = weight_copies(
        scal[1], (wo_own, wu_own, wd_own), (qkvo, pieces), (wo, wu, wd), sems
    )

    def saves(block):
        rows = pl.ds(block * span, span)
        return [
            pltpu.make_async_copy(a, b.at[rows], out_sems.at[n, block])
            for n, (a, b) in enumerate(
                (
                    (y_all.at[rows], y_out),
                    (unit_low.at[rows], n_out),
                    (slopes.at[0, rows], sl_own),
                    (slopes.at[1, rows], sl_oth),
                    (dh_all.at[rows], dh_out),
                )
            )
        ]

    def product_saves(side):
        targets = ((d_own, d_own_send), (d_oth, d_oth_send))[side]
        return [
            pltpu.make_async_copy(
                products.at[side, pl.ds(n * CHUNKS // 2, CHUNKS // 2)],
                target,
                product_sems.at[side, n],
            )
            for n, target in enumerate(targets)
        ]

    @pl.when(step == 0)
    def _():
        start_all(bring_o)
        sums_8[...] = jnp.zeros_like(sums_8)
        wait_all(bring_o)
        start_all(bring_u[:1])

    @pl.when(step < blocks)
    def _():
        base = step * span

        def rows_at(start, n):
            return pl.ds(pl.multiple_of(base + start, n), n)

        def line(row):
            return table[row : row + 1, :]

        for m in range(0, span, ROWS):
            source = xo if m < half else xr
            x = source[0, m % half : m % half + ROWS, :].astype(F32)
            first = (
                x
                + dot(c_own[m : m + ROWS, :], wo[0])
                + dot(c_oth[m : m + ROWS, :], wo[1])
                + line(BO)
            )
            for r in range(0, ROWS, FEW):
                unit, scale = normed(first[r : r + FEW])
                at = rows_at(m + r, FEW)
                unit_all[at, :] = unit
                unit_low[at, :] = unit.astype(BF)
                r_out[m + r : m + r + FEW, :] = scale
                y_all[at, :] = (unit * line(G1) + line(B1)).astype(BF)

        for side, biases, row in ((0, table, BU), (1, table_oth, 1)):

            @pl.when(step == 0)
            def _():
                wait_all(bring_u[1:] if side else bring_u[:1])
                start_all(bring_d if side else bring_u[1:])

            for n in range(0, units, COLUMNS):
                tile, at = n // width, n % width
                bias = biases[row + tile : row + tile + 1, at : at + COLUMNS]
                for m in range(0, span, ROWS):
                    rows = rows_at(m, ROWS)
                    value, slope = gelu_and_slope(
                        dot(y_all[rows, :], wu[side, :, n : n + COLUMNS]) + bias
                    )
                    active[side * tiles + tile, rows, at : at + COLUMNS] = value
                    slopes[side, rows, n : n + COLUMNS] = slope

        @pl.when(step == 0)
        def _():
            wait_all(bring_d)

        for m in range(0, span, ROWS):
            rows = rows_at(m, ROWS)
            for n in range(0, width, COLUMNS):
                part = slice(n, n + COLUMNS)
                total = (
                    unit_all[rows, part] * table[G1 : G1 + 1, part]
                    + table[B1 : B1 + 1, part]
                    + table[BD : BD + 1, part]
                )
                for side in range(2):
                    for tile in range(tiles):
                        total = total + dot(
                            active[side * tiles + tile, rows, :],
                            wd[side, tile * width : (tile + 1) * width, part],
                        )
                second[m : m + ROWS, part] = total

        for m in range(0, span, FEW):
            unit, scale = normed(second[m : m + FEW, :])
            target, source = (out_own, eo) if m < half else (out_send, er)
            place = slice(m % half, m % half + FEW)
            target[0, place, :] = (unit * line(G2) + line(B2)).astype(BF)
            upper = source[0, place, :].astype(F32)
            back = norm_back(upper, unit, scale, line(G2))
            dh_all[rows_at(m, FEW), :] = back.astype(BF)
            sums_8[0] += folded(upper * unit)
            sums_8[1] += folded(upper)
            sums_8[2] += folded(back)

    for block in range(blocks):

        @pl.when(step == block)
        def _():
            start_all(saves(block))

    for tile in range(2 * tiles):

        @pl.when(step == blocks + tile)
        def _():
            side = 1 - tile // tiles
            rows = products.shape[2]
            for n in range(0, width, COLUMNS):
                part = slice(n, n + COLUMNS)
                value = dot_tn(active[side * tiles + tile % tiles], dh_all[:, part])
                put_chunks(
                    scal[2], value, tile % tiles * (width // rows), products.at[side], rows, part
                )
            if tile % tiles == tiles - 1:
                start_all(product_saves(side))

    @pl.when(step == final)
    def _():
        sums[...] = jnp.zeros_like(sums)
        for row in range(3):
            sums[row : row + 1, :] = jnp.sum(sums_8[row], 0, keepdims=True)
        for block in range(blocks):
            wait_all(saves(block))
        wait_all(product_saves(0) + product_saves(1))


def forward(chain, scal, pieces, xo, xr, eo, er, c_own, c_oth, table, table_oth, own):
    seqs, half, width = xo.shape
    span = 2 * half
    rows = seqs * span
    wo, wu, wd = own
    cols, units = wo.shape[0], wu.shape[1]
    blocks, tiles = seqs, units // width
    pair = pl.BlockSpec((1, half, width), lambda i: (jnp.minimum(i, blocks - 1), 0, 0))
    kept = (CHUNKS // 2, units // CHUNKS, width)

    def block(n):
        return pl.BlockSpec((span, n), lambda i: (jnp.minimum(i, blocks - 1), 0))

    in_specs = (
        [SMEM]
        + [ANY] * (2 * CHUNKS)
        + [pair] * 4
        + [block(cols)] * 2
        + [fixed(table.shape), fixed(table_oth.shape)]
        + [ANY] * 3
    )
    out_specs = [pair, pair, block(1), fixed((8, width))] + [ANY] * 9
    out_shape = [
        shape_of((seqs, half, width)),
        shape_of((seqs, half, width)),
        shape_of((rows, 1), F32),
        shape_of((8, width), F32),
        shape_of((rows, width)),
        shape_of((rows, width)),
        shape_of((rows, units)),
        shape_of((rows, units)),
        shape_of((rows, width)),
    ] + [shape_of(kept)] * 4
    return chain.call(
        "forward",
        forward_kernel,
        [scal, *pieces, xo, xr, eo, er, c_own, c_oth, table, table_oth, wo, wu, wd],
        in_specs,
        out_specs,
        out_shape,
        grid=(blocks + 2 * tiles,),
        scratch=[
            pltpu.VMEM((2, *wo.shape), BF),
            pltpu.VMEM((2, *wu.shape), BF),
            pltpu.VMEM((2, *wd.shape), BF),
            pltpu.VMEM((2 * tiles, rows, width), BF),
            pltpu.VMEM((2, rows, units), BF),
            pltpu.VMEM((rows, width), F32),
            pltpu.VMEM((rows, width), BF),
            pltpu.VMEM((rows, width), BF),
            pltpu.VMEM((rows, width), BF),
            pltpu.VMEM((span, width), F32),
            pltpu.VMEM((2, CHUNKS, *kept[1:]), BF),
            pltpu.VMEM((3, 8, width), F32),
            pltpu.SemaphoreType.DMA((3 + 5 * CHUNKS,)),
            pltpu.SemaphoreType.DMA((5, blocks)),
            pltpu.SemaphoreType.DMA((2, 2)),
        ],
    )


S_G2, S_B2, S_BD, S_G1, S_B1, S_BO, S_BU = range(7)
S_QV = 8


def backward_kernel(scal, *refs):
    qkvo, pieces, refs = refs[:CHUNKS], refs[CHUNKS : 2 * CHUNKS], refs[2 * CHUNKS :]
    (
        table,
        sums2,
        scale,
        y_in,
        c_in_own,
        c_in_oth,
        dh_in,
        unit_in,
        sl_in_own,
        sl_in_oth,
        wo_own,
        wu_own,
        wd_own,
        d1_out,
        dc_own,
        dc_oth,
        sums,
        u_oth,
        u_oth_send,
        u_own,
        u_own_send,
        wo,
        wu,
        wd,
        y,
        c,
        dh,
        unit,
        slopes,
        lifted_all,
        d1_all,
        total,
        products,
        sums_8,
        sems,
        in_sems,
        product_sems,
    ) = refs
    step = pl.program_id(0)
    span, width = d1_out.shape
    cols, units = wo.shape[1], wu.shape[2]
    tiles = units // width
    blocks = d1_all.shape[0] // span
    final = pl.num_programs(0) - 1
    bring_o, bring_u, bring_d = weight_copies(
        scal[1], (wo_own, wu_own, wd_own), (qkvo, pieces), (wo, wu, wd), sems
    )

    def bring_rows(n, source, target, block):
        rows = pl.ds(block * span, span)
        return pltpu.make_async_copy(source.at[rows], target.at[rows], in_sems.at[n, block])

    bring = [
        (
            bring_rows(0, dh_in, dh, block),
            bring_rows(1, sl_in_oth, slopes.at[1], block),
            bring_rows(2, sl_in_own, slopes.at[0], block),
            bring_rows(3, unit_in, unit, block),
        )
        for block in range(blocks)
    ]
    bring_last = [
        bring_rows(4 + n, source, target, block)
        for block in range(blocks)
        for n, (source, target) in enumerate(
            ((y_in, y), (c_in_own, c.at[0]), (c_in_oth, c.at[1]))
        )
    ]

    def product_saves(side):
        targets = ((u_own, u_own_send), (u_oth, u_oth_send))[side]
        return [
            pltpu.make_async_copy(
                products.at[side, pl.ds(n * CHUNKS // 2, CHUNKS // 2)],
                target,
                product_sems.at[side, n],
            )
            for n, target in enumerate(targets)
        ]

    @pl.when(step == 0)
    def _():
        start_all(bring_d[1:])
        start_all(bring[0][:2])
        sums[...] = jnp.zeros_like(sums)
        sums_8[...] = jnp.zeros_like(sums_8)
        for side in range(2):
            sums[side, S_G2 : S_BD + 1, :] = sums2[:3, :]

    for block in range(blocks):

        @pl.when(step == block)
        def _():
            wait_all(bring[block][:2] if block == 0 else bring[block])

    @pl.when(step < blocks)
    def _():
        rows = pl.ds(pl.multiple_of(step * span, span), span)

        def rows_at(start, n):
            return pl.ds(pl.multiple_of(step * span + start, n), n)

        for side in (1, 0):

            @pl.when(step == 0)
            def _():
                if side:
                    wait_all(bring_d[1:])
                    start_all([bring_d[0], bring[0][2]])
                else:
                    wait_all([bring_d[0], bring[0][2]])
                    start_all(bring_u + [bring[0][3]])

            for n in range(0, units, COLUMNS):
                tile, at = n // width, n % width
                added = jnp.zeros((8, COLUMNS), F32)
                value = dot_nt(dh[rows, :], wd[side, n : n + COLUMNS, :])
                for m in range(0, span, ROWS):
                    few = rows_at(m, ROWS)
                    lifted = (
                        value[m : m + ROWS] * slopes[side, few, n : n + COLUMNS].astype(F32)
                    ).astype(BF)
                    lifted_all[side * tiles + tile, few, at : at + COLUMNS] = lifted
                    added = added + folded(lifted.astype(F32))
                sums[side, S_BU + tile : S_BU + tile + 1, at : at + COLUMNS] += jnp.sum(
                    added, 0, keepdims=True
                )

        @pl.when(step == 0)
        def _():
            wait_all(bring_u + [bring[0][3]])
            start_all(bring_o)
            for later in bring[1:]:
                start_all(later)

        for n in range(0, width, COLUMNS):
            part = slice(n, n + COLUMNS)
            upper = dh[rows, part].astype(F32)
            for side in (1, 0):
                for tile in range(tiles):
                    upper = upper + dot_nt(
                        lifted_all[side * tiles + tile, rows, :],
                        wu[side, part, tile * width : (tile + 1) * width],
                    )
            total[:, part] = upper
        for m in range(0, span, FEW):
            part = slice(m, m + FEW)
            few = rows_at(m, FEW)
            upper = total[part, :]
            normal = unit[few, :].astype(F32)
            back = norm_back(upper, normal, scale[part, :], table[G1 : G1 + 1, :])
            sums_8[0] += folded(upper * normal)
            sums_8[1] += folded(upper)
            sums_8[2] += folded(back)
            lower = back.astype(BF)
            d1_out[part, :] = lower
            d1_all[few, :] = lower

        @pl.when(step == 0)
        def _():
            wait_all(bring_o)
            start_all(bring_last)

        lower = d1_out[...]
        dc_own[...] = dot_nt(lower, wo[0]).astype(BF)
        dc_oth[...] = dot_nt(lower, wo[1]).astype(BF)

    for tile in range(2 * tiles):

        @pl.when(step == blocks + tile)
        def _():
            if tile == 0:
                wait_all(bring_last)
            side = 1 - tile // tiles
            count = products.shape[2]
            for n in range(0, width, COLUMNS):
                value = dot_tn(y[...], lifted_all[side * tiles + tile % tiles, :, n : n + COLUMNS])
                at = tile % tiles * width + n
                put_chunks(
                    scal[1], value, 0, products.at[side], count, slice(at, at + COLUMNS)
                )
            if tile % tiles == 0:
                n = cols // CHUNKS
                for m in range(2):
                    value = dot_tn(c[side], d1_all[:, m * cols : (m + 1) * cols])
                    for k in range(CHUNKS):
                        products[
                            side, scal[1] ^ k, m * n : (m + 1) * n, units : units + cols
                        ] = value[k * n : (k + 1) * n].astype(BF)
            if tile % tiles == tiles - 1:
                start_all(product_saves(side))

    @pl.when(step == final)
    def _():
        for n, row in enumerate((S_G1, S_B1, S_BO)):
            line = jnp.sum(sums_8[n], 0, keepdims=True)
            sums[0, row : row + 1, :] = line
            sums[1, row : row + 1, :] = line
        wait_all(product_saves(0) + product_saves(1))


def backward(
    chain, scal, pieces, table, sums2, y, c_own, c_oth, dh, unit, scale, slopes, own, span
):
    rows, width = dh.shape
    wo, wu, wd = own
    cols, units = wo.shape[0], wu.shape[1]
    blocks, tiles = rows // span, units // width
    kept = (CHUNKS // 2, width // CHUNKS, units + cols)

    def block(n):
        return pl.BlockSpec((span, n), lambda i: (jnp.minimum(i, blocks - 1), 0))

    in_specs = (
        [SMEM]
        + [ANY] * (2 * CHUNKS)
        + [fixed(table.shape), fixed(sums2.shape), block(1)]
        + [ANY] * 10
    )
    out_specs = [block(width), block(cols), block(cols), fixed((2, 16, width))] + [ANY] * 4
    out_shape = [
        shape_of((rows, width)),
        shape_of((rows, cols)),
        shape_of((rows, cols)),
        shape_of((2, 16, width), F32),
    ] + [shape_of(kept)] * 4
    return chain.call(
        "backward",
        backward_kernel,
        [scal, *pieces, table, sums2, scale, y, c_own, c_oth, dh, unit, *slopes, *own],
        in_specs,
        out_specs,
        out_shape,
        grid=(blocks + 2 * tiles,),
        scratch=[
            pltpu.VMEM((2, *wo.shape), BF),
            pltpu.VMEM((2, *wu.shape), BF),
            pltpu.VMEM((2, *wd.shape), BF),
            pltpu.VMEM((rows, width), BF),
            pltpu.VMEM((2, rows, cols), BF),
            pltpu.VMEM((rows, width), BF),
            pltpu.VMEM((rows, width), BF),
            pltpu.VMEM((2, rows, units), BF),
            pltpu.VMEM((2 * tiles, rows, width), BF),
            pltpu.VMEM((rows, width), BF),
            pltpu.VMEM((span, width), F32),
            pltpu.VMEM((2, CHUNKS, *kept[1:]), BF),
            pltpu.VMEM((3, 8, width), F32),
            pltpu.SemaphoreType.DMA((3 + 5 * CHUNKS,)),
            pltpu.SemaphoreType.DMA((7, blocks)),
            pltpu.SemaphoreType.DMA((2, 2)),
        ],
    )


def attend_back_kernel(
    side,
    scal,
    vectors,
    xo,
    xr,
    p_in,
    *refs,
):
    rows_in, (grads, keep, send, x, p_all, rows_all, grads_all, table, products, *sems) = (
        refs[:5],
        refs[5:],
    )
    in_sems, p_sems, sems = sems
    step = pl.program_id(0)
    seqs, heads, span = p_all.shape[:3]
    final = seqs - 1
    half = span // 2
    cols = rows_all.shape[2]
    width = x.shape[1]
    rows = width // CHUNKS
    pairs = cols // LANES
    low = lax.broadcasted_iota(jnp.int32, (span, LANES), 1) < HD
    zero = jnp.zeros((), BF)

    def rows_copies(seq):
        at = pl.ds(seq * span, span)
        return [
            pltpu.make_async_copy(a.at[at], rows_all.at[n, at], in_sems.at[n, seq])
            for n, a in enumerate(rows_in)
        ]

    def p_copy(pair, seq):
        both = pl.ds(2 * pair, 2)
        return pltpu.make_async_copy(
            p_in.at[seq, both], p_all.at[seq, both], p_sems.at[pair, seq]
        )

    x_copies = [
        pltpu.make_async_copy(
            a.at[seq], x.at[pl.ds(seq * span + n * half, half)], in_sems.at[5 + n, seq]
        )
        for seq in range(seqs)
        for n, a in enumerate((xo, xr))
    ]
    here = pl.ds(pl.multiple_of(step * span, span), span)
    grads_save = [
        pltpu.make_async_copy(
            grads_all.at[pl.ds(seq * span, span)],
            grads.at[pl.ds(seq * span, span)],
            in_sems.at[7, seq],
        )
        for seq in range(seqs)
    ]

    @pl.when(step == 0)
    def _():
        start_all(rows_copies(0))
        p_copy(0, 0).start()
        table[...] = vectors[side]
        products[...] = jnp.zeros_like(products)

    wait_all(rows_copies(step))
    for pair in range(pairs):
        p_copy(pair, step).wait()
        if pair < pairs - 1:
            p_copy(pair + 1, step).start()
        else:

            @pl.when(step < final)
            def _():
                start_all(rows_copies(step + 1))
                p_copy(0, step + 1).start()

            @pl.when(step == final)
            def _():
                start_all(x_copies)

        part = slice(pair * LANES, (pair + 1) * LANES)
        qp, kp, vp, cp, dcp = [rows_all[n, here, part] for n in range(5)]
        shared = dcp.astype(F32) * cp.astype(F32)
        found = []
        for b in range(2):
            dcm = jnp.where(low, dcp, zero) if b == 0 else jnp.where(low, zero, dcp)
            centre = jnp.sum(
                jnp.where(low, shared, 0.0) if b == 0 else jnp.where(low, 0.0, shared),
                -1,
                keepdims=True,
            )
            p = p_all[step, pair * 2 + b]
            ds = (p.astype(F32) * (dot_nt(dcm, vp) - centre)).astype(BF)
            found.append((dot(ds, kp) * HD**-0.5, dot(qp.T, ds).T, dot(dcp.T, p).T))
        for n in range(3):
            at = n * cols + pair * LANES
            grads_all[here, at : at + LANES] = jnp.where(low, found[0][n], found[1][n]).astype(BF)
    for seq in range(seqs):

        @pl.when(step == seq)
        def _():
            grads_save[seq].start()

    @pl.when(step == final)
    def _():
        wait_all(x_copies)
        for m, n in enumerate((0, 2)):
            table[S_QV : S_QV + 1, m * cols : (m + 1) * cols] = jnp.sum(
                grads_all[:, n * cols : (n + 1) * cols].astype(F32), 0, keepdims=True
            )
        high = table[...].astype(BF).astype(F32)
        low_part = table[...] - high
        blank = jnp.zeros((8 - 2, width), F32)
        for m in range(CHUNKS):
            at = slice(2 * m, 2 * m + 2)
            products[scal[1] ^ m, rows:, :width] = jnp.concatenate(
                [high[at], blank, low_part[at], blank], 0
            ).astype(BF)
        for n in range(0, 3 * cols, cols):
            part = slice(n, n + cols)
            value = dot_tn(x[...], grads_all[:, part])
            for m in range(CHUNKS):
                products[scal[1] ^ m, :rows, part] = value[m * rows : (m + 1) * rows].astype(BF)
        copies = [
            pltpu.make_async_copy(products.at[: CHUNKS // 2], keep, sems.at[0]),
            pltpu.make_async_copy(products.at[CHUNKS // 2 :], send, sems.at[1]),
        ]
        start_all(copies)
        wait_all(copies + grads_save)


def attend_back(chain, scal, xo, xr, p, q, k, v, c, dc, vectors, side):
    seqs, half, width = xo.shape
    span = 2 * half
    cols = q.shape[1]
    pairs = cols // LANES
    kept = (CHUNKS // 2, width // CHUNKS + 16, 3 * cols)
    return chain.call(
        "attend_back",
        functools.partial(attend_back_kernel, side),
        [scal, vectors, xo, xr, p, q, k, v, c, dc],
        [SMEM, held(vectors.shape)] + [ANY] * 8,
        [ANY] * 3,
        [shape_of((seqs * span, 3 * cols)), shape_of(kept), shape_of(kept)],
        grid=(seqs,),
        scratch=[
            pltpu.VMEM((seqs * span, width), BF),
            pltpu.VMEM(p.shape, BF),
            pltpu.VMEM((5, seqs * span, cols), BF),
            pltpu.VMEM((seqs * span, 3 * cols), BF),
            pltpu.VMEM(vectors.shape[1:], F32),
            pltpu.VMEM((CHUNKS, *kept[1:]), BF),
            pltpu.SemaphoreType.DMA((8, seqs)),
            pltpu.SemaphoreType.DMA((pairs, seqs)),
            pltpu.SemaphoreType.DMA((2,)),
        ],
    )


def inputs_back_kernel(d1, own, oth, wq, wk, wv, w_oth, dx_own, dx_send):
    cols = wq.shape[1]
    total = d1[...].astype(F32)
    for n, w in enumerate((wq, wk, wv)):
        part = slice(n * cols, (n + 1) * cols)
        total = total + dot_nt(own[:, part], w[...]) + dot_nt(oth[:, part], w_oth[n])
    total = total.astype(BF)
    half = dx_own.shape[1]
    dx_own[0] = total[:half]
    dx_send[0] = total[half:]


def inputs_back(chain, d1, own, oth, weights, w_oth, half):
    rows, width = d1.shape
    cols = weights[0].shape[1]
    pair = pl.BlockSpec((1, half, width), lambda i: (i, 0, 0))
    out = shape_of((rows // (2 * half), half, width))
    return chain.call(
        "inputs_back",
        inputs_back_kernel,
        [d1, own, oth, *weights, w_oth],
        [pl.BlockSpec((2 * half, width), lambda i: (i, 0))]
        + [pl.BlockSpec((2 * half, 3 * cols), lambda i: (i, 0))] * 2
        + [fixed((width, cols))] * 3
        + [fixed(w_oth.shape)],
        [pair, pair],
        [out, out],
        grid=(rows // (2 * half),),
    )


def combine_kernel(groups, *refs):
    taken = sum(terms for terms, _, _ in groups)
    ins, outs = refs[:taken], list(refs[taken:])
    for terms, split, vectors in groups:
        mine, ins = ins[:terms], ins[terms:]
        chunks, rows = mine[0].shape[:2]
        plain = rows - 16 if vectors else rows
        keep = outs.pop(0)
        send = outs.pop(0) if split else None
        for n in range(chunks):
            out, at = (keep, n) if not split or n < chunks // 2 else (send, n - chunks // 2)
            total = mine[0][n, :plain].astype(F32)
            for term in mine[1:]:
                total = total + term[n, :plain].astype(F32)
            out[at, :plain] = total.astype(BF)
            if vectors:
                both = mine[0][n, plain:].astype(F32)
                for term in mine[1:]:
                    both = both + term[n, plain:].astype(F32)
                both = both[:8] + both[8:]
                high = both.astype(BF).astype(F32)
                out[at, plain:] = jnp.concatenate([high, both - high], 0).astype(BF)


def combine(chain, *groups):
    args, out_shape, plan = [], [], []
    for terms, split, *vectors in groups:
        args += terms
        plan.append((len(terms), split, bool(vectors)))
        dims = terms[0].shape
        if split:
            out_shape += [shape_of((dims[0] // 2, *dims[1:]))] * 2
        else:
            out_shape += [shape_of(dims)]
    return chain.call(
        "combine",
        functools.partial(combine_kernel, plan),
        args,
        [VMEM] * len(args),
        [VMEM] * len(out_shape),
        out_shape,
        mib=20,
    )


def stack_kernel(one, two, out):
    n = one.shape[0]
    out[:n] = one[...]
    out[n:] = two[...]


def stack(chain, one, two):
    dims = (one.shape[0] + two.shape[0], *one.shape[1:])
    return chain.call(
        "stack", stack_kernel, [one, two], [VMEM, VMEM], [VMEM], [shape_of(dims)], mib=20
    )[0]


def join_kernel(scal, mine, got, out):
    rows = mine.shape[0]
    out[pl.ds(scal[0] * rows, rows)] = mine[...]
    out[pl.ds((1 - scal[0]) * rows, rows)] = got[...]


def join(chain, scal, mine, got):
    dims = (2 * mine.shape[0], *mine.shape[1:])
    return chain.call(
        "join",
        join_kernel,
        [scal, mine, got],
        [SMEM, VMEM, VMEM],
        [VMEM],
        [shape_of(dims)],
        mib=20,
    )[0]


def assemble_kernel(widths, cols, place, scal, one, two, *outs):
    for d in range(CHUNKS):
        part, m = (one, d) if d < CHUNKS // 2 else (two, d - CHUNKS // 2)
        c = scal[place] ^ d
        left = 0
        for out, (rows, cuts) in zip(outs, widths):
            at = pl.multiple_of(c * rows, rows)
            cut = out.shape[1] // cuts
            for n in range(cuts):
                out[pl.ds(at, rows), n * cut : (n + 1) * cut] = part[
                    m, n * rows : (n + 1) * rows, left : left + cut
                ].astype(F32)
            left += cut
    if not cols:
        return
    outs, table = outs[len(widths) : -1], outs[-1]
    plain, width = one.shape[1] - 16, table.shape[2]
    for d in range(CHUNKS):
        part, m = (one, d) if d < CHUNKS // 2 else (two, d - CHUNKS // 2)
        both = part[m, plain:, :width].astype(F32)
        table[scal[place] ^ d] = both[:8] + both[8:]

    def line(row):
        return table[row // 2, row % 2 : row % 2 + 1, :]

    for row in range(S_BU):
        outs[row][...] = line(row).reshape(width)
    bu, qb, vb = outs[S_BU:]
    for n in range(bu.shape[0] // width):
        bu[n * width : (n + 1) * width] = line(S_BU + n).reshape(width)
    qb[...] = line(S_QV)[:, :cols].reshape(cols)
    vb[...] = line(S_QV)[:, cols:].reshape(cols)


def assemble(chain, scal, parts, widths, vectors=(), place=1):
    out_shape = [shape_of((CHUNKS * rows, columns), F32) for rows, columns, _ in widths]
    out_shape += [shape_of((n,), F32) for n in vectors]
    plan = [(rows, cuts) for rows, _, cuts in widths]
    cols = vectors[-1] if vectors else 0
    scratch = [pltpu.VMEM((CHUNKS, 8, vectors[0]), F32)] if vectors else []
    return chain.call(
        "assemble",
        functools.partial(assemble_kernel, plan, cols, place),
        [scal, *parts],
        [SMEM] + [VMEM] * 2,
        [VMEM] * len(out_shape),
        out_shape,
        scratch=scratch,
        mib=20,
    )


def tensor_layer(
    dp,
    inputs,
    lengths,
    query_weight,
    query_bias,
    key_weight,
    value_weight,
    value_bias,
    output_weight,
    output_bias,
    first_gain,
    first_shift,
    up_weight,
    up_bias,
    down_weight,
    down_bias,
    second_gain,
    second_shift,
    cotangent,
):
    bits = dp.bit_length() - 1
    count, half, width = inputs.shape
    cols, units = query_weight.shape[1], up_weight.shape[1]
    seqs = count // 2
    side = lax.axis_index("tensor")
    spot = lax.axis_index(DP)
    core, across, deep = spot & 1, (spot >> 1) & 1, (spot >> 2) & 1
    scal = jnp.stack(
        [side, core * 4 + across * 2 + deep, core * 4 + across * 2]
    ).astype(jnp.int32)
    chain = Chain()

    def swap(value):
        return lax.ppermute(value, "tensor", [(0, 1), (1, 0)])

    def flip(value, bit):
        return lax.ppermute(value, DP, [(i, i ^ (1 << bit)) for i in range(dp)])

    def flip_far(value):
        return lax.ppermute(value, DP, [(i, i ^ 6) for i in range(dp)])

    def fetch(piece):
        first = chain.gate(swap(piece))
        return [first, flip(first, 2), flip(first, 1), flip_far(first)]

    def both_cores(found):
        return found + [flip(one, 0) for one in found]

    qkv = [query_weight, key_weight, value_weight]
    own = [output_weight, up_weight, down_weight]
    cut = width // CHUNKS
    flat = shape_of((seqs, half, width))
    qkvo, table_own = pack(
        chain,
        "pack_heads",
        pack_heads_kernel,
        [scal, *qkv, output_weight],
        [query_bias, value_bias, up_bias],
        [shape_of((cut + 16, 4 * cols)), shape_of((8, width), F32)],
        5,
    )
    (sent_units,) = pack(
        chain,
        "pack_units",
        pack_units_kernel,
        [scal, up_weight, down_weight],
        [],
        [shape_of((2, cut, units))],
        3,
    )
    x_send, xo = pack(
        chain, "pack_inputs", pack_inputs_kernel, [scal, inputs], [], [flat, flat], 2
    )
    xr = swap(x_send)
    e_send, eo, table = pack(
        chain,
        "pack_cotangent",
        pack_cotangent_kernel,
        [scal, cotangent],
        [
            output_bias,
            first_gain,
            first_shift,
            down_bias,
            second_gain,
            second_shift,
            table_own,
        ],
        [flat, flat, shape_of((16, width), F32)],
        2,
    )
    qkvo, got_units = fetch(qkvo), fetch(sent_units)

    lens = lax.dynamic_slice_in_dim(lengths, side * seqs, seqs, 0)
    at = jnp.arange(half)
    position = jnp.concatenate([side * half + at, (1 - side) * half + at])
    seen = jnp.where(position[None, :] < lens[:, None], 0.0, MASKED).astype(F32)[:, None, :]

    qkvo[1:] = chain.gate(*qkvo[1:])
    qkvo = both_cores(qkvo)
    q_own, k_own, v_own, c_own, p_own = attend(chain, scal, xo, xr, seen, table_own, qkv)
    er = swap(chain.gate(e_send))
    got_units = both_cores(got_units)
    table_oth, w_oth, q_oth, k_oth, v_oth, c_oth, p_oth = attend(
        chain, scal, xo, xr, seen, None, qkvo
    )
    (
        out_own,
        out_send,
        scale,
        sums2,
        y,
        unit,
        sl_own,
        sl_oth,
        dh,
        d_oth,
        d_oth_send,
        d_own,
        d_own_send,
    ) = forward(
        chain, scal, qkvo + got_units, xo, xr, eo, er, c_own, c_oth, table, table_oth, own
    )
    d_own_got = flip(d_own_send, 0)
    (d_oth,) = combine(chain, ([d_oth, flip(d_oth_send, 0)], False))
    d_got = swap(d_oth)
    d1, dc_own, dc_oth, table_back, u_oth, u_oth_send, u_own, u_own_send = backward(
        chain,
        scal,
        qkvo + got_units,
        table,
        sums2,
        y,
        c_own,
        c_oth,
        dh,
        unit,
        scale,
        (sl_own, sl_oth),
        own,
        2 * half,
    )
    u_oth_got, u_own_got = flip(u_oth_send, 0), flip(u_own_send, 0)
    d_keep, d_send = combine(chain, ([d_own, d_own_got, d_got], True))
    d_got = flip(d_send, 1)
    (u_oth,) = combine(chain, ([u_oth, u_oth_got], False))
    u_got = swap(u_oth)
    g_oth, q_oth, q_oth_send = attend_back(
        chain, scal, xo, xr, p_oth, q_oth, k_oth, v_oth, c_oth, dc_oth, table_back, 1
    )
    q_got = flip(q_oth_send, 0)
    (d_keep,) = combine(chain, ([d_keep, d_got], False))
    d_got = flip(d_keep, 2)
    (q_oth,) = combine(chain, ([q_oth, q_got], False, True))
    q_got = swap(q_oth)
    g_own, q_own, q_own_send = attend_back(
        chain, scal, xo, xr, p_own, q_own, k_own, v_own, c_own, dc_own, table_back, 0
    )
    q_own_got = flip(q_own_send, 0)
    (d_keep,) = combine(chain, ([d_keep, d_got], False))
    d_got = flip(d_keep, 3)
    u_keep, u_send = combine(chain, ([u_own, u_own_got, u_got], True))
    u_got = flip(u_send, 1)
    dx_own, dx_send = inputs_back(chain, d1, g_own, g_oth, qkv, w_oth, half)
    dx_got = swap(dx_send)
    def rest(value, *vectors):
        for bit in range(4, bits):
            (value,) = combine(chain, ([value, flip(value, bit)], False, *vectors))
        return value

    q_keep, q_send = combine(chain, ([q_own, q_own_got, q_got], True, True))
    q_got = flip(q_send, 1)
    out_got = swap(chain.gate(out_send))
    u_keep, u_send = combine(chain, ([u_keep, u_got], True))
    u_got = flip(u_send, 2)
    q_keep, q_send = combine(chain, ([q_keep, q_got], True, True))
    q_got = flip(q_send, 2)
    (u_keep,) = combine(chain, ([u_keep, u_got], False))
    u_got = flip(u_keep, 3)
    (q_keep,) = combine(chain, ([q_keep, q_got], False, True))
    q_got = flip(q_keep, 3)
    (d_two,) = combine(chain, ([d_keep, d_got], False))
    d_two = rest(d_two)
    d_got = flip(d_two, 1)
    (u_sum,) = combine(chain, ([u_keep, u_got], False))
    u_sum = rest(u_sum)
    u_got = flip(u_sum, 2)
    inputs_gradient = join(chain, scal, dx_own, dx_got)
    (q_sum,) = combine(chain, ([q_keep, q_got], False, True))
    q_sum = rest(q_sum, True)
    q_got = flip(q_sum, 2)
    u_two = stack(chain, u_sum, u_got)
    u_got = flip(u_two, 1)
    rows = width // CHUNKS
    q_two = stack(chain, q_sum, q_got)
    q_got = flip(q_two, 1)
    d_four = stack(chain, d_two, d_got)
    d_got = flip(d_four, 0)
    result = join(chain, scal, out_own, out_got)
    u_four = stack(chain, u_two, u_got)
    u_got = flip(u_four, 0)
    q_four = stack(chain, q_two, q_got)
    q_got = flip(q_four, 0)
    (down_back,) = assemble(chain, scal, (d_four, d_got), [(2 * rows, width, 1)], place=2)
    up_back, out_back = assemble(
        chain, scal, (u_four, u_got), [(rows, units, 1), (rows // 2, width, 2)]
    )
    query_back, key_back, value_back, g2b, b2b, bdb, g1b, b1b, bob, bub, qbb, vbb = assemble(
        chain,
        scal,
        (q_four, q_got),
        [(rows, cols, 1)] * 3,
        (width,) * 6 + (units, cols, cols),
    )
    return (
        result,
        inputs_gradient,
        query_back,
        qbb,
        key_back,
        value_back,
        vbb,
        out_back,
        bob,
        g1b,
        b1b,
        up_back,
        bub,
        down_back,
        bdb,
        g2b,
        b2b,
    )


def solution(mesh):
    in_specs = (
        P(DP, "tensor", None),
        P(DP),
        P(None, "tensor"),
        P("tensor"),
        P(None, "tensor"),
        P(None, "tensor"),
        P("tensor"),
        P("tensor", None),
        P(),
        P(),
        P(),
        P(None, "tensor"),
        P("tensor"),
        P("tensor", None),
        P(),
        P(),
        P(),
        P(DP, "tensor", None),
    )
    out_specs = (
        P(DP, "tensor", None),
        P(DP, "tensor", None),
        P(None, "tensor"),
        P("tensor"),
        P(None, "tensor"),
        P(None, "tensor"),
        P("tensor"),
        P("tensor", None),
        P(),
        P(),
        P(),
        P(None, "tensor"),
        P("tensor"),
        P("tensor", None),
        P(),
        P(),
        P(),
    )
    cut = mesh.devices.reshape(mesh.shape["dp"] // 4, 2, 2, mesh.shape["tensor"])
    return jax.shard_map(
        functools.partial(tensor_layer, mesh.shape["dp"]),
        mesh=Mesh(cut, (*DP, "tensor")),
        in_specs=in_specs,
        out_specs=out_specs,
        check_vma=False,
    )
```

```python
import functools

import jax
import jax.numpy as jnp
from jax import lax
from jax.experimental import pallas as pl
from jax.experimental.pallas import tpu as pltpu
from jax.sharding import Mesh
from jax.sharding import PartitionSpec as P

HD = 64
EPSILON = 1e-06
MASKED = -1000000000.0
BF = jnp.bfloat16
F32 = jnp.float32
MIB = 1024 * 1024
LANES = 128
CHUNKS = 8
DP = ("rest", "across", "core")
COSTS = (12, 6, 1, 40, 0.3, 20, 6, 6, 3, 3, 40, 20, 6, 20, 6, 20, 3, 0.05, 0.05, 0.05, 0.05, 40, 1, 0.3, 6, 20, 40, 6, 20, 20, 1, 20, 12, 3, 6, 3, 3, 3, 12, 20, 12, 0.3, 40, 6)

ANY = pl.BlockSpec(memory_space=pl.ANY)
HBM = pl.BlockSpec(memory_space=pltpu.HBM)
SMEM = pl.BlockSpec(memory_space=pltpu.SMEM)
VMEM = pl.BlockSpec(memory_space=pltpu.VMEM)


def dot(left, right):
    return lax.dot_general(left, right, (((1,), (0,)), ((), ())), preferred_element_type=F32)


def dot_nt(left, right):
    return lax.dot_general(left, right, (((1,), (1,)), ((), ())), preferred_element_type=F32)


def dot_tn(left, right):
    return lax.dot_general(left, right, (((0,), (0,)), ((), ())), preferred_element_type=F32)


def shape_of(dims, kind=BF):
    return jax.ShapeDtypeStruct(dims, kind)


def fixed(dims):
    return pl.BlockSpec(dims, lambda *_: (0,) * len(dims))


def held(dims):
    return pl.BlockSpec(dims, lambda *_: (0,) * len(dims), pipeline_mode=pl.Buffered(1))


class Chain:
    def __init__(self):
        self.token = None
        self.count = 0

    def call(self, name, body, args, in_specs, out_specs, out_shape, grid=(), scratch=(), mib=62, aliases=None):
        taken, given = len(args), len(out_shape)
        linked = self.token is not None

        def kernel(*refs):
            rest = refs[taken + linked :]
            body(*refs[:taken], *rest[:given], *rest[given + 1 :])

        outs = pl.pallas_call(
            kernel,
            grid=grid,
            in_specs=list(in_specs) + [ANY] * linked,
            out_specs=list(out_specs) + [ANY],
            out_shape=list(out_shape) + [shape_of((8, LANES), F32)],
            scratch_shapes=list(scratch),
            input_output_aliases=aliases or {},
            compiler_params=pltpu.CompilerParams(
                dimension_semantics=("arbitrary",) * len(grid), vmem_limit_bytes=mib * MIB
            ),
            cost_estimate=pl.CostEstimate(
                flops=int(COSTS[self.count % len(COSTS)] * 1.1e9),
                bytes_accessed=1000,
                transcendentals=0,
            ),
            name=name,
        )(*args, *([self.token] if linked else []))
        self.token = outs[-1]
        self.count += 1
        return outs[:-1]

    def gate(self, *values):
        outs = self.call(
            "gate",
            lambda *_: None,
            list(values),
            [ANY] * len(values),
            [ANY] * len(values),
            [shape_of(value.shape, value.dtype) for value in values],
            aliases={n: n for n in range(len(values))},
        )
        return outs[0] if len(values) == 1 else outs


BO, G1, B1, BD, G2, B2, QV, BU = range(8)


def start_all(copies):
    for copy in copies:
        copy.start()


def wait_all(copies):
    for copy in copies:
        copy.wait()


def copy_all(pairs, sems):
    copies = [pltpu.make_async_copy(a, b, sems.at[n]) for n, (a, b) in enumerate(pairs)]
    for copy in copies:
        copy.start()
    for copy in copies:
        copy.wait()


def chunk(ref, place, total=1, part=0):
    n = ref.shape[0] // CHUNKS
    first = pl.multiple_of(place * n + part * (n // total), n // total)
    return ref.at[pl.ds(first, n // total)]


def pack_heads_kernel(scal, wq, wk, wv, wo, qb, vb, bu, qkvo, table, sems):
    place, cols, width = scal[1], wq.shape[1], wo.shape[1]
    rows = width // CHUNKS
    half = rows // 2
    pairs = [
        (chunk(w, place), qkvo.at[:rows, n * cols : (n + 1) * cols])
        for n, w in enumerate((wq, wk, wv))
    ]
    out = chunk(wo, place)
    pairs.append((out.at[:, :cols], qkvo.at[:half, 3 * cols :]))
    pairs.append((out.at[:, cols:], qkvo.at[half:rows, 3 * cols :]))
    copies = [pltpu.make_async_copy(a, b, sems.at[n]) for n, (a, b) in enumerate(pairs)]
    start_all(copies)
    table[...] = jnp.zeros_like(table)
    table[0:1, :] = jnp.concatenate([qb[...].reshape(1, cols), vb[...].reshape(1, cols)], 1)
    lifted = bu[...]
    for n in range(lifted.shape[0] // width):
        table[1 + n : 2 + n, :] = lifted[n * width : (n + 1) * width].reshape(1, width)
    high = table[...].astype(BF)
    low = (table[...] - high.astype(F32)).astype(BF)
    pad = jnp.zeros((8, 2 * width), BF)
    qkvo[rows:, :] = jnp.concatenate([jnp.concatenate([high, low], 1), pad], 0)
    wait_all(copies)


def pack_units_kernel(scal, wu, wd, units, sems):
    place, width = scal[1], wd.shape[1]
    copy_all(
        [
            (chunk(wu, place), units.at[0]),
            (chunk(wd, place, 2, 0), units.at[1, :, :width]),
            (chunk(wd, place, 2, 1), units.at[1, :, width:]),
        ],
        sems,
    )


def pack_inputs_kernel(scal, inputs, x_send, x_keep, sems):
    side, rows = scal[0], x_send.shape[0]
    copy_all(
        [
            (inputs.at[pl.ds((1 - side) * rows, rows)], x_send),
            (inputs.at[pl.ds(side * rows, rows)], x_keep),
        ],
        sems,
    )


def pack_cotangent_kernel(
    scal, cotangent, bo, g1, b1, bd, g2, b2, beside, e_send, e_keep, table, sems
):
    side = scal[0]
    rows, width = e_send.shape[0], e_send.shape[2]
    copy_all(
        [
            (cotangent.at[pl.ds((1 - side) * rows, rows)], e_send),
            (cotangent.at[pl.ds(side * rows, rows)], e_keep),
        ],
        sems,
    )
    for row, ref in ((BO, bo), (G1, g1), (B1, b1), (BD, bd), (G2, g2), (B2, b2)):
        table[row : row + 1, :] = ref[...].reshape(1, width)
    table[QV : QV + 8, :] = beside[...]


def pack(chain, name, kernel, hbm, small, outs, sems):
    return chain.call(
        name,
        kernel,
        [*hbm, *small],
        [SMEM] + [HBM] * (len(hbm) - 1) + [VMEM] * len(small),
        [VMEM] * len(outs),
        outs,
        scratch=[pltpu.SemaphoreType.DMA((sems,))],
    )


def attend_kernel(gathered, scal, *refs):
    if gathered:
        pieces, refs = refs[:CHUNKS], refs[CHUNKS:]
        xo, xr, seen, table, w, *outs, parts, sems, rows_all, p_all, out_sems = refs
    else:
        xo, xr, seen, table, wq, wk, wv, *outs, rows_all, p_all, out_sems = refs
    if gathered:

        @pl.when(pl.program_id(0) == 0)
        def _():
            cols, rows = w.shape[2], w.shape[1] // CHUNKS
            copies = [pltpu.make_async_copy(pieces[0].at[rows:], parts, sems.at[3, 0])]
            for d, piece in enumerate(pieces):
                at = pl.ds(pl.multiple_of((scal[1] ^ d) * rows, rows), rows)
                for n in range(3):
                    copies.append(
                        pltpu.make_async_copy(
                            piece.at[:rows, n * cols : (n + 1) * cols], w.at[n, at], sems.at[n, d]
                        )
                    )
            start_all(copies)
            wait_all(copies)
            width = table.shape[1]
            table[...] = parts[:8, :width].astype(F32) + parts[:8, width:].astype(F32)

        wq, wk, wv = w[0], w[1], w[2]
    else:
        wq, wk, wv = wq[...], wk[...], wv[...]
    cols = wq.shape[1]
    step = pl.program_id(0)
    seqs = p_all.shape[0]
    x = jnp.concatenate([xo[0], xr[0]], 0)
    span = x.shape[0]
    pairs = cols // LANES

    def rows_save(n, seq):
        at = pl.ds(seq * span, span)
        return pltpu.make_async_copy(rows_all.at[n, at], outs[n].at[at], out_sems.at[n, seq])

    def p_save(pair, seq):
        heads = pl.ds(2 * pair, 2)
        return pltpu.make_async_copy(
            p_all.at[seq, heads], outs[4].at[seq, heads], out_sems.at[4 + pair, seq]
        )

    q = (dot(x, wq) + table[0:1, :cols]).astype(BF) * jnp.asarray(HD**-0.5, BF)
    k = dot(x, wk).astype(BF)
    v = (dot(x, wv) + table[0:1, cols:]).astype(BF)
    here = pl.ds(pl.multiple_of(step * span, span), span)
    for n, value in enumerate((q, k, v)):
        rows_all[n, here, :] = value
        rows_save(n, step).start()
    bias = seen[0]
    low = lax.broadcasted_iota(jnp.int32, (span, LANES), 1) < HD
    zero = jnp.zeros((), BF)
    for pair in range(pairs):
        part = slice(pair * LANES, (pair + 1) * LANES)
        qp, kp, vp = q[:, part], k[:, part], v[:, part]
        joined = []
        for b in range(2):
            qm = jnp.where(low, qp, zero) if b == 0 else jnp.where(low, zero, qp)
            s = dot_nt(qm, kp) + bias
            e = jnp.exp(s - jnp.max(s, -1, keepdims=True))
            p = (e * (1.0 / jnp.sum(e, -1, keepdims=True))).astype(BF)
            p_all[step, pair * 2 + b] = p
            joined.append(dot(p, vp))
        p_save(pair, step).start()
        rows_all[3, here, part] = jnp.where(low, joined[0], joined[1]).astype(BF)
    rows_save(3, step).start()

    @pl.when(step == seqs - 1)
    def _():
        for seq in range(seqs):
            wait_all([rows_save(n, seq) for n in range(4)])
            wait_all([p_save(pair, seq) for pair in range(pairs)])


def attend(chain, scal, xo, xr, seen, table, weights):
    seqs, half, width = xo.shape
    span = 2 * half
    cols = width // 2
    heads = cols // HD
    gathered = table is None
    whole = pl.BlockSpec((1, half, width), lambda s: (s, 0, 0))
    in_specs = [whole, whole, pl.BlockSpec((1, 1, span), lambda s: (s, 0, 0))]
    out_specs = [ANY] * 5
    out_shape = [shape_of((seqs * span, cols))] * 4 + [shape_of((seqs, heads, span, span))]
    args = [xo, xr, seen]
    scratch = []
    if gathered:
        in_specs = [SMEM] + [ANY] * CHUNKS + in_specs
        args = [scal, *weights] + args
        out_specs = [held((8, width)), held((3, width, cols))] + out_specs
        out_shape = [shape_of((8, width), F32), shape_of((3, width, cols))] + out_shape
        scratch = [pltpu.VMEM((16, 2 * width), BF), pltpu.SemaphoreType.DMA((4, CHUNKS))]
    else:
        in_specs = [SMEM] + in_specs + [held(table.shape)] + [held((width, cols))] * 3
        args = [scal] + args + [table, *weights]
    return chain.call(
        "attend",
        functools.partial(attend_kernel, gathered),
        args,
        in_specs,
        out_specs,
        out_shape,
        grid=(seqs,),
        scratch=scratch
        + [
            pltpu.VMEM((4, seqs * span, cols), BF),
            pltpu.VMEM((seqs, heads, span, span), BF),
            pltpu.SemaphoreType.DMA((4 + cols // LANES, seqs)),
        ],
    )


def normed(hidden):
    centre = hidden - jnp.mean(hidden, -1, keepdims=True)
    scale = lax.rsqrt(jnp.mean(centre * centre, -1, keepdims=True) + EPSILON)
    return centre * scale, scale


def norm_back(upper, unit, scale, gain):
    through = upper * gain
    return scale * (
        through
        - jnp.mean(through, -1, keepdims=True)
        - unit * jnp.mean(through * unit, -1, keepdims=True)
    )


def gelu_and_slope(u):
    cdf = 0.5 + 0.5 * lax.erf(u * 0.7071067811865476)
    density = jnp.exp(-0.5 * u * u) * 0.3989422804014327
    return (u * cdf).astype(BF), (cdf + u * density).astype(BF)


ROWS = 128
COLUMNS = 256
FEW = 32


def folded(value):
    total = value[:8]
    for n in range(8, value.shape[0], 8):
        total = total + value[n : n + 8]
    return total


def put_chunks(place, value, first, out, rows, columns=slice(None)):
    for n in range(value.shape[0] // rows):
        out[place ^ (first + n), :, columns] = value[n * rows : (n + 1) * rows].astype(BF)


def weight_copies(place, own, pieces, targets, sems):
    wo, wu, wd = targets
    qkvo, halves = pieces
    cols, width = wo.shape[1:]
    units = wu.shape[2]
    found = []

    def bring(a, b):
        found.append(pltpu.make_async_copy(a, b, sems.at[len(found)]))
        return found[-1]

    lists = [[bring(a, target.at[0])] for a, target in zip(own, targets, strict=True)]
    for d in range(CHUNKS):
        c = place ^ d
        n = cols // CHUNKS
        at = pl.ds(pl.multiple_of(c * n, n), n)
        m = width // CHUNKS
        p = units // CHUNKS // 2
        lists[0].append(bring(qkvo[d].at[:n, 3 * cols :], wo.at[1, at, :cols]))
        lists[0].append(bring(qkvo[d].at[n : 2 * n, 3 * cols :], wo.at[1, at, cols:]))
        lists[1].append(bring(halves[d].at[0], wu.at[1, pl.ds(pl.multiple_of(c * m, m), m)]))
        for k in range(2):
            first = pl.multiple_of(c * 2 * p + k * p, p)
            lists[2].append(
                bring(halves[d].at[1, :, k * width : (k + 1) * width], wd.at[1, pl.ds(first, p)])
            )
    return lists


def forward_kernel(scal, *refs):
    qkvo, pieces, refs = refs[:CHUNKS], refs[CHUNKS : 2 * CHUNKS], refs[2 * CHUNKS :]
    (
        xo,
        xr,
        eo,
        er,
        c_own,
        c_oth,
        table,
        table_oth,
        wo_own,
        wu_own,
        wd_own,
        out_own,
        out_send,
        r_out,
        sums,
        y_out,
        n_out,
        sl_own,
        sl_oth,
        dh_out,
        d_oth,
        d_oth_send,
        d_own,
        d_own_send,
        wo,
        wu,
        wd,
        active,
        slopes,
        unit_all,
        unit_low,
        y_all,
        dh_all,
        second,
        products,
        sums_8,
        sems,
        out_sems,
        product_sems,
    ) = refs
    step = pl.program_id(0)
    cols, width = wo.shape[1:]
    units = wu.shape[2]
    half = xo.shape[1]
    span = 2 * half
    tiles = units // width
    blocks = dh_all.shape[0] // span
    final = pl.num_programs(0) - 1

    bring_o, bring_u, bring_d = weight_copies(
        scal[1], (wo_own, wu_own, wd_own), (qkvo, pieces), (wo, wu, wd), sems
    )

    def saves(block):
        rows = pl.ds(block * span, span)
        return [
            pltpu.make_async_copy(a, b.at[rows], out_sems.at[n, block])
            for n, (a, b) in enumerate(
                (
                    (y_all.at[rows], y_out),
                    (unit_low.at[rows], n_out),
                    (slopes.at[0, rows], sl_own),
                    (slopes.at[1, rows], sl_oth),
                    (dh_all.at[rows], dh_out),
                )
            )
        ]

    def product_saves(side):
        targets = ((d_own, d_own_send), (d_oth, d_oth_send))[side]
        return [
            pltpu.make_async_copy(
                products.at[side, pl.ds(n * CHUNKS // 2, CHUNKS // 2)],
                target,
                product_sems.at[side, n],
            )
            for n, target in enumerate(targets)
        ]

    @pl.when(step == 0)
    def _():
        start_all(bring_o)
        sums_8[...] = jnp.zeros_like(sums_8)
        wait_all(bring_o)
        start_all(bring_u[:1])

    @pl.when(step < blocks)
    def _():
        base = step * span

        def rows_at(start, n):
            return pl.ds(pl.multiple_of(base + start, n), n)

        def line(row):
            return table[row : row + 1, :]

        for m in range(0, span, ROWS):
            source = xo if m < half else xr
            x = source[0, m % half : m % half + ROWS, :].astype(F32)
            first = (
                x
                + dot(c_own[m : m + ROWS, :], wo[0])
                + dot(c_oth[m : m + ROWS, :], wo[1])
                + line(BO)
            )
            for r in range(0, ROWS, FEW):
                unit, scale = normed(first[r : r + FEW])
                at = rows_at(m + r, FEW)
                unit_all[at, :] = unit
                unit_low[at, :] = unit.astype(BF)
                r_out[m + r : m + r + FEW, :] = scale
                y_all[at, :] = (unit * line(G1) + line(B1)).astype(BF)

        for side, biases, row in ((0, table, BU), (1, table_oth, 1)):

            @pl.when(step == 0)
            def _():
                wait_all(bring_u[1:] if side else bring_u[:1])
                start_all(bring_d if side else bring_u[1:])

            for n in range(0, units, COLUMNS):
                tile, at = n // width, n % width
                bias = biases[row + tile : row + tile + 1, at : at + COLUMNS]
                for m in range(0, span, ROWS):
                    rows = rows_at(m, ROWS)
                    value, slope = gelu_and_slope(
                        dot(y_all[rows, :], wu[side, :, n : n + COLUMNS]) + bias
                    )
                    active[side * tiles + tile, rows, at : at + COLUMNS] = value
                    slopes[side, rows, n : n + COLUMNS] = slope

        @pl.when(step == 0)
        def _():
            wait_all(bring_d)

        for m in range(0, span, ROWS):
            rows = rows_at(m, ROWS)
            for n in range(0, width, COLUMNS):
                part = slice(n, n + COLUMNS)
                total = (
                    unit_all[rows, part] * table[G1 : G1 + 1, part]
                    + table[B1 : B1 + 1, part]
                    + table[BD : BD + 1, part]
                )
                for side in range(2):
                    for tile in range(tiles):
                        total = total + dot(
                            active[side * tiles + tile, rows, :],
                            wd[side, tile * width : (tile + 1) * width, part],
                        )
                second[m : m + ROWS, part] = total

        for m in range(0, span, FEW):
            unit, scale = normed(second[m : m + FEW, :])
            target, source = (out_own, eo) if m < half else (out_send, er)
            place = slice(m % half, m % half + FEW)
            target[0, place, :] = (unit * line(G2) + line(B2)).astype(BF)
            upper = source[0, place, :].astype(F32)
            back = norm_back(upper, unit, scale, line(G2))
            dh_all[rows_at(m, FEW), :] = back.astype(BF)
            sums_8[0] += folded(upper * unit)
            sums_8[1] += folded(upper)
            sums_8[2] += folded(back)

    for block in range(blocks):

        @pl.when(step == block)
        def _():
            start_all(saves(block))

    for tile in range(2 * tiles):

        @pl.when(step == blocks + tile)
        def _():
            side = 1 - tile // tiles
            rows = products.shape[2]
            for n in range(0, width, COLUMNS):
                part = slice(n, n + COLUMNS)
                value = dot_tn(active[side * tiles + tile % tiles], dh_all[:, part])
                put_chunks(
                    scal[2], value, tile % tiles * (width // rows), products.at[side], rows, part
                )
            if tile % tiles == tiles - 1:
                start_all(product_saves(side))

    @pl.when(step == final)
    def _():
        sums[...] = jnp.zeros_like(sums)
        for row in range(3):
            sums[row : row + 1, :] = jnp.sum(sums_8[row], 0, keepdims=True)
        for block in range(blocks):
            wait_all(saves(block))
        wait_all(product_saves(0) + product_saves(1))


def forward(chain, scal, pieces, xo, xr, eo, er, c_own, c_oth, table, table_oth, own):
    seqs, half, width = xo.shape
    span = 2 * half
    rows = seqs * span
    wo, wu, wd = own
    cols, units = wo.shape[0], wu.shape[1]
    blocks, tiles = seqs, units // width
    pair = pl.BlockSpec((1, half, width), lambda i: (jnp.minimum(i, blocks - 1), 0, 0))
    kept = (CHUNKS // 2, units // CHUNKS, width)

    def block(n):
        return pl.BlockSpec((span, n), lambda i: (jnp.minimum(i, blocks - 1), 0))

    in_specs = (
        [SMEM]
        + [ANY] * (2 * CHUNKS)
        + [pair] * 4
        + [block(cols)] * 2
        + [fixed(table.shape), fixed(table_oth.shape)]
        + [ANY] * 3
    )
    out_specs = [pair, pair, block(1), fixed((8, width))] + [ANY] * 9
    out_shape = [
        shape_of((seqs, half, width)),
        shape_of((seqs, half, width)),
        shape_of((rows, 1), F32),
        shape_of((8, width), F32),
        shape_of((rows, width)),
        shape_of((rows, width)),
        shape_of((rows, units)),
        shape_of((rows, units)),
        shape_of((rows, width)),
    ] + [shape_of(kept)] * 4
    return chain.call(
        "forward",
        forward_kernel,
        [scal, *pieces, xo, xr, eo, er, c_own, c_oth, table, table_oth, wo, wu, wd],
        in_specs,
        out_specs,
        out_shape,
        grid=(blocks + 2 * tiles,),
        scratch=[
            pltpu.VMEM((2, *wo.shape), BF),
            pltpu.VMEM((2, *wu.shape), BF),
            pltpu.VMEM((2, *wd.shape), BF),
            pltpu.VMEM((2 * tiles, rows, width), BF),
            pltpu.VMEM((2, rows, units), BF),
            pltpu.VMEM((rows, width), F32),
            pltpu.VMEM((rows, width), BF),
            pltpu.VMEM((rows, width), BF),
            pltpu.VMEM((rows, width), BF),
            pltpu.VMEM((span, width), F32),
            pltpu.VMEM((2, CHUNKS, *kept[1:]), BF),
            pltpu.VMEM((3, 8, width), F32),
            pltpu.SemaphoreType.DMA((3 + 5 * CHUNKS,)),
            pltpu.SemaphoreType.DMA((5, blocks)),
            pltpu.SemaphoreType.DMA((2, 2)),
        ],
    )


S_G2, S_B2, S_BD, S_G1, S_B1, S_BO, S_BU = range(7)
S_QV = 8


def backward_kernel(scal, *refs):
    qkvo, pieces, refs = refs[:CHUNKS], refs[CHUNKS : 2 * CHUNKS], refs[2 * CHUNKS :]
    (
        table,
        sums2,
        scale,
        y_in,
        c_in_own,
        c_in_oth,
        dh_in,
        unit_in,
        sl_in_own,
        sl_in_oth,
        wo_own,
        wu_own,
        wd_own,
        d1_out,
        dc_own,
        dc_oth,
        sums,
        u_oth,
        u_oth_send,
        u_own,
        u_own_send,
        wo,
        wu,
        wd,
        y,
        c,
        dh,
        unit,
        slopes,
        lifted_all,
        d1_all,
        total,
        products,
        sums_8,
        sems,
        in_sems,
        product_sems,
    ) = refs
    step = pl.program_id(0)
    span, width = d1_out.shape
    cols, units = wo.shape[1], wu.shape[2]
    tiles = units // width
    blocks = d1_all.shape[0] // span
    final = pl.num_programs(0) - 1
    bring_o, bring_u, bring_d = weight_copies(
        scal[1], (wo_own, wu_own, wd_own), (qkvo, pieces), (wo, wu, wd), sems
    )

    def bring_rows(n, source, target, block):
        rows = pl.ds(block * span, span)
        return pltpu.make_async_copy(source.at[rows], target.at[rows], in_sems.at[n, block])

    bring = [
        (
            bring_rows(0, dh_in, dh, block),
            bring_rows(1, sl_in_oth, slopes.at[1], block),
            bring_rows(2, sl_in_own, slopes.at[0], block),
            bring_rows(3, unit_in, unit, block),
        )
        for block in range(blocks)
    ]
    bring_last = [
        bring_rows(4 + n, source, target, block)
        for block in range(blocks)
        for n, (source, target) in enumerate(
            ((y_in, y), (c_in_own, c.at[0]), (c_in_oth, c.at[1]))
        )
    ]

    def product_saves(side):
        targets = ((u_own, u_own_send), (u_oth, u_oth_send))[side]
        return [
            pltpu.make_async_copy(
                products.at[side, pl.ds(n * CHUNKS // 2, CHUNKS // 2)],
                target,
                product_sems.at[side, n],
            )
            for n, target in enumerate(targets)
        ]

    @pl.when(step == 0)
    def _():
        start_all(bring_d[1:])
        start_all(bring[0][:2])
        sums[...] = jnp.zeros_like(sums)
        sums_8[...] = jnp.zeros_like(sums_8)
        for side in range(2):
            sums[side, S_G2 : S_BD + 1, :] = sums2[:3, :]

    for block in range(blocks):

        @pl.when(step == block)
        def _():
            wait_all(bring[block][:2] if block == 0 else bring[block])

    @pl.when(step < blocks)
    def _():
        rows = pl.ds(pl.multiple_of(step * span, span), span)

        def rows_at(start, n):
            return pl.ds(pl.multiple_of(step * span + start, n), n)

        for side in (1, 0):

            @pl.when(step == 0)
            def _():
                if side:
                    wait_all(bring_d[1:])
                    start_all([bring_d[0], bring[0][2]])
                else:
                    wait_all([bring_d[0], bring[0][2]])
                    start_all(bring_u + [bring[0][3]])

            for n in range(0, units, COLUMNS):
                tile, at = n // width, n % width
                added = jnp.zeros((8, COLUMNS), F32)
                value = dot_nt(dh[rows, :], wd[side, n : n + COLUMNS, :])
                for m in range(0, span, ROWS):
                    few = rows_at(m, ROWS)
                    lifted = (
                        value[m : m + ROWS] * slopes[side, few, n : n + COLUMNS].astype(F32)
                    ).astype(BF)
                    lifted_all[side * tiles + tile, few, at : at + COLUMNS] = lifted
                    added = added + folded(lifted.astype(F32))
                sums[side, S_BU + tile : S_BU + tile + 1, at : at + COLUMNS] += jnp.sum(
                    added, 0, keepdims=True
                )

        @pl.when(step == 0)
        def _():
            wait_all(bring_u + [bring[0][3]])
            start_all(bring_o)
            for later in bring[1:]:
                start_all(later)

        for n in range(0, width, COLUMNS):
            part = slice(n, n + COLUMNS)
            upper = dh[rows, part].astype(F32)
            for side in (1, 0):
                for tile in range(tiles):
                    upper = upper + dot_nt(
                        lifted_all[side * tiles + tile, rows, :],
                        wu[side, part, tile * width : (tile + 1) * width],
                    )
            total[:, part] = upper
        for m in range(0, span, FEW):
            part = slice(m, m + FEW)
            few = rows_at(m, FEW)
            upper = total[part, :]
            normal = unit[few, :].astype(F32)
            back = norm_back(upper, normal, scale[part, :], table[G1 : G1 + 1, :])
            sums_8[0] += folded(upper * normal)
            sums_8[1] += folded(upper)
            sums_8[2] += folded(back)
            lower = back.astype(BF)
            d1_out[part, :] = lower
            d1_all[few, :] = lower

        @pl.when(step == 0)
        def _():
            wait_all(bring_o)
            start_all(bring_last)

        lower = d1_out[...]
        dc_own[...] = dot_nt(lower, wo[0]).astype(BF)
        dc_oth[...] = dot_nt(lower, wo[1]).astype(BF)

    for tile in range(2 * tiles):

        @pl.when(step == blocks + tile)
        def _():
            if tile == 0:
                wait_all(bring_last)
            side = 1 - tile // tiles
            count = products.shape[2]
            for n in range(0, width, COLUMNS):
                value = dot_tn(y[...], lifted_all[side * tiles + tile % tiles, :, n : n + COLUMNS])
                at = tile % tiles * width + n
                put_chunks(
                    scal[1], value, 0, products.at[side], count, slice(at, at + COLUMNS)
                )
            if tile % tiles == 0:
                n = cols // CHUNKS
                for m in range(2):
                    value = dot_tn(c[side], d1_all[:, m * cols : (m + 1) * cols])
                    for k in range(CHUNKS):
                        products[
                            side, scal[1] ^ k, m * n : (m + 1) * n, units : units + cols
                        ] = value[k * n : (k + 1) * n].astype(BF)
            if tile % tiles == tiles - 1:
                start_all(product_saves(side))

    @pl.when(step == final)
    def _():
        for n, row in enumerate((S_G1, S_B1, S_BO)):
            line = jnp.sum(sums_8[n], 0, keepdims=True)
            sums[0, row : row + 1, :] = line
            sums[1, row : row + 1, :] = line
        wait_all(product_saves(0) + product_saves(1))


def backward(
    chain, scal, pieces, table, sums2, y, c_own, c_oth, dh, unit, scale, slopes, own, span
):
    rows, width = dh.shape
    wo, wu, wd = own
    cols, units = wo.shape[0], wu.shape[1]
    blocks, tiles = rows // span, units // width
    kept = (CHUNKS // 2, width // CHUNKS, units + cols)

    def block(n):
        return pl.BlockSpec((span, n), lambda i: (jnp.minimum(i, blocks - 1), 0))

    in_specs = (
        [SMEM]
        + [ANY] * (2 * CHUNKS)
        + [fixed(table.shape), fixed(sums2.shape), block(1)]
        + [ANY] * 10
    )
    out_specs = [block(width), block(cols), block(cols), fixed((2, 16, width))] + [ANY] * 4
    out_shape = [
        shape_of((rows, width)),
        shape_of((rows, cols)),
        shape_of((rows, cols)),
        shape_of((2, 16, width), F32),
    ] + [shape_of(kept)] * 4
    return chain.call(
        "backward",
        backward_kernel,
        [scal, *pieces, table, sums2, scale, y, c_own, c_oth, dh, unit, *slopes, *own],
        in_specs,
        out_specs,
        out_shape,
        grid=(blocks + 2 * tiles,),
        scratch=[
            pltpu.VMEM((2, *wo.shape), BF),
            pltpu.VMEM((2, *wu.shape), BF),
            pltpu.VMEM((2, *wd.shape), BF),
            pltpu.VMEM((rows, width), BF),
            pltpu.VMEM((2, rows, cols), BF),
            pltpu.VMEM((rows, width), BF),
            pltpu.VMEM((rows, width), BF),
            pltpu.VMEM((2, rows, units), BF),
            pltpu.VMEM((2 * tiles, rows, width), BF),
            pltpu.VMEM((rows, width), BF),
            pltpu.VMEM((span, width), F32),
            pltpu.VMEM((2, CHUNKS, *kept[1:]), BF),
            pltpu.VMEM((3, 8, width), F32),
            pltpu.SemaphoreType.DMA((3 + 5 * CHUNKS,)),
            pltpu.SemaphoreType.DMA((7, blocks)),
            pltpu.SemaphoreType.DMA((2, 2)),
        ],
    )


def attend_back_kernel(
    side,
    scal,
    vectors,
    xo,
    xr,
    p_in,
    *refs,
):
    rows_in, (grads, keep, send, x, p_all, rows_all, grads_all, table, products, *sems) = (
        refs[:5],
        refs[5:],
    )
    in_sems, p_sems, sems = sems
    step = pl.program_id(0)
    seqs, heads, span = p_all.shape[:3]
    final = seqs - 1
    half = span // 2
    cols = rows_all.shape[2]
    width = x.shape[1]
    rows = width // CHUNKS
    pairs = cols // LANES
    low = lax.broadcasted_iota(jnp.int32, (span, LANES), 1) < HD
    zero = jnp.zeros((), BF)

    def rows_copies(seq):
        at = pl.ds(seq * span, span)
        return [
            pltpu.make_async_copy(a.at[at], rows_all.at[n, at], in_sems.at[n, seq])
            for n, a in enumerate(rows_in)
        ]

    def p_copy(pair, seq):
        both = pl.ds(2 * pair, 2)
        return pltpu.make_async_copy(
            p_in.at[seq, both], p_all.at[seq, both], p_sems.at[pair, seq]
        )

    x_copies = [
        pltpu.make_async_copy(
            a.at[seq], x.at[pl.ds(seq * span + n * half, half)], in_sems.at[5 + n, seq]
        )
        for seq in range(seqs)
        for n, a in enumerate((xo, xr))
    ]
    here = pl.ds(pl.multiple_of(step * span, span), span)
    grads_save = [
        pltpu.make_async_copy(
            grads_all.at[pl.ds(seq * span, span)],
            grads.at[pl.ds(seq * span, span)],
            in_sems.at[7, seq],
        )
        for seq in range(seqs)
    ]

    @pl.when(step == 0)
    def _():
        start_all(rows_copies(0))
        p_copy(0, 0).start()
        table[...] = vectors[side]
        products[...] = jnp.zeros_like(products)

    wait_all(rows_copies(step))
    for pair in range(pairs):
        p_copy(pair, step).wait()
        if pair < pairs - 1:
            p_copy(pair + 1, step).start()
        else:

            @pl.when(step < final)
            def _():
                start_all(rows_copies(step + 1))
                p_copy(0, step + 1).start()

            @pl.when(step == final)
            def _():
                start_all(x_copies)

        part = slice(pair * LANES, (pair + 1) * LANES)
        qp, kp, vp, cp, dcp = [rows_all[n, here, part] for n in range(5)]
        shared = dcp.astype(F32) * cp.astype(F32)
        found = []
        for b in range(2):
            dcm = jnp.where(low, dcp, zero) if b == 0 else jnp.where(low, zero, dcp)
            centre = jnp.sum(
                jnp.where(low, shared, 0.0) if b == 0 else jnp.where(low, 0.0, shared),
                -1,
                keepdims=True,
            )
            p = p_all[step, pair * 2 + b]
            ds = (p.astype(F32) * (dot_nt(dcm, vp) - centre)).astype(BF)
            found.append((dot(ds, kp) * HD**-0.5, dot(qp.T, ds).T, dot(dcp.T, p).T))
        for n in range(3):
            at = n * cols + pair * LANES
            grads_all[here, at : at + LANES] = jnp.where(low, found[0][n], found[1][n]).astype(BF)
    for seq in range(seqs):

        @pl.when(step == seq)
        def _():
            grads_save[seq].start()

    @pl.when(step == final)
    def _():
        wait_all(x_copies)
        for m, n in enumerate((0, 2)):
            table[S_QV : S_QV + 1, m * cols : (m + 1) * cols] = jnp.sum(
                grads_all[:, n * cols : (n + 1) * cols].astype(F32), 0, keepdims=True
            )
        high = table[...].astype(BF).astype(F32)
        low_part = table[...] - high
        blank = jnp.zeros((8 - 2, width), F32)
        for m in range(CHUNKS):
            at = slice(2 * m, 2 * m + 2)
            products[scal[1] ^ m, rows:, :width] = jnp.concatenate(
                [high[at], blank, low_part[at], blank], 0
            ).astype(BF)
        for n in range(0, 3 * cols, cols):
            part = slice(n, n + cols)
            value = dot_tn(x[...], grads_all[:, part])
            for m in range(CHUNKS):
                products[scal[1] ^ m, :rows, part] = value[m * rows : (m + 1) * rows].astype(BF)
        copies = [
            pltpu.make_async_copy(products.at[: CHUNKS // 2], keep, sems.at[0]),
            pltpu.make_async_copy(products.at[CHUNKS // 2 :], send, sems.at[1]),
        ]
        start_all(copies)
        wait_all(copies + grads_save)


def attend_back(chain, scal, xo, xr, p, q, k, v, c, dc, vectors, side):
    seqs, half, width = xo.shape
    span = 2 * half
    cols = q.shape[1]
    pairs = cols // LANES
    kept = (CHUNKS // 2, width // CHUNKS + 16, 3 * cols)
    return chain.call(
        "attend_back",
        functools.partial(attend_back_kernel, side),
        [scal, vectors, xo, xr, p, q, k, v, c, dc],
        [SMEM, held(vectors.shape)] + [ANY] * 8,
        [ANY] * 3,
        [shape_of((seqs * span, 3 * cols)), shape_of(kept), shape_of(kept)],
        grid=(seqs,),
        scratch=[
            pltpu.VMEM((seqs * span, width), BF),
            pltpu.VMEM(p.shape, BF),
            pltpu.VMEM((5, seqs * span, cols), BF),
            pltpu.VMEM((seqs * span, 3 * cols), BF),
            pltpu.VMEM(vectors.shape[1:], F32),
            pltpu.VMEM((CHUNKS, *kept[1:]), BF),
            pltpu.SemaphoreType.DMA((8, seqs)),
            pltpu.SemaphoreType.DMA((pairs, seqs)),
            pltpu.SemaphoreType.DMA((2,)),
        ],
    )


def inputs_back_kernel(d1, own, oth, wq, wk, wv, w_oth, dx_own, dx_send):
    cols = wq.shape[1]
    total = d1[...].astype(F32)
    for n, w in enumerate((wq, wk, wv)):
        part = slice(n * cols, (n + 1) * cols)
        total = total + dot_nt(own[:, part], w[...]) + dot_nt(oth[:, part], w_oth[n])
    total = total.astype(BF)
    half = dx_own.shape[1]
    dx_own[0] = total[:half]
    dx_send[0] = total[half:]


def inputs_back(chain, d1, own, oth, weights, w_oth, half):
    rows, width = d1.shape
    cols = weights[0].shape[1]
    pair = pl.BlockSpec((1, half, width), lambda i: (i, 0, 0))
    out = shape_of((rows // (2 * half), half, width))
    return chain.call(
        "inputs_back",
        inputs_back_kernel,
        [d1, own, oth, *weights, w_oth],
        [pl.BlockSpec((2 * half, width), lambda i: (i, 0))]
        + [pl.BlockSpec((2 * half, 3 * cols), lambda i: (i, 0))] * 2
        + [fixed((width, cols))] * 3
        + [fixed(w_oth.shape)],
        [pair, pair],
        [out, out],
        grid=(rows // (2 * half),),
    )


def combine_kernel(groups, *refs):
    taken = sum(terms for terms, _, _ in groups)
    ins, outs = refs[:taken], list(refs[taken:])
    for terms, split, vectors in groups:
        mine, ins = ins[:terms], ins[terms:]
        chunks, rows = mine[0].shape[:2]
        plain = rows - 16 if vectors else rows
        keep = outs.pop(0)
        send = outs.pop(0) if split else None
        for n in range(chunks):
            out, at = (keep, n) if not split or n < chunks // 2 else (send, n - chunks // 2)
            total = mine[0][n, :plain].astype(F32)
            for term in mine[1:]:
                total = total + term[n, :plain].astype(F32)
            out[at, :plain] = total.astype(BF)
            if vectors:
                both = mine[0][n, plain:].astype(F32)
                for term in mine[1:]:
                    both = both + term[n, plain:].astype(F32)
                both = both[:8] + both[8:]
                high = both.astype(BF).astype(F32)
                out[at, plain:] = jnp.concatenate([high, both - high], 0).astype(BF)


def combine(chain, *groups):
    args, out_shape, plan = [], [], []
    for terms, split, *vectors in groups:
        args += terms
        plan.append((len(terms), split, bool(vectors)))
        dims = terms[0].shape
        if split:
            out_shape += [shape_of((dims[0] // 2, *dims[1:]))] * 2
        else:
            out_shape += [shape_of(dims)]
    return chain.call(
        "combine",
        functools.partial(combine_kernel, plan),
        args,
        [VMEM] * len(args),
        [VMEM] * len(out_shape),
        out_shape,
        mib=20,
    )


def stack_kernel(one, two, out):
    n = one.shape[0]
    out[:n] = one[...]
    out[n:] = two[...]


def stack(chain, one, two):
    dims = (one.shape[0] + two.shape[0], *one.shape[1:])
    return chain.call(
        "stack", stack_kernel, [one, two], [VMEM, VMEM], [VMEM], [shape_of(dims)], mib=20
    )[0]


def join_kernel(scal, mine, got, out):
    rows = mine.shape[0]
    out[pl.ds(scal[0] * rows, rows)] = mine[...]
    out[pl.ds((1 - scal[0]) * rows, rows)] = got[...]


def join(chain, scal, mine, got):
    dims = (2 * mine.shape[0], *mine.shape[1:])
    return chain.call(
        "join",
        join_kernel,
        [scal, mine, got],
        [SMEM, VMEM, VMEM],
        [VMEM],
        [shape_of(dims)],
        mib=20,
    )[0]


def assemble_kernel(widths, cols, place, order, scal, one, two, *outs):
    for d in range(CHUNKS):
        part, m = (one, d) if d < CHUNKS // 2 else (two, d - CHUNKS // 2)
        c = scal[place] ^ order[d]
        left = 0
        for out, (rows, cuts) in zip(outs, widths):
            at = pl.multiple_of(c * rows, rows)
            cut = out.shape[1] // cuts
            for n in range(cuts):
                out[pl.ds(at, rows), n * cut : (n + 1) * cut] = part[
                    m, n * rows : (n + 1) * rows, left : left + cut
                ].astype(F32)
            left += cut
    if not cols:
        return
    outs, table = outs[len(widths) : -1], outs[-1]
    plain, width = one.shape[1] - 16, table.shape[2]
    for d in range(CHUNKS):
        part, m = (one, d) if d < CHUNKS // 2 else (two, d - CHUNKS // 2)
        both = part[m, plain:, :width].astype(F32)
        table[scal[place] ^ order[d]] = both[:8] + both[8:]

    def line(row):
        return table[row // 2, row % 2 : row % 2 + 1, :]

    for row in range(S_BU):
        outs[row][...] = line(row).reshape(width)
    bu, qb, vb = outs[S_BU:]
    for n in range(bu.shape[0] // width):
        bu[n * width : (n + 1) * width] = line(S_BU + n).reshape(width)
    qb[...] = line(S_QV)[:, :cols].reshape(cols)
    vb[...] = line(S_QV)[:, cols:].reshape(cols)


def assemble(chain, scal, parts, widths, vectors=(), place=1, order=range(CHUNKS)):
    out_shape = [shape_of((CHUNKS * rows, columns), F32) for rows, columns, _ in widths]
    out_shape += [shape_of((n,), F32) for n in vectors]
    plan = [(rows, cuts) for rows, _, cuts in widths]
    cols = vectors[-1] if vectors else 0
    scratch = [pltpu.VMEM((CHUNKS, 8, vectors[0]), F32)] if vectors else []
    return chain.call(
        "assemble",
        functools.partial(assemble_kernel, plan, cols, place, order),
        [scal, *parts],
        [SMEM] + [VMEM] * 2,
        [VMEM] * len(out_shape),
        out_shape,
        scratch=scratch,
        mib=20,
    )


def tensor_layer(
    dp,
    inputs,
    lengths,
    query_weight,
    query_bias,
    key_weight,
    value_weight,
    value_bias,
    output_weight,
    output_bias,
    first_gain,
    first_shift,
    up_weight,
    up_bias,
    down_weight,
    down_bias,
    second_gain,
    second_shift,
    cotangent,
):
    bits = dp.bit_length() - 1
    count, half, width = inputs.shape
    cols, units = query_weight.shape[1], up_weight.shape[1]
    seqs = count // 2
    side = lax.axis_index("tensor")
    spot = lax.axis_index(DP)
    core, across, deep = spot & 1, (spot >> 1) & 1, (spot >> 2) & 1
    scal = jnp.stack(
        [side, core * 4 + across * 2 + deep, core * 4 + across * 2]
    ).astype(jnp.int32)
    chain = Chain()

    def swap(value):
        return lax.ppermute(value, "tensor", [(0, 1), (1, 0)])

    def flip(value, bit):
        return lax.ppermute(value, DP, [(i, i ^ (1 << bit)) for i in range(dp)])

    def flip_far(value):
        return lax.ppermute(value, DP, [(i, i ^ 6) for i in range(dp)])

    def fetch(piece):
        first = chain.gate(swap(piece))
        return [first, flip(first, 2), flip(first, 1), flip_far(first)]

    def both_cores(found):
        return found + [flip(one, 0) for one in found]

    qkv = [query_weight, key_weight, value_weight]
    own = [output_weight, up_weight, down_weight]
    cut = width // CHUNKS
    flat = shape_of((seqs, half, width))
    qkvo, table_own = pack(
        chain,
        "pack_heads",
        pack_heads_kernel,
        [scal, *qkv, output_weight],
        [query_bias, value_bias, up_bias],
        [shape_of((cut + 16, 4 * cols)), shape_of((8, width), F32)],
        5,
    )
    (sent_units,) = pack(
        chain,
        "pack_units",
        pack_units_kernel,
        [scal, up_weight, down_weight],
        [],
        [shape_of((2, cut, units))],
        3,
    )
    x_send, xo = pack(
        chain, "pack_inputs", pack_inputs_kernel, [scal, inputs], [], [flat, flat], 2
    )
    xr = swap(x_send)
    e_send, eo, table = pack(
        chain,
        "pack_cotangent",
        pack_cotangent_kernel,
        [scal, cotangent],
        [
            output_bias,
            first_gain,
            first_shift,
            down_bias,
            second_gain,
            second_shift,
            table_own,
        ],
        [flat, flat, shape_of((16, width), F32)],
        2,
    )
    qkvo, got_units = fetch(qkvo), fetch(sent_units)

    lens = lax.dynamic_slice_in_dim(lengths, side * seqs, seqs, 0)
    at = jnp.arange(half)
    position = jnp.concatenate([side * half + at, (1 - side) * half + at])
    seen = jnp.where(position[None, :] < lens[:, None], 0.0, MASKED).astype(F32)[:, None, :]

    qkvo[1:] = chain.gate(*qkvo[1:])
    qkvo = both_cores(qkvo)
    q_own, k_own, v_own, c_own, p_own = attend(chain, scal, xo, xr, seen, table_own, qkv)
    er = swap(chain.gate(e_send))
    got_units = both_cores(got_units)
    table_oth, w_oth, q_oth, k_oth, v_oth, c_oth, p_oth = attend(
        chain, scal, xo, xr, seen, None, qkvo
    )
    (
        out_own,
        out_send,
        scale,
        sums2,
        y,
        unit,
        sl_own,
        sl_oth,
        dh,
        d_oth,
        d_oth_send,
        d_own,
        d_own_send,
    ) = forward(
        chain, scal, qkvo + got_units, xo, xr, eo, er, c_own, c_oth, table, table_oth, own
    )
    d_own_got = flip(d_own_send, 0)
    (d_oth,) = combine(chain, ([d_oth, flip(d_oth_send, 0)], False))
    d_got = swap(d_oth)
    d1, dc_own, dc_oth, table_back, u_oth, u_oth_send, u_own, u_own_send = backward(
        chain,
        scal,
        qkvo + got_units,
        table,
        sums2,
        y,
        c_own,
        c_oth,
        dh,
        unit,
        scale,
        (sl_own, sl_oth),
        own,
        2 * half,
    )
    u_oth_got, u_own_got = flip(u_oth_send, 0), flip(u_own_send, 0)
    d_keep, d_send = combine(chain, ([d_own, d_own_got, d_got], True))
    d_got = flip(d_send, 1)
    (u_oth,) = combine(chain, ([u_oth, u_oth_got], False))
    u_got = swap(u_oth)
    g_oth, q_oth, q_oth_send = attend_back(
        chain, scal, xo, xr, p_oth, q_oth, k_oth, v_oth, c_oth, dc_oth, table_back, 1
    )
    q_got = flip(q_oth_send, 0)
    (d_keep,) = combine(chain, ([d_keep, d_got], False))
    d_got = flip(d_keep, 2)
    (q_oth,) = combine(chain, ([q_oth, q_got], False, True))
    q_got = swap(q_oth)
    g_own, q_own, q_own_send = attend_back(
        chain, scal, xo, xr, p_own, q_own, k_own, v_own, c_own, dc_own, table_back, 0
    )
    q_own_got = flip(q_own_send, 0)
    u_keep, u_send = combine(chain, ([u_own, u_own_got, u_got], True))
    u_got = flip(u_send, 1)
    (d_keep,) = combine(chain, ([d_keep, d_got], False))
    d_got = flip(d_keep, 3)
    dx_own, dx_send = inputs_back(chain, d1, g_own, g_oth, qkv, w_oth, half)
    dx_got = swap(dx_send)
    def rest(value, *vectors):
        for bit in range(4, bits):
            (value,) = combine(chain, ([value, flip(value, bit)], False, *vectors))
        return value

    q_keep, q_send = combine(chain, ([q_own, q_own_got, q_got], True, True))
    q_got = flip(q_send, 1)
    out_got = swap(chain.gate(out_send))
    u_keep, u_send = combine(chain, ([u_keep, u_got], True))
    u_got = flip(u_send, 2)
    q_keep, q_send = combine(chain, ([q_keep, q_got], True, True))
    q_got = flip(q_send, 2)
    (u_keep,) = combine(chain, ([u_keep, u_got], False))
    u_got = flip(u_keep, 3)
    (q_keep,) = combine(chain, ([q_keep, q_got], False, True))
    q_got = flip(q_keep, 3)
    (d_two,) = combine(chain, ([d_keep, d_got], False))
    d_two = rest(d_two)
    d_got = flip(d_two, 1)
    (u_sum,) = combine(chain, ([u_keep, u_got], False))
    u_sum = rest(u_sum)
    u_got = flip(u_sum, 2)
    inputs_gradient = join(chain, scal, dx_own, dx_got)
    (q_sum,) = combine(chain, ([q_keep, q_got], False, True))
    q_sum = rest(q_sum, True)
    q_got = flip(q_sum, 1)
    u_two = stack(chain, u_sum, u_got)
    u_got = flip(u_two, 1)
    q_two = stack(chain, q_sum, q_got)
    q_got = flip(q_two, 2)
    rows = width // CHUNKS
    d_four = stack(chain, d_two, d_got)
    d_got = flip(d_four, 0)
    result = join(chain, scal, out_own, out_got)
    q_four = stack(chain, q_two, q_got)
    q_got = flip(q_four, 0)
    u_four = stack(chain, u_two, u_got)
    u_got = flip(u_four, 0)
    (down_back,) = assemble(chain, scal, (d_four, d_got), [(2 * rows, width, 1)], place=2)
    up_back, out_back = assemble(
        chain, scal, (u_four, u_got), [(rows, units, 1), (rows // 2, width, 2)]
    )
    query_back, key_back, value_back, g2b, b2b, bdb, g1b, b1b, bob, bub, qbb, vbb = assemble(
        chain,
        scal,
        (q_four, q_got),
        [(rows, cols, 1)] * 3,
        (width,) * 6 + (units, cols, cols),
        order=(0, 2, 1, 3, 4, 6, 5, 7),
    )
    return (
        result,
        inputs_gradient,
        query_back,
        qbb,
        key_back,
        value_back,
        vbb,
        out_back,
        bob,
        g1b,
        b1b,
        up_back,
        bub,
        down_back,
        bdb,
        g2b,
        b2b,
    )


def solution(mesh):
    in_specs = (
        P(DP, "tensor", None),
        P(DP),
        P(None, "tensor"),
        P("tensor"),
        P(None, "tensor"),
        P(None, "tensor"),
        P("tensor"),
        P("tensor", None),
        P(),
        P(),
        P(),
        P(None, "tensor"),
        P("tensor"),
        P("tensor", None),
        P(),
        P(),
        P(),
        P(DP, "tensor", None),
    )
    out_specs = (
        P(DP, "tensor", None),
        P(DP, "tensor", None),
        P(None, "tensor"),
        P("tensor"),
        P(None, "tensor"),
        P(None, "tensor"),
        P("tensor"),
        P("tensor", None),
        P(),
        P(),
        P(),
        P(None, "tensor"),
        P("tensor"),
        P("tensor", None),
        P(),
        P(),
        P(),
    )
    cut = mesh.devices.reshape(mesh.shape["dp"] // 4, 2, 2, mesh.shape["tensor"])
    return jax.shard_map(
        functools.partial(tensor_layer, mesh.shape["dp"]),
        mesh=Mesh(cut, (*DP, "tensor")),
        in_specs=in_specs,
        out_specs=out_specs,
        check_vma=False,
    )
```

```python
import functools

import jax
import jax.numpy as jnp
from jax import lax
from jax.experimental import pallas as pl
from jax.experimental.pallas import tpu as pltpu
from jax.sharding import Mesh
from jax.sharding import PartitionSpec as P

HD = 64
EPSILON = 1e-06
MASKED = -1000000000.0
BF = jnp.bfloat16
F32 = jnp.float32
MIB = 1024 * 1024
LANES = 128
CHUNKS = 8
DP = ("rest", "across", "core")
COSTS = (12, 6, 1, 40, 0.3, 20, 6, 6, 3, 3, 40, 20, 6, 20, 6, 20, 3, 0.05, 0.05, 0.05, 40, 1, 0.3, 6, 20, 40, 6, 20, 20, 1, 20, 12, 3, 6, 3, 3, 3, 12, 20, 12, 0.3, 40, 6)

ANY = pl.BlockSpec(memory_space=pl.ANY)
HBM = pl.BlockSpec(memory_space=pltpu.HBM)
SMEM = pl.BlockSpec(memory_space=pltpu.SMEM)
VMEM = pl.BlockSpec(memory_space=pltpu.VMEM)


def dot(left, right):
    return lax.dot_general(left, right, (((1,), (0,)), ((), ())), preferred_element_type=F32)


def dot_nt(left, right):
    return lax.dot_general(left, right, (((1,), (1,)), ((), ())), preferred_element_type=F32)


def dot_tn(left, right):
    return lax.dot_general(left, right, (((0,), (0,)), ((), ())), preferred_element_type=F32)


def shape_of(dims, kind=BF):
    return jax.ShapeDtypeStruct(dims, kind)


def fixed(dims):
    return pl.BlockSpec(dims, lambda *_: (0,) * len(dims))


def held(dims):
    return pl.BlockSpec(dims, lambda *_: (0,) * len(dims), pipeline_mode=pl.Buffered(1))


class Chain:
    def __init__(self):
        self.token = None
        self.count = 0

    def call(self, name, body, args, in_specs, out_specs, out_shape, grid=(), scratch=(), mib=62, aliases=None):
        taken, given = len(args), len(out_shape)
        linked = self.token is not None

        def kernel(*refs):
            rest = refs[taken + linked :]
            body(*refs[:taken], *rest[:given], *rest[given + 1 :])

        outs = pl.pallas_call(
            kernel,
            grid=grid,
            in_specs=list(in_specs) + [ANY] * linked,
            out_specs=list(out_specs) + [ANY],
            out_shape=list(out_shape) + [shape_of((8, LANES), F32)],
            scratch_shapes=list(scratch),
            input_output_aliases=aliases or {},
            compiler_params=pltpu.CompilerParams(
                dimension_semantics=("arbitrary",) * len(grid), vmem_limit_bytes=mib * MIB
            ),
            cost_estimate=pl.CostEstimate(
                flops=int(COSTS[self.count % len(COSTS)] * 1.1e9),
                bytes_accessed=1000,
                transcendentals=0,
            ),
            name=name,
        )(*args, *([self.token] if linked else []))
        self.token = outs[-1]
        self.count += 1
        return outs[:-1]

    def gate(self, *values):
        outs = self.call(
            "gate",
            lambda *_: None,
            list(values),
            [ANY] * len(values),
            [ANY] * len(values),
            [shape_of(value.shape, value.dtype) for value in values],
            aliases={n: n for n in range(len(values))},
        )
        return outs[0] if len(values) == 1 else outs


BO, G1, B1, BD, G2, B2, QV, BU = range(8)


def start_all(copies):
    for copy in copies:
        copy.start()


def wait_all(copies):
    for copy in copies:
        copy.wait()


def copy_all(pairs, sems):
    copies = [pltpu.make_async_copy(a, b, sems.at[n]) for n, (a, b) in enumerate(pairs)]
    for copy in copies:
        copy.start()
    for copy in copies:
        copy.wait()


def chunk(ref, place, total=1, part=0):
    n = ref.shape[0] // CHUNKS
    first = pl.multiple_of(place * n + part * (n // total), n // total)
    return ref.at[pl.ds(first, n // total)]


def pack_heads_kernel(scal, wq, wk, wv, wo, qb, vb, bu, qkvo, table, sems):
    place, cols, width = scal[1], wq.shape[1], wo.shape[1]
    rows = width // CHUNKS
    half = rows // 2
    pairs = [
        (chunk(w, place), qkvo.at[:rows, n * cols : (n + 1) * cols])
        for n, w in enumerate((wq, wk, wv))
    ]
    out = chunk(wo, place)
    pairs.append((out.at[:, :cols], qkvo.at[:half, 3 * cols :]))
    pairs.append((out.at[:, cols:], qkvo.at[half:rows, 3 * cols :]))
    copies = [pltpu.make_async_copy(a, b, sems.at[n]) for n, (a, b) in enumerate(pairs)]
    start_all(copies)
    table[...] = jnp.zeros_like(table)
    table[0:1, :] = jnp.concatenate([qb[...].reshape(1, cols), vb[...].reshape(1, cols)], 1)
    lifted = bu[...]
    for n in range(lifted.shape[0] // width):
        table[1 + n : 2 + n, :] = lifted[n * width : (n + 1) * width].reshape(1, width)
    high = table[...].astype(BF)
    low = (table[...] - high.astype(F32)).astype(BF)
    pad = jnp.zeros((8, 2 * width), BF)
    qkvo[rows:, :] = jnp.concatenate([jnp.concatenate([high, low], 1), pad], 0)
    wait_all(copies)


def pack_units_kernel(scal, wu, wd, units, sems):
    place, width = scal[1], wd.shape[1]
    copy_all(
        [
            (chunk(wu, place), units.at[0]),
            (chunk(wd, place, 2, 0), units.at[1, :, :width]),
            (chunk(wd, place, 2, 1), units.at[1, :, width:]),
        ],
        sems,
    )


def pack_inputs_kernel(scal, inputs, x_send, x_keep, sems):
    side, rows = scal[0], x_send.shape[0]
    copy_all(
        [
            (inputs.at[pl.ds((1 - side) * rows, rows)], x_send),
            (inputs.at[pl.ds(side * rows, rows)], x_keep),
        ],
        sems,
    )


def pack_cotangent_kernel(
    scal, cotangent, bo, g1, b1, bd, g2, b2, beside, e_send, e_keep, table, sems
):
    side = scal[0]
    rows, width = e_send.shape[0], e_send.shape[2]
    copy_all(
        [
            (cotangent.at[pl.ds((1 - side) * rows, rows)], e_send),
            (cotangent.at[pl.ds(side * rows, rows)], e_keep),
        ],
        sems,
    )
    for row, ref in ((BO, bo), (G1, g1), (B1, b1), (BD, bd), (G2, g2), (B2, b2)):
        table[row : row + 1, :] = ref[...].reshape(1, width)
    table[QV : QV + 8, :] = beside[...]


def pack(chain, name, kernel, hbm, small, outs, sems):
    return chain.call(
        name,
        kernel,
        [*hbm, *small],
        [SMEM] + [HBM] * (len(hbm) - 1) + [VMEM] * len(small),
        [VMEM] * len(outs),
        outs,
        scratch=[pltpu.SemaphoreType.DMA((sems,))],
    )


def attend_kernel(gathered, scal, *refs):
    if gathered:
        pieces, refs = refs[:CHUNKS], refs[CHUNKS:]
        xo, xr, seen, table, w, *outs, parts, sems, rows_all, p_all, out_sems = refs
    else:
        xo, xr, seen, table, wq, wk, wv, *outs, rows_all, p_all, out_sems = refs
    if gathered:

        @pl.when(pl.program_id(0) == 0)
        def _():
            cols, rows = w.shape[2], w.shape[1] // CHUNKS
            copies = [pltpu.make_async_copy(pieces[0].at[rows:], parts, sems.at[3, 0])]
            for d, piece in enumerate(pieces):
                at = pl.ds(pl.multiple_of((scal[1] ^ d) * rows, rows), rows)
                for n in range(3):
                    copies.append(
                        pltpu.make_async_copy(
                            piece.at[:rows, n * cols : (n + 1) * cols], w.at[n, at], sems.at[n, d]
                        )
                    )
            start_all(copies)
            wait_all(copies)
            width = table.shape[1]
            table[...] = parts[:8, :width].astype(F32) + parts[:8, width:].astype(F32)

        wq, wk, wv = w[0], w[1], w[2]
    else:
        wq, wk, wv = wq[...], wk[...], wv[...]
    cols = wq.shape[1]
    step = pl.program_id(0)
    seqs = p_all.shape[0]
    x = jnp.concatenate([xo[0], xr[0]], 0)
    span = x.shape[0]
    pairs = cols // LANES

    def rows_save(n, seq):
        at = pl.ds(seq * span, span)
        return pltpu.make_async_copy(rows_all.at[n, at], outs[n].at[at], out_sems.at[n, seq])

    def p_save(pair, seq):
        heads = pl.ds(2 * pair, 2)
        return pltpu.make_async_copy(
            p_all.at[seq, heads], outs[4].at[seq, heads], out_sems.at[4 + pair, seq]
        )

    q = (dot(x, wq) + table[0:1, :cols]).astype(BF) * jnp.asarray(HD**-0.5, BF)
    k = dot(x, wk).astype(BF)
    v = (dot(x, wv) + table[0:1, cols:]).astype(BF)
    here = pl.ds(pl.multiple_of(step * span, span), span)
    for n, value in enumerate((q, k, v)):
        rows_all[n, here, :] = value
        rows_save(n, step).start()
    bias = seen[0]
    low = lax.broadcasted_iota(jnp.int32, (span, LANES), 1) < HD
    zero = jnp.zeros((), BF)
    for pair in range(pairs):
        part = slice(pair * LANES, (pair + 1) * LANES)
        qp, kp, vp = q[:, part], k[:, part], v[:, part]
        joined = []
        for b in range(2):
            qm = jnp.where(low, qp, zero) if b == 0 else jnp.where(low, zero, qp)
            s = dot_nt(qm, kp) + bias
            e = jnp.exp(s - jnp.max(s, -1, keepdims=True))
            p = (e * (1.0 / jnp.sum(e, -1, keepdims=True))).astype(BF)
            p_all[step, pair * 2 + b] = p
            joined.append(dot(p, vp))
        p_save(pair, step).start()
        rows_all[3, here, part] = jnp.where(low, joined[0], joined[1]).astype(BF)
    rows_save(3, step).start()

    @pl.when(step == seqs - 1)
    def _():
        for seq in range(seqs):
            wait_all([rows_save(n, seq) for n in range(4)])
            wait_all([p_save(pair, seq) for pair in range(pairs)])


def attend(chain, scal, xo, xr, seen, table, weights):
    seqs, half, width = xo.shape
    span = 2 * half
    cols = width // 2
    heads = cols // HD
    gathered = table is None
    whole = pl.BlockSpec((1, half, width), lambda s: (s, 0, 0))
    in_specs = [whole, whole, pl.BlockSpec((1, 1, span), lambda s: (s, 0, 0))]
    out_specs = [ANY] * 5
    out_shape = [shape_of((seqs * span, cols))] * 4 + [shape_of((seqs, heads, span, span))]
    args = [xo, xr, seen]
    scratch = []
    if gathered:
        in_specs = [SMEM] + [ANY] * CHUNKS + in_specs
        args = [scal, *weights] + args
        out_specs = [held((8, width)), held((3, width, cols))] + out_specs
        out_shape = [shape_of((8, width), F32), shape_of((3, width, cols))] + out_shape
        scratch = [pltpu.VMEM((16, 2 * width), BF), pltpu.SemaphoreType.DMA((4, CHUNKS))]
    else:
        in_specs = [SMEM] + in_specs + [held(table.shape)] + [held((width, cols))] * 3
        args = [scal] + args + [table, *weights]
    return chain.call(
        "attend",
        functools.partial(attend_kernel, gathered),
        args,
        in_specs,
        out_specs,
        out_shape,
        grid=(seqs,),
        scratch=scratch
        + [
            pltpu.VMEM((4, seqs * span, cols), BF),
            pltpu.VMEM((seqs, heads, span, span), BF),
            pltpu.SemaphoreType.DMA((4 + cols // LANES, seqs)),
        ],
    )


def normed(hidden):
    centre = hidden - jnp.mean(hidden, -1, keepdims=True)
    scale = lax.rsqrt(jnp.mean(centre * centre, -1, keepdims=True) + EPSILON)
    return centre * scale, scale


def norm_back(upper, unit, scale, gain):
    through = upper * gain
    return scale * (
        through
        - jnp.mean(through, -1, keepdims=True)
        - unit * jnp.mean(through * unit, -1, keepdims=True)
    )


def gelu_and_slope(u):
    cdf = 0.5 + 0.5 * lax.erf(u * 0.7071067811865476)
    density = jnp.exp(-0.5 * u * u) * 0.3989422804014327
    return (u * cdf).astype(BF), (cdf + u * density).astype(BF)


ROWS = 128
COLUMNS = 256
FEW = 32


def folded(value):
    total = value[:8]
    for n in range(8, value.shape[0], 8):
        total = total + value[n : n + 8]
    return total


def put_chunks(place, value, first, out, rows, columns=slice(None)):
    for n in range(value.shape[0] // rows):
        out[place ^ (first + n), :, columns] = value[n * rows : (n + 1) * rows].astype(BF)


def weight_copies(place, own, pieces, targets, sems):
    wo, wu, wd = targets
    qkvo, halves = pieces
    cols, width = wo.shape[1:]
    units = wu.shape[2]
    found = []

    def bring(a, b):
        found.append(pltpu.make_async_copy(a, b, sems.at[len(found)]))
        return found[-1]

    lists = [[bring(a, target.at[0])] for a, target in zip(own, targets, strict=True)]
    for d in range(CHUNKS):
        c = place ^ d
        n = cols // CHUNKS
        at = pl.ds(pl.multiple_of(c * n, n), n)
        m = width // CHUNKS
        p = units // CHUNKS // 2
        lists[0].append(bring(qkvo[d].at[:n, 3 * cols :], wo.at[1, at, :cols]))
        lists[0].append(bring(qkvo[d].at[n : 2 * n, 3 * cols :], wo.at[1, at, cols:]))
        lists[1].append(bring(halves[d].at[0], wu.at[1, pl.ds(pl.multiple_of(c * m, m), m)]))
        for k in range(2):
            first = pl.multiple_of(c * 2 * p + k * p, p)
            lists[2].append(
                bring(halves[d].at[1, :, k * width : (k + 1) * width], wd.at[1, pl.ds(first, p)])
            )
    return lists


def forward_kernel(scal, *refs):
    qkvo, pieces, refs = refs[:CHUNKS], refs[CHUNKS : 2 * CHUNKS], refs[2 * CHUNKS :]
    (
        xo,
        xr,
        eo,
        er,
        c_own,
        c_oth,
        table,
        table_oth,
        wo_own,
        wu_own,
        wd_own,
        out_own,
        out_send,
        r_out,
        sums,
        y_out,
        n_out,
        sl_own,
        sl_oth,
        dh_out,
        d_oth,
        d_oth_send,
        d_own,
        d_own_send,
        wo,
        wu,
        wd,
        active,
        slopes,
        unit_all,
        unit_low,
        y_all,
        dh_all,
        second,
        products,
        sums_8,
        sems,
        out_sems,
        product_sems,
    ) = refs
    step = pl.program_id(0)
    cols, width = wo.shape[1:]
    units = wu.shape[2]
    half = xo.shape[1]
    span = 2 * half
    tiles = units // width
    blocks = dh_all.shape[0] // span
    final = pl.num_programs(0) - 1

    bring_o, bring_u, bring_d = weight_copies(
        scal[1], (wo_own, wu_own, wd_own), (qkvo, pieces), (wo, wu, wd), sems
    )

    def saves(block):
        rows = pl.ds(block * span, span)
        return [
            pltpu.make_async_copy(a, b.at[rows], out_sems.at[n, block])
            for n, (a, b) in enumerate(
                (
                    (y_all.at[rows], y_out),
                    (unit_low.at[rows], n_out),
                    (slopes.at[0, rows], sl_own),
                    (slopes.at[1, rows], sl_oth),
                    (dh_all.at[rows], dh_out),
                )
            )
        ]

    def product_saves(side):
        targets = ((d_own, d_own_send), (d_oth, d_oth_send))[side]
        return [
            pltpu.make_async_copy(
                products.at[side, pl.ds(n * CHUNKS // 2, CHUNKS // 2)],
                target,
                product_sems.at[side, n],
            )
            for n, target in enumerate(targets)
        ]

    @pl.when(step == 0)
    def _():
        start_all(bring_o)
        sums_8[...] = jnp.zeros_like(sums_8)
        wait_all(bring_o)
        start_all(bring_u[:1])

    @pl.when(step < blocks)
    def _():
        base = step * span

        def rows_at(start, n):
            return pl.ds(pl.multiple_of(base + start, n), n)

        def line(row):
            return table[row : row + 1, :]

        for m in range(0, span, ROWS):
            source = xo if m < half else xr
            x = source[0, m % half : m % half + ROWS, :].astype(F32)
            first = (
                x
                + dot(c_own[m : m + ROWS, :], wo[0])
                + dot(c_oth[m : m + ROWS, :], wo[1])
                + line(BO)
            )
            for r in range(0, ROWS, FEW):
                unit, scale = normed(first[r : r + FEW])
                at = rows_at(m + r, FEW)
                unit_all[at, :] = unit
                unit_low[at, :] = unit.astype(BF)
                r_out[m + r : m + r + FEW, :] = scale
                y_all[at, :] = (unit * line(G1) + line(B1)).astype(BF)

        for side, biases, row in ((0, table, BU), (1, table_oth, 1)):

            @pl.when(step == 0)
            def _():
                wait_all(bring_u[1:] if side else bring_u[:1])
                start_all(bring_d if side else bring_u[1:])

            for n in range(0, units, COLUMNS):
                tile, at = n // width, n % width
                bias = biases[row + tile : row + tile + 1, at : at + COLUMNS]
                for m in range(0, span, ROWS):
                    rows = rows_at(m, ROWS)
                    value, slope = gelu_and_slope(
                        dot(y_all[rows, :], wu[side, :, n : n + COLUMNS]) + bias
                    )
                    active[side * tiles + tile, rows, at : at + COLUMNS] = value
                    slopes[side, rows, n : n + COLUMNS] = slope

        @pl.when(step == 0)
        def _():
            wait_all(bring_d)

        for m in range(0, span, ROWS):
            rows = rows_at(m, ROWS)
            for n in range(0, width, COLUMNS):
                part = slice(n, n + COLUMNS)
                total = (
                    unit_all[rows, part] * table[G1 : G1 + 1, part]
                    + table[B1 : B1 + 1, part]
                    + table[BD : BD + 1, part]
                )
                for side in range(2):
                    for tile in range(tiles):
                        total = total + dot(
                            active[side * tiles + tile, rows, :],
                            wd[side, tile * width : (tile + 1) * width, part],
                        )
                second[m : m + ROWS, part] = total

        for m in range(0, span, FEW):
            unit, scale = normed(second[m : m + FEW, :])
            target, source = (out_own, eo) if m < half else (out_send, er)
            place = slice(m % half, m % half + FEW)
            target[0, place, :] = (unit * line(G2) + line(B2)).astype(BF)
            upper = source[0, place, :].astype(F32)
            back = norm_back(upper, unit, scale, line(G2))
            dh_all[rows_at(m, FEW), :] = back.astype(BF)
            sums_8[0] += folded(upper * unit)
            sums_8[1] += folded(upper)
            sums_8[2] += folded(back)

    for block in range(blocks):

        @pl.when(step == block)
        def _():
            start_all(saves(block))

    for tile in range(2 * tiles):

        @pl.when(step == blocks + tile)
        def _():
            side = 1 - tile // tiles
            rows = products.shape[2]
            for n in range(0, width, COLUMNS):
                part = slice(n, n + COLUMNS)
                value = dot_tn(active[side * tiles + tile % tiles], dh_all[:, part])
                put_chunks(
                    scal[2], value, tile % tiles * (width // rows), products.at[side], rows, part
                )
            if tile % tiles == tiles - 1:
                start_all(product_saves(side))

    @pl.when(step == final)
    def _():
        sums[...] = jnp.zeros_like(sums)
        for row in range(3):
            sums[row : row + 1, :] = jnp.sum(sums_8[row], 0, keepdims=True)
        for block in range(blocks):
            wait_all(saves(block))
        wait_all(product_saves(0) + product_saves(1))


def forward(chain, scal, pieces, xo, xr, eo, er, c_own, c_oth, table, table_oth, own):
    seqs, half, width = xo.shape
    span = 2 * half
    rows = seqs * span
    wo, wu, wd = own
    cols, units = wo.shape[0], wu.shape[1]
    blocks, tiles = seqs, units // width
    pair = pl.BlockSpec((1, half, width), lambda i: (jnp.minimum(i, blocks - 1), 0, 0))
    kept = (CHUNKS // 2, units // CHUNKS, width)

    def block(n):
        return pl.BlockSpec((span, n), lambda i: (jnp.minimum(i, blocks - 1), 0))

    in_specs = (
        [SMEM]
        + [ANY] * (2 * CHUNKS)
        + [pair] * 4
        + [block(cols)] * 2
        + [fixed(table.shape), fixed(table_oth.shape)]
        + [ANY] * 3
    )
    out_specs = [pair, pair, block(1), fixed((8, width))] + [ANY] * 9
    out_shape = [
        shape_of((seqs, half, width)),
        shape_of((seqs, half, width)),
        shape_of((rows, 1), F32),
        shape_of((8, width), F32),
        shape_of((rows, width)),
        shape_of((rows, width)),
        shape_of((rows, units)),
        shape_of((rows, units)),
        shape_of((rows, width)),
    ] + [shape_of(kept)] * 4
    return chain.call(
        "forward",
        forward_kernel,
        [scal, *pieces, xo, xr, eo, er, c_own, c_oth, table, table_oth, wo, wu, wd],
        in_specs,
        out_specs,
        out_shape,
        grid=(blocks + 2 * tiles,),
        scratch=[
            pltpu.VMEM((2, *wo.shape), BF),
            pltpu.VMEM((2, *wu.shape), BF),
            pltpu.VMEM((2, *wd.shape), BF),
            pltpu.VMEM((2 * tiles, rows, width), BF),
            pltpu.VMEM((2, rows, units), BF),
            pltpu.VMEM((rows, width), F32),
            pltpu.VMEM((rows, width), BF),
            pltpu.VMEM((rows, width), BF),
            pltpu.VMEM((rows, width), BF),
            pltpu.VMEM((span, width), F32),
            pltpu.VMEM((2, CHUNKS, *kept[1:]), BF),
            pltpu.VMEM((3, 8, width), F32),
            pltpu.SemaphoreType.DMA((3 + 5 * CHUNKS,)),
            pltpu.SemaphoreType.DMA((5, blocks)),
            pltpu.SemaphoreType.DMA((2, 2)),
        ],
    )


S_G2, S_B2, S_BD, S_G1, S_B1, S_BO, S_BU = range(7)
S_QV = 8


def backward_kernel(scal, *refs):
    qkvo, pieces, refs = refs[:CHUNKS], refs[CHUNKS : 2 * CHUNKS], refs[2 * CHUNKS :]
    (
        table,
        sums2,
        scale,
        y_in,
        c_in_own,
        c_in_oth,
        dh_in,
        unit_in,
        sl_in_own,
        sl_in_oth,
        wo_own,
        wu_own,
        wd_own,
        d1_out,
        dc_own,
        dc_oth,
        sums,
        u_oth,
        u_oth_send,
        u_own,
        u_own_send,
        wo,
        wu,
        wd,
        y,
        c,
        dh,
        unit,
        slopes,
        lifted_all,
        d1_all,
        total,
        products,
        sums_8,
        sems,
        in_sems,
        product_sems,
    ) = refs
    step = pl.program_id(0)
    span, width = d1_out.shape
    cols, units = wo.shape[1], wu.shape[2]
    tiles = units // width
    blocks = d1_all.shape[0] // span
    final = pl.num_programs(0) - 1
    bring_o, bring_u, bring_d = weight_copies(
        scal[1], (wo_own, wu_own, wd_own), (qkvo, pieces), (wo, wu, wd), sems
    )

    def bring_rows(n, source, target, block):
        rows = pl.ds(block * span, span)
        return pltpu.make_async_copy(source.at[rows], target.at[rows], in_sems.at[n, block])

    bring = [
        (
            bring_rows(0, dh_in, dh, block),
            bring_rows(1, sl_in_oth, slopes.at[1], block),
            bring_rows(2, sl_in_own, slopes.at[0], block),
            bring_rows(3, unit_in, unit, block),
        )
        for block in range(blocks)
    ]
    bring_last = [
        bring_rows(4 + n, source, target, block)
        for block in range(blocks)
        for n, (source, target) in enumerate(
            ((y_in, y), (c_in_own, c.at[0]), (c_in_oth, c.at[1]))
        )
    ]

    def product_saves(side):
        targets = ((u_own, u_own_send), (u_oth, u_oth_send))[side]
        return [
            pltpu.make_async_copy(
                products.at[side, pl.ds(n * CHUNKS // 2, CHUNKS // 2)],
                target,
                product_sems.at[side, n],
            )
            for n, target in enumerate(targets)
        ]

    @pl.when(step == 0)
    def _():
        start_all(bring_d[1:])
        start_all(bring[0][:2])
        sums[...] = jnp.zeros_like(sums)
        sums_8[...] = jnp.zeros_like(sums_8)
        for side in range(2):
            sums[side, S_G2 : S_BD + 1, :] = sums2[:3, :]

    for block in range(blocks):

        @pl.when(step == block)
        def _():
            wait_all(bring[block][:2] if block == 0 else bring[block])

    @pl.when(step < blocks)
    def _():
        rows = pl.ds(pl.multiple_of(step * span, span), span)

        def rows_at(start, n):
            return pl.ds(pl.multiple_of(step * span + start, n), n)

        for side in (1, 0):

            @pl.when(step == 0)
            def _():
                if side:
                    wait_all(bring_d[1:])
                    start_all([bring_d[0], bring[0][2]])
                else:
                    wait_all([bring_d[0], bring[0][2]])
                    start_all(bring_u + [bring[0][3]])

            for n in range(0, units, COLUMNS):
                tile, at = n // width, n % width
                added = jnp.zeros((8, COLUMNS), F32)
                value = dot_nt(dh[rows, :], wd[side, n : n + COLUMNS, :])
                for m in range(0, span, ROWS):
                    few = rows_at(m, ROWS)
                    lifted = (
                        value[m : m + ROWS] * slopes[side, few, n : n + COLUMNS].astype(F32)
                    ).astype(BF)
                    lifted_all[side * tiles + tile, few, at : at + COLUMNS] = lifted
                    added = added + folded(lifted.astype(F32))
                sums[side, S_BU + tile : S_BU + tile + 1, at : at + COLUMNS] += jnp.sum(
                    added, 0, keepdims=True
                )

        @pl.when(step == 0)
        def _():
            wait_all(bring_u + [bring[0][3]])
            start_all(bring_o)
            for later in bring[1:]:
                start_all(later)

        for n in range(0, width, COLUMNS):
            part = slice(n, n + COLUMNS)
            upper = dh[rows, part].astype(F32)
            for side in (1, 0):
                for tile in range(tiles):
                    upper = upper + dot_nt(
                        lifted_all[side * tiles + tile, rows, :],
                        wu[side, part, tile * width : (tile + 1) * width],
                    )
            total[:, part] = upper
        for m in range(0, span, FEW):
            part = slice(m, m + FEW)
            few = rows_at(m, FEW)
            upper = total[part, :]
            normal = unit[few, :].astype(F32)
            back = norm_back(upper, normal, scale[part, :], table[G1 : G1 + 1, :])
            sums_8[0] += folded(upper * normal)
            sums_8[1] += folded(upper)
            sums_8[2] += folded(back)
            lower = back.astype(BF)
            d1_out[part, :] = lower
            d1_all[few, :] = lower

        @pl.when(step == 0)
        def _():
            wait_all(bring_o)
            start_all(bring_last)

        lower = d1_out[...]
        dc_own[...] = dot_nt(lower, wo[0]).astype(BF)
        dc_oth[...] = dot_nt(lower, wo[1]).astype(BF)

    for tile in range(2 * tiles):

        @pl.when(step == blocks + tile)
        def _():
            if tile == 0:
                wait_all(bring_last)
            side = 1 - tile // tiles
            count = products.shape[2]
            for n in range(0, width, COLUMNS):
                value = dot_tn(y[...], lifted_all[side * tiles + tile % tiles, :, n : n + COLUMNS])
                at = tile % tiles * width + n
                put_chunks(
                    scal[1], value, 0, products.at[side], count, slice(at, at + COLUMNS)
                )
            if tile % tiles == 0:
                n = cols // CHUNKS
                for m in range(2):
                    value = dot_tn(c[side], d1_all[:, m * cols : (m + 1) * cols])
                    for k in range(CHUNKS):
                        products[
                            side, scal[1] ^ k, m * n : (m + 1) * n, units : units + cols
                        ] = value[k * n : (k + 1) * n].astype(BF)
            if tile % tiles == tiles - 1:
                start_all(product_saves(side))

    @pl.when(step == final)
    def _():
        for n, row in enumerate((S_G1, S_B1, S_BO)):
            line = jnp.sum(sums_8[n], 0, keepdims=True)
            sums[0, row : row + 1, :] = line
            sums[1, row : row + 1, :] = line
        wait_all(product_saves(0) + product_saves(1))


def backward(
    chain, scal, pieces, table, sums2, y, c_own, c_oth, dh, unit, scale, slopes, own, span
):
    rows, width = dh.shape
    wo, wu, wd = own
    cols, units = wo.shape[0], wu.shape[1]
    blocks, tiles = rows // span, units // width
    kept = (CHUNKS // 2, width // CHUNKS, units + cols)

    def block(n):
        return pl.BlockSpec((span, n), lambda i: (jnp.minimum(i, blocks - 1), 0))

    in_specs = (
        [SMEM]
        + [ANY] * (2 * CHUNKS)
        + [fixed(table.shape), fixed(sums2.shape), block(1)]
        + [ANY] * 10
    )
    out_specs = [block(width), block(cols), block(cols), fixed((2, 16, width))] + [ANY] * 4
    out_shape = [
        shape_of((rows, width)),
        shape_of((rows, cols)),
        shape_of((rows, cols)),
        shape_of((2, 16, width), F32),
    ] + [shape_of(kept)] * 4
    return chain.call(
        "backward",
        backward_kernel,
        [scal, *pieces, table, sums2, scale, y, c_own, c_oth, dh, unit, *slopes, *own],
        in_specs,
        out_specs,
        out_shape,
        grid=(blocks + 2 * tiles,),
        scratch=[
            pltpu.VMEM((2, *wo.shape), BF),
            pltpu.VMEM((2, *wu.shape), BF),
            pltpu.VMEM((2, *wd.shape), BF),
            pltpu.VMEM((rows, width), BF),
            pltpu.VMEM((2, rows, cols), BF),
            pltpu.VMEM((rows, width), BF),
            pltpu.VMEM((rows, width), BF),
            pltpu.VMEM((2, rows, units), BF),
            pltpu.VMEM((2 * tiles, rows, width), BF),
            pltpu.VMEM((rows, width), BF),
            pltpu.VMEM((span, width), F32),
            pltpu.VMEM((2, CHUNKS, *kept[1:]), BF),
            pltpu.VMEM((3, 8, width), F32),
            pltpu.SemaphoreType.DMA((3 + 5 * CHUNKS,)),
            pltpu.SemaphoreType.DMA((7, blocks)),
            pltpu.SemaphoreType.DMA((2, 2)),
        ],
    )


def attend_back_kernel(
    side,
    scal,
    vectors,
    xo,
    xr,
    p_in,
    *refs,
):
    rows_in, (grads, keep, send, x, p_all, rows_all, grads_all, table, products, *sems) = (
        refs[:5],
        refs[5:],
    )
    in_sems, p_sems, sems = sems
    step = pl.program_id(0)
    seqs, heads, span = p_all.shape[:3]
    final = seqs - 1
    half = span // 2
    cols = rows_all.shape[2]
    width = x.shape[1]
    rows = width // CHUNKS
    pairs = cols // LANES
    low = lax.broadcasted_iota(jnp.int32, (span, LANES), 1) < HD
    zero = jnp.zeros((), BF)

    def rows_copies(seq):
        at = pl.ds(seq * span, span)
        return [
            pltpu.make_async_copy(a.at[at], rows_all.at[n, at], in_sems.at[n, seq])
            for n, a in enumerate(rows_in)
        ]

    def p_copy(pair, seq):
        both = pl.ds(2 * pair, 2)
        return pltpu.make_async_copy(
            p_in.at[seq, both], p_all.at[seq, both], p_sems.at[pair, seq]
        )

    x_copies = [
        pltpu.make_async_copy(
            a.at[seq], x.at[pl.ds(seq * span + n * half, half)], in_sems.at[5 + n, seq]
        )
        for seq in range(seqs)
        for n, a in enumerate((xo, xr))
    ]
    here = pl.ds(pl.multiple_of(step * span, span), span)
    grads_save = [
        pltpu.make_async_copy(
            grads_all.at[pl.ds(seq * span, span)],
            grads.at[pl.ds(seq * span, span)],
            in_sems.at[7, seq],
        )
        for seq in range(seqs)
    ]

    @pl.when(step == 0)
    def _():
        start_all(rows_copies(0))
        p_copy(0, 0).start()
        table[...] = vectors[side]
        products[...] = jnp.zeros_like(products)

    wait_all(rows_copies(step))
    for pair in range(pairs):
        p_copy(pair, step).wait()
        if pair < pairs - 1:
            p_copy(pair + 1, step).start()
        else:

            @pl.when(step < final)
            def _():
                start_all(rows_copies(step + 1))
                p_copy(0, step + 1).start()

            @pl.when(step == final)
            def _():
                start_all(x_copies)

        part = slice(pair * LANES, (pair + 1) * LANES)
        qp, kp, vp, cp, dcp = [rows_all[n, here, part] for n in range(5)]
        shared = dcp.astype(F32) * cp.astype(F32)
        found = []
        for b in range(2):
            dcm = jnp.where(low, dcp, zero) if b == 0 else jnp.where(low, zero, dcp)
            centre = jnp.sum(
                jnp.where(low, shared, 0.0) if b == 0 else jnp.where(low, 0.0, shared),
                -1,
                keepdims=True,
            )
            p = p_all[step, pair * 2 + b]
            ds = (p.astype(F32) * (dot_nt(dcm, vp) - centre)).astype(BF)
            found.append((dot(ds, kp) * HD**-0.5, dot(qp.T, ds).T, dot(dcp.T, p).T))
        for n in range(3):
            at = n * cols + pair * LANES
            grads_all[here, at : at + LANES] = jnp.where(low, found[0][n], found[1][n]).astype(BF)
    for seq in range(seqs):

        @pl.when(step == seq)
        def _():
            grads_save[seq].start()

    @pl.when(step == final)
    def _():
        wait_all(x_copies)
        for m, n in enumerate((0, 2)):
            table[S_QV : S_QV + 1, m * cols : (m + 1) * cols] = jnp.sum(
                grads_all[:, n * cols : (n + 1) * cols].astype(F32), 0, keepdims=True
            )
        high = table[...].astype(BF).astype(F32)
        low_part = table[...] - high
        blank = jnp.zeros((8 - 2, width), F32)
        for m in range(CHUNKS):
            at = slice(2 * m, 2 * m + 2)
            products[scal[1] ^ m, rows:, :width] = jnp.concatenate(
                [high[at], blank, low_part[at], blank], 0
            ).astype(BF)
        for n in range(0, 3 * cols, cols):
            part = slice(n, n + cols)
            value = dot_tn(x[...], grads_all[:, part])
            for m in range(CHUNKS):
                products[scal[1] ^ m, :rows, part] = value[m * rows : (m + 1) * rows].astype(BF)
        copies = [
            pltpu.make_async_copy(products.at[: CHUNKS // 2], keep, sems.at[0]),
            pltpu.make_async_copy(products.at[CHUNKS // 2 :], send, sems.at[1]),
        ]
        start_all(copies)
        wait_all(copies + grads_save)


def attend_back(chain, scal, xo, xr, p, q, k, v, c, dc, vectors, side):
    seqs, half, width = xo.shape
    span = 2 * half
    cols = q.shape[1]
    pairs = cols // LANES
    kept = (CHUNKS // 2, width // CHUNKS + 16, 3 * cols)
    return chain.call(
        "attend_back",
        functools.partial(attend_back_kernel, side),
        [scal, vectors, xo, xr, p, q, k, v, c, dc],
        [SMEM, held(vectors.shape)] + [ANY] * 8,
        [ANY] * 3,
        [shape_of((seqs * span, 3 * cols)), shape_of(kept), shape_of(kept)],
        grid=(seqs,),
        scratch=[
            pltpu.VMEM((seqs * span, width), BF),
            pltpu.VMEM(p.shape, BF),
            pltpu.VMEM((5, seqs * span, cols), BF),
            pltpu.VMEM((seqs * span, 3 * cols), BF),
            pltpu.VMEM(vectors.shape[1:], F32),
            pltpu.VMEM((CHUNKS, *kept[1:]), BF),
            pltpu.SemaphoreType.DMA((8, seqs)),
            pltpu.SemaphoreType.DMA((pairs, seqs)),
            pltpu.SemaphoreType.DMA((2,)),
        ],
    )


def inputs_back_kernel(d1, own, oth, wq, wk, wv, w_oth, dx_own, dx_send):
    cols = wq.shape[1]
    total = d1[...].astype(F32)
    for n, w in enumerate((wq, wk, wv)):
        part = slice(n * cols, (n + 1) * cols)
        total = total + dot_nt(own[:, part], w[...]) + dot_nt(oth[:, part], w_oth[n])
    total = total.astype(BF)
    half = dx_own.shape[1]
    dx_own[0] = total[:half]
    dx_send[0] = total[half:]


def inputs_back(chain, d1, own, oth, weights, w_oth, half):
    rows, width = d1.shape
    cols = weights[0].shape[1]
    pair = pl.BlockSpec((1, half, width), lambda i: (i, 0, 0))
    out = shape_of((rows // (2 * half), half, width))
    return chain.call(
        "inputs_back",
        inputs_back_kernel,
        [d1, own, oth, *weights, w_oth],
        [pl.BlockSpec((2 * half, width), lambda i: (i, 0))]
        + [pl.BlockSpec((2 * half, 3 * cols), lambda i: (i, 0))] * 2
        + [fixed((width, cols))] * 3
        + [fixed(w_oth.shape)],
        [pair, pair],
        [out, out],
        grid=(rows // (2 * half),),
    )


def combine_kernel(groups, *refs):
    taken = sum(terms for terms, _, _ in groups)
    ins, outs = refs[:taken], list(refs[taken:])
    for terms, split, vectors in groups:
        mine, ins = ins[:terms], ins[terms:]
        chunks, rows = mine[0].shape[:2]
        plain = rows - 16 if vectors else rows
        keep = outs.pop(0)
        send = outs.pop(0) if split else None
        for n in range(chunks):
            out, at = (keep, n) if not split or n < chunks // 2 else (send, n - chunks // 2)
            total = mine[0][n, :plain].astype(F32)
            for term in mine[1:]:
                total = total + term[n, :plain].astype(F32)
            out[at, :plain] = total.astype(BF)
            if vectors:
                both = mine[0][n, plain:].astype(F32)
                for term in mine[1:]:
                    both = both + term[n, plain:].astype(F32)
                both = both[:8] + both[8:]
                high = both.astype(BF).astype(F32)
                out[at, plain:] = jnp.concatenate([high, both - high], 0).astype(BF)


def combine(chain, *groups):
    args, out_shape, plan = [], [], []
    for terms, split, *vectors in groups:
        args += terms
        plan.append((len(terms), split, bool(vectors)))
        dims = terms[0].shape
        if split:
            out_shape += [shape_of((dims[0] // 2, *dims[1:]))] * 2
        else:
            out_shape += [shape_of(dims)]
    return chain.call(
        "combine",
        functools.partial(combine_kernel, plan),
        args,
        [VMEM] * len(args),
        [VMEM] * len(out_shape),
        out_shape,
        mib=20,
    )


def stack_kernel(one, two, out):
    n = one.shape[0]
    out[:n] = one[...]
    out[n:] = two[...]


def stack(chain, one, two):
    dims = (one.shape[0] + two.shape[0], *one.shape[1:])
    return chain.call(
        "stack", stack_kernel, [one, two], [VMEM, VMEM], [VMEM], [shape_of(dims)], mib=20
    )[0]


def join_kernel(scal, mine, got, out):
    rows = mine.shape[0]
    out[pl.ds(scal[0] * rows, rows)] = mine[...]
    out[pl.ds((1 - scal[0]) * rows, rows)] = got[...]


def join(chain, scal, mine, got):
    dims = (2 * mine.shape[0], *mine.shape[1:])
    return chain.call(
        "join",
        join_kernel,
        [scal, mine, got],
        [SMEM, VMEM, VMEM],
        [VMEM],
        [shape_of(dims)],
        mib=20,
    )[0]


def assemble_kernel(widths, cols, place, order, scal, one, two, *outs):
    for d in range(CHUNKS):
        part, m = (one, d) if d < CHUNKS // 2 else (two, d - CHUNKS // 2)
        c = scal[place] ^ order[d]
        left = 0
        for out, (rows, cuts) in zip(outs, widths):
            at = pl.multiple_of(c * rows, rows)
            cut = out.shape[1] // cuts
            for n in range(cuts):
                out[pl.ds(at, rows), n * cut : (n + 1) * cut] = part[
                    m, n * rows : (n + 1) * rows, left : left + cut
                ].astype(F32)
            left += cut
    if not cols:
        return
    outs, table = outs[len(widths) : -1], outs[-1]
    plain, width = one.shape[1] - 16, table.shape[2]
    for d in range(CHUNKS):
        part, m = (one, d) if d < CHUNKS // 2 else (two, d - CHUNKS // 2)
        both = part[m, plain:, :width].astype(F32)
        table[scal[place] ^ order[d]] = both[:8] + both[8:]

    def line(row):
        return table[row // 2, row % 2 : row % 2 + 1, :]

    for row in range(S_BU):
        outs[row][...] = line(row).reshape(width)
    bu, qb, vb = outs[S_BU:]
    for n in range(bu.shape[0] // width):
        bu[n * width : (n + 1) * width] = line(S_BU + n).reshape(width)
    qb[...] = line(S_QV)[:, :cols].reshape(cols)
    vb[...] = line(S_QV)[:, cols:].reshape(cols)


def assemble(chain, scal, parts, widths, vectors=(), place=1, order=range(CHUNKS)):
    out_shape = [shape_of((CHUNKS * rows, columns), F32) for rows, columns, _ in widths]
    out_shape += [shape_of((n,), F32) for n in vectors]
    plan = [(rows, cuts) for rows, _, cuts in widths]
    cols = vectors[-1] if vectors else 0
    scratch = [pltpu.VMEM((CHUNKS, 8, vectors[0]), F32)] if vectors else []
    return chain.call(
        "assemble",
        functools.partial(assemble_kernel, plan, cols, place, order),
        [scal, *parts],
        [SMEM] + [VMEM] * 2,
        [VMEM] * len(out_shape),
        out_shape,
        scratch=scratch,
        mib=20,
    )


def tensor_layer(
    dp,
    inputs,
    lengths,
    query_weight,
    query_bias,
    key_weight,
    value_weight,
    value_bias,
    output_weight,
    output_bias,
    first_gain,
    first_shift,
    up_weight,
    up_bias,
    down_weight,
    down_bias,
    second_gain,
    second_shift,
    cotangent,
):
    bits = dp.bit_length() - 1
    count, half, width = inputs.shape
    cols, units = query_weight.shape[1], up_weight.shape[1]
    seqs = count // 2
    side = lax.axis_index("tensor")
    spot = lax.axis_index(DP)
    core, across, deep = spot & 1, (spot >> 1) & 1, (spot >> 2) & 1
    scal = jnp.stack(
        [side, core * 4 + across * 2 + deep, core * 4 + across * 2]
    ).astype(jnp.int32)
    chain = Chain()

    def swap(value):
        return lax.ppermute(value, "tensor", [(0, 1), (1, 0)])

    def flip(value, bit):
        return lax.ppermute(value, DP, [(i, i ^ (1 << bit)) for i in range(dp)])

    def flip_far(value):
        return lax.ppermute(value, DP, [(i, i ^ 6) for i in range(dp)])

    def fetch(piece):
        first = chain.gate(swap(piece))
        return [first, flip(first, 2), flip(first, 1), flip_far(first)]

    def both_cores(found):
        return found + [flip(one, 0) for one in found]

    qkv = [query_weight, key_weight, value_weight]
    own = [output_weight, up_weight, down_weight]
    cut = width // CHUNKS
    flat = shape_of((seqs, half, width))
    qkvo, table_own = pack(
        chain,
        "pack_heads",
        pack_heads_kernel,
        [scal, *qkv, output_weight],
        [query_bias, value_bias, up_bias],
        [shape_of((cut + 16, 4 * cols)), shape_of((8, width), F32)],
        5,
    )
    (sent_units,) = pack(
        chain,
        "pack_units",
        pack_units_kernel,
        [scal, up_weight, down_weight],
        [],
        [shape_of((2, cut, units))],
        3,
    )
    x_send, xo = pack(
        chain, "pack_inputs", pack_inputs_kernel, [scal, inputs], [], [flat, flat], 2
    )
    xr = swap(x_send)
    e_send, eo, table = pack(
        chain,
        "pack_cotangent",
        pack_cotangent_kernel,
        [scal, cotangent],
        [
            output_bias,
            first_gain,
            first_shift,
            down_bias,
            second_gain,
            second_shift,
            table_own,
        ],
        [flat, flat, shape_of((16, width), F32)],
        2,
    )
    qkvo, got_units = fetch(qkvo), fetch(sent_units)

    lens = lax.dynamic_slice_in_dim(lengths, side * seqs, seqs, 0)
    at = jnp.arange(half)
    position = jnp.concatenate([side * half + at, (1 - side) * half + at])
    seen = jnp.where(position[None, :] < lens[:, None], 0.0, MASKED).astype(F32)[:, None, :]

    qkvo[1:] = chain.gate(*qkvo[1:])
    qkvo = both_cores(qkvo)
    q_own, k_own, v_own, c_own, p_own = attend(chain, scal, xo, xr, seen, table_own, qkv)
    er = swap(chain.gate(e_send))
    got_units = both_cores(got_units)
    table_oth, w_oth, q_oth, k_oth, v_oth, c_oth, p_oth = attend(
        chain, scal, xo, xr, seen, None, qkvo
    )
    (
        out_own,
        out_send,
        scale,
        sums2,
        y,
        unit,
        sl_own,
        sl_oth,
        dh,
        d_oth,
        d_oth_send,
        d_own,
        d_own_send,
    ) = forward(
        chain, scal, qkvo + got_units, xo, xr, eo, er, c_own, c_oth, table, table_oth, own
    )
    d_own_got = flip(d_own_send, 0)
    (d_oth,) = combine(chain, ([d_oth, flip(d_oth_send, 0)], False))
    d_got = swap(d_oth)
    d1, dc_own, dc_oth, table_back, u_oth, u_oth_send, u_own, u_own_send = backward(
        chain,
        scal,
        qkvo + got_units,
        table,
        sums2,
        y,
        c_own,
        c_oth,
        dh,
        unit,
        scale,
        (sl_own, sl_oth),
        own,
        2 * half,
    )
    u_oth_got, u_own_got = flip(u_oth_send, 0), flip(u_own_send, 0)
    d_keep, d_send = combine(chain, ([d_own, d_own_got, d_got], True))
    d_got = flip(d_send, 1)
    (u_oth,) = combine(chain, ([u_oth, u_oth_got], False))
    u_got = swap(u_oth)
    g_oth, q_oth, q_oth_send = attend_back(
        chain, scal, xo, xr, p_oth, q_oth, k_oth, v_oth, c_oth, dc_oth, table_back, 1
    )
    q_got = flip(q_oth_send, 0)
    (d_keep,) = combine(chain, ([d_keep, d_got], False))
    d_got = flip(d_keep, 2)
    (q_oth,) = combine(chain, ([q_oth, q_got], False, True))
    q_got = swap(q_oth)
    g_own, q_own, q_own_send = attend_back(
        chain, scal, xo, xr, p_own, q_own, k_own, v_own, c_own, dc_own, table_back, 0
    )
    q_own_got = flip(q_own_send, 0)
    u_keep, u_send, d_keep = combine(
        chain, ([u_own, u_own_got, u_got], True), ([d_keep, d_got], False)
    )
    u_got = flip(u_send, 1)
    d_got = flip(d_keep, 3)
    dx_own, dx_send = inputs_back(chain, d1, g_own, g_oth, qkv, w_oth, half)
    dx_got = swap(dx_send)
    def rest(value, *vectors):
        for bit in range(4, bits):
            (value,) = combine(chain, ([value, flip(value, bit)], False, *vectors))
        return value

    q_keep, q_send = combine(chain, ([q_own, q_own_got, q_got], True, True))
    q_got = flip(q_send, 1)
    out_got = swap(chain.gate(out_send))
    u_keep, u_send = combine(chain, ([u_keep, u_got], True))
    u_got = flip(u_send, 2)
    q_keep, q_send = combine(chain, ([q_keep, q_got], True, True))
    q_got = flip(q_send, 2)
    (u_keep,) = combine(chain, ([u_keep, u_got], False))
    u_got = flip(u_keep, 3)
    (q_keep,) = combine(chain, ([q_keep, q_got], False, True))
    q_got = flip(q_keep, 3)
    (d_two,) = combine(chain, ([d_keep, d_got], False))
    d_two = rest(d_two)
    d_got = flip(d_two, 1)
    (u_sum,) = combine(chain, ([u_keep, u_got], False))
    u_sum = rest(u_sum)
    u_got = flip(u_sum, 2)
    inputs_gradient = join(chain, scal, dx_own, dx_got)
    (q_sum,) = combine(chain, ([q_keep, q_got], False, True))
    q_sum = rest(q_sum, True)
    q_got = flip(q_sum, 1)
    u_two = stack(chain, u_sum, u_got)
    u_got = flip(u_two, 1)
    q_two = stack(chain, q_sum, q_got)
    q_got = flip(q_two, 2)
    rows = width // CHUNKS
    d_four = stack(chain, d_two, d_got)
    d_got = flip(d_four, 0)
    result = join(chain, scal, out_own, out_got)
    q_four = stack(chain, q_two, q_got)
    q_got = flip(q_four, 0)
    u_four = stack(chain, u_two, u_got)
    u_got = flip(u_four, 0)
    (down_back,) = assemble(chain, scal, (d_four, d_got), [(2 * rows, width, 1)], place=2)
    up_back, out_back = assemble(
        chain, scal, (u_four, u_got), [(rows, units, 1), (rows // 2, width, 2)]
    )
    query_back, key_back, value_back, g2b, b2b, bdb, g1b, b1b, bob, bub, qbb, vbb = assemble(
        chain,
        scal,
        (q_four, q_got),
        [(rows, cols, 1)] * 3,
        (width,) * 6 + (units, cols, cols),
        order=(0, 2, 1, 3, 4, 6, 5, 7),
    )
    return (
        result,
        inputs_gradient,
        query_back,
        qbb,
        key_back,
        value_back,
        vbb,
        out_back,
        bob,
        g1b,
        b1b,
        up_back,
        bub,
        down_back,
        bdb,
        g2b,
        b2b,
    )


def solution(mesh):
    in_specs = (
        P(DP, "tensor", None),
        P(DP),
        P(None, "tensor"),
        P("tensor"),
        P(None, "tensor"),
        P(None, "tensor"),
        P("tensor"),
        P("tensor", None),
        P(),
        P(),
        P(),
        P(None, "tensor"),
        P("tensor"),
        P("tensor", None),
        P(),
        P(),
        P(),
        P(DP, "tensor", None),
    )
    out_specs = (
        P(DP, "tensor", None),
        P(DP, "tensor", None),
        P(None, "tensor"),
        P("tensor"),
        P(None, "tensor"),
        P(None, "tensor"),
        P("tensor"),
        P("tensor", None),
        P(),
        P(),
        P(),
        P(None, "tensor"),
        P("tensor"),
        P("tensor", None),
        P(),
        P(),
        P(),
    )
    cut = mesh.devices.reshape(mesh.shape["dp"] // 4, 2, 2, mesh.shape["tensor"])
    return jax.shard_map(
        functools.partial(tensor_layer, mesh.shape["dp"]),
        mesh=Mesh(cut, (*DP, "tensor")),
        in_specs=in_specs,
        out_specs=out_specs,
        check_vma=False,
    )
```
